32 devices in a mesh: row: 16 (over z, y, core), col: 2 (over x).
Axes of the slice: x: 2, y: 2, z: 4, core: 2. Of those that a mesh axis runs over, the one named last changes fastest.
Arguments:
- grad_x: float32 [1536, 1024], P('row', 'col'), may hold values from -6 to 6
- grad_y: float32 [1536, 1024], P('row', 'col'), may hold values from -6 to 6
- weight_x: float32 [1536, 1024], P('row', 'col'), may hold values from 0.1 to 10
- weight_y: float32 [1536, 1024], P('row', 'col'), may hold values from 0.1 to 10
- anchor: float32 [1536, 1024], P('row', 'col'), may hold values from 0.02 to 0.5
- prior: float32 [1536, 1024], P('row', 'col'), may hold values from -6 to 6
Outputs:
- heights: float32 [1536, 1024], P('row', 'col')
- residual: float32 [1536, 1024], P('row', 'col')
The draws below stay inside these ranges and needn't reach their ends.
All inputs are finite; a program needn't handle non-finite values.
Results may differ from the reference program's by a relative error of at most 0.0002.
Values sent between devices are 32-bit elements; how exact they have to be, the bound alone decides.
No kernel may reach another device: no remote copies, remote signals or barrier semaphores. Data moves between devices by JAX's collectives and lax.ppermute only.
A program may use at most 64 MiB of HBM per device.

```python
import math
import jax
import jax.numpy as jnp
from jax import lax

ITERS = 3
SWEEPS = 4
NR = 1536
NC = 1024


def steps_of(stream_key, extent, shards, low, top_value):
    loudness = 1.0
    for position, shards_of in shards:
        draws = jax.random.uniform(jax.random.fold_in(jax.random.fold_in(stream_key, 6), position), (shards_of,), jnp.float32, low / len(shards), top_value / len(shards))
        loudness = loudness * jnp.repeat(jnp.exp(draws), extent[position] // shards_of).reshape((-1,) + (1,) * (len(extent) - 1 - position))
    return loudness


def scatter_about(stream_key, extent, scale, most, split=(), dtype=jnp.bfloat16):
    loudness = steps_of(stream_key, extent, split, -0.22, 0.18) if split else 1.0
    entries = jax.random.normal(stream_key, extent, jnp.float32) * scale * loudness
    return jnp.minimum(jnp.maximum(entries, -most), most).astype(dtype)


def setup_inputs(seed: int = 0) -> dict:
    arg_keys = jax.random.split(jax.random.key(seed), 7)
    grad_x = scatter_about(arg_keys[0], (NR, NC), 1.0, 6.0, ((0, 16), (1, 2)), jnp.float32)
    grad_y = scatter_about(arg_keys[1], (NR, NC), 1.0, 6.0, ((0, 16), (1, 2)), jnp.float32)
    weight_x = jnp.clip(jnp.exp(math.log(10.0) - 4.6051702 * jax.random.uniform(arg_keys[2], (NR, NC), jnp.float32) ** steps_of(arg_keys[2], (NR, NC), ((0, 16), (1, 2)), -0.2, 0.2)), 0.1, 10.0)
    weight_y = jnp.clip(jnp.exp(math.log(10.0) - 4.6051702 * jax.random.uniform(arg_keys[3], (NR, NC), jnp.float32) ** steps_of(arg_keys[3], (NR, NC), ((0, 16), (1, 2)), -0.2, 0.2)), 0.1, 10.0)
    anchor = jnp.clip(jnp.exp(math.log(0.5) - 3.218876 * jax.random.uniform(arg_keys[4], (NR, NC), jnp.float32) ** steps_of(arg_keys[4], (NR, NC), ((0, 16), (1, 2)), -0.2, 0.2)), 0.02, 0.5)
    prior = scatter_about(arg_keys[5], (NR, NC), 1.0, 6.0, ((0, 16), (1, 2)), jnp.float32)
    return dict(grad_x=grad_x, grad_y=grad_y, weight_x=weight_x, weight_y=weight_y, anchor=anchor, prior=prior)


damping = 2.0 / 3.0


def block_view(field):
    return field.reshape(field.shape[0] // 4, 4, field.shape[1] // 4, 4)


def sweep(padded, coarse, coeffs):
    centre = padded[1:-1, 1:-1]
    beside = coeffs[0] * padded[1:-1, :-2] + coeffs[1] * padded[1:-1, 2:]
    beside = beside + coeffs[2] * padded[:-2, 1:-1] + coeffs[3] * padded[2:, 1:-1]
    return (1.0 - damping) * centre + damping * coeffs[4] * (coarse + beside)


def reference(grad_x, grad_y, weight_x, weight_y, anchor, prior):
    total_rows, total_cols = grad_x.shape
    row_ids = lax.broadcasted_iota(jnp.int32, grad_x.shape, 0)
    col_ids = lax.broadcasted_iota(jnp.int32, grad_x.shape, 1)
    right_w = jnp.where(col_ids < total_cols - 1, weight_x, jnp.float32(0.0))
    down_w = jnp.where(row_ids < total_rows - 1, weight_y, jnp.float32(0.0))
    left_w = jnp.pad(right_w, ((0, 0), (1, 0)))[:, :-1]
    up_w = jnp.pad(down_w, ((1, 0), (0, 0)))[:-1, :]
    flux_x = right_w * grad_x
    flux_y = down_w * grad_y
    source = anchor * prior + jnp.pad(flux_x, ((0, 0), (1, 0)))[:, :-1] - flux_x
    source = source + jnp.pad(flux_y, ((1, 0), (0, 0)))[:-1, :] - flux_y
    diag = anchor + left_w + right_w + up_w + down_w
    inverse = 1.0 / diag
    c_left = block_view(left_w)[:, :, :, 0].sum(1)
    c_right = block_view(right_w)[:, :, :, 3].sum(1)
    c_up = block_view(up_w)[:, 0, :, :].sum(2)
    c_down = block_view(down_w)[:, 3, :, :].sum(2)
    c_anchor = block_view(anchor).sum((1, 3))
    c_inverse = 1.0 / (c_anchor + c_left + c_right + c_up + c_down)
    coeffs = (c_left, c_right, c_up, c_down, c_inverse)

    def operate(field):
        padded = jnp.pad(field, 1)
        beside = left_w * padded[1:-1, :-2] + right_w * padded[1:-1, 2:]
        beside = beside + up_w * padded[:-2, 1:-1] + down_w * padded[2:, 1:-1]
        return diag * field - beside

    def precondition(resid):
        coarse = block_view(resid).sum((1, 3))
        level = damping * c_inverse * coarse
        for turn in range(SWEEPS - 1):
            level = sweep(jnp.pad(level, 1), coarse, coeffs)
        spread = jnp.broadcast_to(level[:, None, :, None], (level.shape[0], 4, level.shape[1], 4))
        return inverse * resid + spread.reshape(resid.shape)

    heights = jnp.zeros_like(source)
    residual = source
    smooth = precondition(residual)
    agree = jnp.sum(residual * smooth)
    direction = smooth
    for step in range(ITERS):
        image = operate(direction)
        alpha = agree / jnp.sum(direction * image)
        heights = heights + alpha * direction
        residual = residual - alpha * image
        if step + 1 < ITERS:
            smooth = precondition(residual)
            agree_next = jnp.sum(residual * smooth)
            direction = smooth + (agree_next / agree) * direction
            agree = agree_next
    return heights, residual
```

```python
import functools

import jax
import jax.numpy as jnp
from jax import lax
from jax.experimental import pallas as pl
from jax.experimental.pallas import tpu as pltpu
from jax.sharding import PartitionSpec as P

DAMP = 2.0 / 3.0
SHIFT = 1.0
HC = 64
HR = 20
FG = 24
GUARD = 8
VMEM = pl.BlockSpec(memory_space=pltpu.VMEM)
SMEM = pl.BlockSpec(memory_space=pltpu.SMEM)
F32 = jnp.float32


def lanes(shape):
    return lax.broadcasted_iota(jnp.int32, shape, 1)


def rows(shape):
    return lax.broadcasted_iota(jnp.int32, shape, 0)


def left_of(x, k=1):
    return pltpu.roll(x, k, 1)


def right_of(x, k=1):
    return pltpu.roll(x, x.shape[1] - k, 1)


def group_sum(x):
    lane = lanes(x.shape)
    x = x + jnp.where(lane % 2 == 0, right_of(x), left_of(x))
    return x + jnp.where(lane % 4 < 2, right_of(x, 2), left_of(x, 2))


def ld(ref, start, count=8, step=1):
    rows_of = pl.ds(start, count, stride=step) if step > 1 else slice(start, start + count)
    return jnp.concatenate([ref[j, rows_of, :] for j in range(ref.shape[0])], axis=1)


def st(ref, start, value, step=1):
    count = value.shape[0]
    rows_of = pl.ds(start, count, stride=step) if step > 1 else slice(start, start + count)
    for j in range(ref.shape[0]):
        ref[j, rows_of, :] = value[:, j * 128 : (j + 1) * 128]


def four_rows(ref, start, count):
    parts = [ld(ref, start + k, count, 4) for k in range(4)]
    return (parts[0] + parts[1]) + (parts[2] + parts[3])


def pack_columns(flags, gx, gy, wx, wy, an, pr, out):
    n = gx.shape[0]
    last = flags[0] == 1
    shape = gx.shape
    row, lane = rows(shape), lanes(shape)
    w_x = wx[...]
    w_y = jnp.where((row == n - 1) & (flags[1] == 1), F32(0.0), wy[...])
    fx = w_x * gx[...]
    fy = w_y * gy[...]
    a = an[...]
    before_x = jnp.where(lane == 0, F32(0.0), left_of(fx))
    before_y = jnp.where(row == 0, F32(0.0), pltpu.roll(fy, 1, 0))
    src = a * pr[...] + before_x - fx + before_y - fy

    def pair(x, y):
        low = jnp.where(lane < HC, x, left_of(y, HC))
        high = jnp.where(lane < HC, left_of(x, HC), y)
        return jnp.where(last, high, low)

    first = pair(src, w_x)
    edge = jnp.broadcast_to(fx[:, 127:128], shape)
    out[0:n, 0:128] = jnp.where((lane == 0) & last, edge, first)
    out[0:n, 128:256] = pair(w_y, a)
    tail = jnp.broadcast_to(pair(fy, fy)[n - 1 : n, :], (8, 128))
    out[n : n + 8, 0:128] = tail
    out[n : n + 8, 128:256] = tail


def pack_rows(has_outer, flags, gx, gy, wx, wy, an, pr, *refs):
    inner, refs = refs[0], refs[1:]
    outer = None
    if has_outer:
        outer, refs = refs[0], refs[1:]
    msg_in, msg_out, r_o, wx_o, wy_o, an_o, fy_o, u_s, t_s, tops = refs
    n, width = gx.shape
    ext = width + 2 * HC
    odd = flags[0] == 1
    end_col = flags[1] == 1
    end_row = flags[2] == 1
    row_odd = flags[3] == 1
    lane = lanes((8, width))
    elane = lanes((8, ext))
    row = rows((8, width))
    zero = F32(0.0)

    def sides(r, c):
        x = inner[r : r + 8, c : c + 128]
        y = outer[r : r + 8, c : c + 128] if has_outer else jnp.zeros_like(x)
        return jnp.where(odd, x, y), jnp.where(odd, y, x)

    carry = jnp.zeros((1, width), F32)
    for r in range(0, n, 8):
        w_x = jnp.where((lane == width - 1) & end_col, zero, wx[r : r + 8, :])
        w_y = wy[r : r + 8, :]
        if r == n - 8:
            w_y = jnp.where((row == 7) & end_row, zero, w_y)
        fx = w_x * gx[r : r + 8, :]
        fy = w_y * gy[r : r + 8, :]
        a = an[r : r + 8, :]
        before_x = jnp.where(lane == 0, zero, left_of(fx))
        before_y = jnp.where(row == 0, jnp.broadcast_to(carry, fy.shape), pltpu.roll(fy, 1, 0))
        carry = fy[7:8, :]
        src = a * pr[r : r + 8, :] + before_x - fx + before_y - fy
        left_a, right_a = sides(r, 0)
        left_b, right_b = sides(r, 128)
        src_e = jnp.concatenate([left_a[:, :HC], src, right_a[:, :HC]], axis=1)
        incoming = jnp.broadcast_to(left_a[:, 0:1], src_e.shape)
        outgoing = jnp.broadcast_to(fx[:, width - 1 : width], src_e.shape)
        src_e = src_e + jnp.where(elane == HC, incoming, jnp.where(elane == HC + width, outgoing, zero))
        st(r_o, r, jnp.where(elane == 0, zero, src_e))
        st(wx_o, r, jnp.concatenate([left_a[:, HC:], w_x, right_a[:, HC:]], axis=1))
        st(wy_o, r, jnp.concatenate([left_b[:, :HC], w_y, right_b[:, :HC]], axis=1))
        st(an_o, r, jnp.concatenate([left_b[:, HC:], a, right_b[:, HC:]], axis=1))
    left_f, right_f = sides(n, 0)
    tail = jnp.broadcast_to(carry, (8, width))
    fy_e = jnp.concatenate([left_f[:, :HC], tail, right_f[:, :HC]], axis=1)
    st(fy_o, 0, fy_e)

    lo, hi = 16, n - 32
    for base in (lo, hi):
        for r in range(base - 8, base + 24, 8):
            w_x, w_y = ld(wx_o, r), ld(wy_o, r)
            diag = ld(an_o, r) + w_x + left_of(w_x) + w_y + ld(wy_o, r - 1)
            st(u_s, r, jnp.where(diag > zero, ld(r_o, r) / diag, zero))
        for r in range(base, base + 16, 8):
            st(t_s, r, apply_a(u_s, wx_o, wy_o, an_o, r))
    four = lanes((4, ext)) % 4
    packed_s = []
    for base in (lo, hi):
        s = group_sum(four_rows(t_s, base, 4))
        keep = jnp.where(four == rows((4, ext)), s, zero)
        packed_s.append((keep[0:1] + keep[1:2]) + (keep[2:3] + keep[3:4]))
    count = (n - 2 * lo) // 4
    four = lanes((count, ext)) % 4
    c_r = group_sum(jnp.where(four == 3, four_rows(wx_o, lo, count), zero))
    c_d = group_sum(ld(wy_o, lo + 3, count, 4))
    c_a = group_sum(four_rows(an_o, lo, count))
    g = group_sum(four_rows(r_o, lo, count))
    packed = jnp.where(four < 2, jnp.where(four == 0, g, c_r), jnp.where(four == 2, c_d, c_a))

    top, bottom = tops.at[0], tops.at[1]
    for k, ref in enumerate((r_o, wx_o, wy_o, an_o)):
        top[:, k * HR : (k + 1) * HR, :] = ref[:, 0:HR, :]
        bottom[:, k * HR : (k + 1) * HR, :] = ref[:, n - HR : n, :]
    st(top, HR - 1, packed_s[0])
    st(bottom, 0, packed_s[1])
    st(bottom, HR, c_d[count - 9 : count - 8, :])
    st(bottom, 3 * HR, fy_e[0:1, :])
    st(top, 4 * HR, packed[0:8, :])
    st(bottom, 4 * HR, packed[count - 8 :, :])

    @pl.when(row_odd)
    def _():
        msg_in[...] = top[...]
        msg_out[...] = bottom[...]

    @pl.when(jnp.logical_not(row_odd))
    def _():
        msg_in[...] = bottom[...]
        msg_out[...] = top[...]


def apply_a(v, w_x, w_y, an, r):
    x = ld(v, r)
    flow = ld(w_x, r) * (x - right_of(x))
    down = ld(w_y, r) * (x - ld(v, r + 1))
    up = ld(w_y, r - 1) * (x - ld(v, r - 1))
    return (ld(an, r) * x + (flow - left_of(flow))) + (down + up)


def main(flags, r_i, wx_i, wy_i, an_i, fy_i, msg_in, msg_out, mom, p0, p1, p2, q0, q1, q2, r0,
         R, WX, WY, AN, DI, SP, PA, PB, QA, C_L, C_R, C_D, C_A, C_I, EA, EB, GC):
    blocks, n, _ = r_i.shape
    ext = blocks * 128
    fine = n + 2 * FG
    coarse = fine // 4 + 12
    zero = F32(0.0)
    odd = flags[3] == 1
    B = GUARD

    def sides(a, b):
        x, y = ld(msg_in, a, b - a), ld(msg_out, a, b - a)
        return jnp.where(odd, x, y), jnp.where(odd, y, x)

    zeros = jnp.zeros((B, ext), F32)
    for ref in (R, WX, WY, AN, PA, PB):
        st(ref, 0, zeros)
        st(ref, B + fine, zeros)
    for k, (ref, own) in enumerate(((R, r_i), (WX, wx_i), (WY, wy_i), (AN, an_i))):
        up, down = sides(k * HR, (k + 1) * HR)
        st(ref, B, zeros[: FG - HR])
        st(ref, B + FG + n + HR, zeros[: FG - HR])
        st(ref, B + FG - HR, up)
        st(ref, B + FG + n, down)
        for r in range(0, n, 8):
            st(ref, B + FG + r, ld(own, r))
    flux_up, _ = sides(3 * HR, 3 * HR + 1)
    st(R, B + FG, ld(R, B + FG, 1) + flux_up)
    st(R, B + FG + n, ld(R, B + FG + n, 1) + ld(fy_i, 0, 1))

    for r in range(B, B + fine, 8):
        w_x, w_y = ld(WX, r), ld(WY, r)
        diag = ld(AN, r) + w_x + left_of(w_x) + w_y + ld(WY, r - 1)
        st(DI, r, jnp.where(diag > zero, F32(1.0) / diag, zero))

    for ref in (EA, EB, C_D):
        st(ref, 0, zeros)
        st(ref, B + coarse, zeros)
    up, down = sides(4 * HR, 4 * HR + 8)
    four = lanes((8, ext)) % 4
    for k, ref in enumerate((GC, C_R, C_D, C_A)):
        st(ref, B, group_sum(jnp.where(four == k, up, zero)))
        st(ref, B + coarse - 8, group_sum(jnp.where(four == k, down, zero)))
    beyond, _ = sides(HR, HR + 1)
    st(C_D, B - 1, beyond)
    for c in range(8, coarse - 8, 8):
        f = B + 4 * c - 24
        st(GC, B + c, group_sum(four_rows(R, f, 8)))
        st(C_R, B + c, group_sum(jnp.where(four == 3, four_rows(WX, f, 8), zero)))
        st(C_D, B + c, group_sum(ld(WY, f + 3, 8, 4)))
        st(C_A, B + c, group_sum(four_rows(AN, f, 8)))
    for c in range(B, B + coarse, 8):
        c_r = ld(C_R, c)
        c_l = left_of(c_r, 4)
        total = ld(C_A, c) + c_l + c_r + ld(C_D, c - 1) + ld(C_D, c)
        st(C_L, c, c_l)
        st(C_I, c, jnp.where(total > zero, F32(DAMP) / total, zero))

    def smooth(lo, hi):
        for c in range(lo, hi, 8):
            st(EA, B + c, ld(C_I, B + c) * ld(GC, B + c))
        if lo > 0:
            st(EA, B + lo - 8, zeros)
            st(EB, B + lo - 8, zeros)
        if hi < coarse:
            st(EA, B + hi, zeros)
            st(EB, B + hi, zeros)
        old, new = EA, EB
        for turn in range(3):
            for c in range(B + lo, B + hi, 8):
                e = ld(old, c)
                beside = ld(C_L, c) * left_of(e, 4) + ld(C_R, c) * right_of(e, 4)
                beside = beside + (ld(C_D, c - 1) * ld(old, c - 1) + ld(C_D, c) * ld(old, c + 1))
                st(new, c, F32(1.0 - DAMP) * e + ld(C_I, c) * (ld(GC, c) + beside))
            old, new = new, old
        first, last = max(lo, 6), min(hi, coarse - 6)
        count = last - first
        for k in range(4):
            st(SP, B + 4 * (first - 6) + k, ld(EB, B + first, count), 4)

    def restrict(q):
        for c in range(8, coarse - 8, 8):
            st(GC, B + c, group_sum(four_rows(q, B + 4 * c - 24, 8)))

    smooth(0, coarse)
    for r in range(B, B + fine, 8):
        st(PA, r, ld(DI, r) * ld(R, r) + ld(SP, r))
    for r in range(B, B + fine, 8):
        st(QA, r, apply_a(PA, WX, WY, AN, r))
    restrict(QA)
    s_up, _ = sides(0, 1)
    _, s_down = sides(HR - 1, HR)
    for c, s, off in ((0, s_up, 4), (coarse - 8, s_down, 0)):
        part = jnp.where(four == rows((8, ext)) - off, jnp.broadcast_to(s, (8, ext)), zero)
        c = B + c
        e = ld(EB, c)
        image = ld(C_A, c) * e + ld(C_L, c) * (e - left_of(e, 4)) + ld(C_R, c) * (e - right_of(e, 4))
        image = image + ld(C_D, c - 1) * (e - ld(EB, c - 1))
        image = image + ld(C_D, c) * (e - ld(EB, c + 1))
        st(GC, c, group_sum(part) + image)
    for r in range(0, n, 8):
        f = B + FG + r
        st(p0, r, ld(PA, f))
        st(q0, r, ld(QA, f))
        st(r0, r, ld(R, f))
    smooth(0, coarse)
    for r in range(B, B + fine, 8):
        st(PB, r, (ld(DI, r) * ld(QA, r) + ld(SP, r)) - F32(SHIFT) * ld(PA, r))
    for r in range(B + 8, B + fine - 8, 8):
        st(QA, r, apply_a(PB, WX, WY, AN, r))
    restrict(QA)
    for r in range(0, n, 8):
        f = B + FG + r
        st(p1, r, ld(PB, f))
        st(q1, r, ld(QA, f))
    smooth(8, coarse - 8)
    for r in range(B + FG - 8, B + FG + n + 8, 8):
        st(PA, r, (ld(DI, r) * ld(QA, r) + ld(SP, r)) - F32(SHIFT) * ld(PB, r))
    own = (lanes((8, ext)) >= HC) & (lanes((8, ext)) < ext - HC)
    acc = [jnp.zeros((8, 128), F32) for _ in range(9)]
    for r in range(0, n, 8):
        f = B + FG + r
        z2 = ld(PA, f)
        image = apply_a(PA, WX, WY, AN, f)
        st(p2, r, z2)
        st(q2, r, image)
        z0, z1 = ld(p0, r), ld(p1, r)
        i0, i1, i2, res = [jnp.where(own, x, zero) for x in (ld(q0, r), ld(q1, r), image, ld(r0, r))]
        pairs = ((z0, i0), (z1, i0), (z1, i1), (z2, i0), (z2, i1), (z2, i2), (z0, res), (z1, res), (z2, res))
        for k, (x, y) in enumerate(pairs):
            prod = x * y
            parts = [prod[:, j : j + 128] for j in range(0, ext, 128)]
            while len(parts) > 1:
                parts = [sum(parts[j : j + 2][1:], parts[j]) for j in range(0, len(parts), 2)]
            acc[k] = acc[k] + parts[0]
    lane = lanes((8, 128))
    line = jnp.zeros((8, 128), F32)
    for k in range(9):
        total = jnp.sum(jnp.sum(acc[k], axis=0, keepdims=True), axis=1, keepdims=True)
        line = jnp.where(lane == k, jnp.broadcast_to(total, (8, 128)), line)
    for j in range(mom.shape[0]):
        mom[j] = line


def combine(mom, p0, p1, p2, q0, q1, q2, r0, heights, residual):
    blocks, n, _ = p0.shape
    ext = blocks * 128
    parts = [mom[j] for j in range(mom.shape[0])]
    while len(parts) > 1:
        parts = [sum(parts[j : j + 2][1:], parts[j]) for j in range(0, len(parts), 2)]
    tot = parts[0]
    m = [jnp.broadcast_to(tot[:, k : k + 1], (8, 128)) for k in range(9)]
    g00, g10, g11, g20, g21, g22, b0, b1, b2 = m
    l10, l20 = g10 / g00, g20 / g00
    d1 = g11 - l10 * g10
    t21 = g21 - l20 * g10
    l21 = t21 / d1
    d2 = g22 - l20 * g20 - l21 * t21
    y1 = b1 - l10 * b0
    y2 = b2 - l20 * b0 - l21 * y1
    x2 = y2 / d2
    x1 = y1 / d1 - l21 * x2
    x0 = b0 / g00 - l10 * x1 - l20 * x2
    reps = ext // 128
    x0, x1, x2 = [jnp.concatenate([x] * reps, axis=1) for x in (x0, x1, x2)]
    for r in range(0, n, 8):
        at = slice(r, r + 8)
        h = x0 * ld(p0, r) + x1 * ld(p1, r) + x2 * ld(p2, r)
        s = ld(r0, r) - (x0 * ld(q0, r) + x1 * ld(q1, r) + x2 * ld(q2, r))
        heights[at, :] = h[:, HC : ext - HC]
        residual[at, :] = s[:, HC : ext - HC]


def swap(x, axis, size, inner):
    if inner:
        pairs = [(i, i ^ 1) for i in range(size) if i ^ 1 < size]
    else:
        pairs = [(i, j) for i in range(size) for j in [((i + 1) ^ 1) - 1] if 0 <= j < size]
    return lax.ppermute(x, axis, pairs)


def local(nrow, ncol, gx, gy, wx, wy, an, pr):
    n, width = gx.shape
    ext = width + 2 * HC
    row, col = lax.axis_index("row"), lax.axis_index("col")
    flags = jnp.stack([col % 2, jnp.int32(col == ncol - 1), jnp.int32(row == nrow - 1), row % 2]).astype(jnp.int32)
    fields = (gx, gy, wx, wy, an, pr)
    blocks = width // 128

    def edge_columns(last):
        edge = jnp.stack([jnp.int32(last), jnp.int32(row == nrow - 1)])
        spec = pl.BlockSpec((n, 128), lambda i, s: (0, s[0] * (blocks - 1)))
        return pl.pallas_call(
            pack_columns,
            grid_spec=pltpu.PrefetchScalarGridSpec(
                num_scalar_prefetch=1,
                grid=(1,),
                in_specs=[spec] * 6,
                out_specs=pl.BlockSpec((n + 8, 256), lambda i, s: (0, 0)),
            ),
            out_shape=jax.ShapeDtypeStruct((n + 8, 256), F32),
            name="edge_columns",
        )(edge, *fields)

    halos = [swap(edge_columns(col % 2 == 0), "col", ncol, True)]
    if ncol > 2:
        halos.append(swap(edge_columns(col % 2 == 1), "col", ncol, False))
    depth = 4 * HR + 8
    nb = ext // 128
    tile = jax.ShapeDtypeStruct((nb, n, 128), F32)
    msg = jax.ShapeDtypeStruct((nb, depth, 128), F32)
    line = jax.ShapeDtypeStruct((nb, 8, 128), F32)
    limit = pltpu.CompilerParams(vmem_limit_bytes=48 * 1024 * 1024)
    to_in, to_out, *ext_fields = pl.pallas_call(
        functools.partial(pack_rows, len(halos) > 1),
        in_specs=[SMEM] + [VMEM] * (6 + len(halos)),
        out_specs=[VMEM] * 7,
        out_shape=[msg, msg, tile, tile, tile, tile, line],
        scratch_shapes=[pltpu.VMEM((nb, n, 128), F32)] * 2 + [pltpu.VMEM((2, nb, depth, 128), F32)],
        compiler_params=limit,
        name="edge_rows",
    )(flags, *fields, *halos)
    from_in = swap(to_in, "row", nrow, True)
    from_out = swap(to_out, "row", nrow, False)
    fine = n + 2 * FG
    coarse = fine // 4 + 12
    big = pltpu.VMEM((nb, fine + 2 * GUARD, 128), F32)
    small = pltpu.VMEM((nb, coarse + 2 * GUARD, 128), F32)
    devices = nrow * ncol
    mom, *vectors = pl.pallas_call(
        main,
        in_specs=[SMEM] + [VMEM] * 7,
        out_specs=[VMEM] * 8,
        out_shape=[jax.ShapeDtypeStruct((devices, 8, 128), F32)] + [tile] * 7,
        scratch_shapes=[big] * 9 + [small] * 8,
        compiler_params=limit,
        name="basis",
    )(flags, *ext_fields, from_in, from_out)
    mom = lax.all_to_all(mom, ("row", "col"), 0, 0, tiled=True)
    out = jax.ShapeDtypeStruct((n, width), F32)
    return tuple(
        pl.pallas_call(
            combine,
            in_specs=[VMEM] * 8,
            out_specs=[VMEM] * 2,
            out_shape=[out, out],
            compiler_params=limit,
            name="combine",
        )(mom, *vectors)
    )


def solution(mesh):
    spec = P("row", "col")
    return jax.shard_map(
        functools.partial(local, mesh.shape["row"], mesh.shape["col"]),
        mesh=mesh,
        in_specs=(spec,) * 6,
        out_specs=(spec, spec),
        check_vma=False,
    )
```

```python
import functools

import jax
import jax.numpy as jnp
from jax import lax
from jax.experimental import pallas as pl
from jax.experimental.pallas import tpu as pltpu
from jax.sharding import PartitionSpec as P

DAMP = 2.0 / 3.0
SHIFT = 1.0
HC = 64
HR = 20
FG = 24
GUARD = 8
VMEM = pl.BlockSpec(memory_space=pltpu.VMEM)
HBM = pl.BlockSpec(memory_space=pltpu.HBM)
F32 = jnp.float32


def lanes(shape):
    return lax.broadcasted_iota(jnp.int32, shape, 1)


def rows(shape):
    return lax.broadcasted_iota(jnp.int32, shape, 0)


def left_of(x, k=1):
    return pltpu.roll(x, k, 1)


def right_of(x, k=1):
    return pltpu.roll(x, x.shape[1] - k, 1)


def group_sum(x):
    lane = lanes(x.shape)
    x = x + jnp.where(lane % 2 == 0, right_of(x), left_of(x))
    return x + jnp.where(lane % 4 < 2, right_of(x, 2), left_of(x, 2))


def ld(ref, start, count=8, step=1):
    rows_of = pl.ds(start, count, stride=step) if step > 1 else slice(start, start + count)
    return jnp.concatenate([ref[j, rows_of, :] for j in range(ref.shape[0])], axis=1)


def st(ref, start, value, step=1):
    count = value.shape[0]
    rows_of = pl.ds(start, count, stride=step) if step > 1 else slice(start, start + count)
    for j in range(ref.shape[0]):
        ref[j, rows_of, :] = value[:, j * 128 : (j + 1) * 128]


def tree(parts):
    while len(parts) > 1:
        parts = [sum(parts[j + 1 : j + 2], parts[j]) for j in range(0, len(parts), 2)]
    return parts[0]


def four_rows(ref, start, count):
    parts = [ld(ref, start + k, count, 4) for k in range(4)]
    return (parts[0] + parts[1]) + (parts[2] + parts[3])


def position():
    row, col = lax.axis_index("row"), lax.axis_index("col")
    end_row = row == lax.axis_size("row") - 1
    end_col = col == lax.axis_size("col") - 1
    return lax.rem(row, 2) == 1, lax.rem(col, 2) == 1, end_row, end_col


def fetch(sources, targets, sems):
    copies = [pltpu.make_async_copy(x, y, sems.at[k]) for k, (x, y) in enumerate(zip(sources, targets))]
    for copy in copies:
        copy.start()
    for copy in copies:
        copy.wait()


def edge_columns(inner, *refs):
    fields, (out, *held, sems) = refs[:6], refs[6:]
    n, width = fields[0].shape
    _, col_odd, end_row, _ = position()
    last = jnp.logical_not(col_odd) if inner else col_odd
    offset = pl.multiple_of(jnp.where(last, width - 128, 0), 128)
    row, lane = rows((8, 128)), lanes((8, 128))
    zero = F32(0.0)
    fetch([f.at[:, pl.ds(offset, 128)] for f in fields], held, sems)

    def pair(x, y):
        low = jnp.where(lane < HC, x, left_of(y, HC))
        high = jnp.where(lane < HC, left_of(x, HC), y)
        return jnp.where(last, high, low)

    carry = jnp.zeros((1, 128), F32)
    for r in range(0, n, 8):
        g_x, g_y, w_x, w_y, a, p = [f[r : r + 8, :] for f in held]
        if r == n - 8:
            w_y = jnp.where((row == 7) & end_row, zero, w_y)
        fx = w_x * g_x
        fy = w_y * g_y
        before_x = jnp.where(lane == 0, zero, left_of(fx))
        before_y = jnp.where(row == 0, jnp.broadcast_to(carry, fy.shape), pltpu.roll(fy, 1, 0))
        carry = fy[7:8, :]
        src = a * p + before_x - fx + before_y - fy
        edge = jnp.broadcast_to(fx[:, 127:128], fx.shape)
        out[r : r + 8, 0:128] = jnp.where((lane == 0) & last, edge, pair(src, w_x))
        out[r : r + 8, 128:256] = pair(w_y, a)
    tail = jnp.broadcast_to(carry, (8, 128))
    tail = pair(tail, tail)
    out[n : n + 8, 0:128] = tail
    out[n : n + 8, 128:256] = tail


def tile_fields(*refs):
    fields, (r_o, wx_o, wy_o, an_o, fx_o, fy_o, *held, sems) = refs[:6], refs[6:]
    gx, gy, wx, wy, an, pr = held
    n, width = gx.shape
    fetch(fields, held, sems)
    _, _, end_row, end_col = position()
    row, lane = rows((8, width)), lanes((8, width))
    zero = F32(0.0)
    carry = jnp.zeros((1, width), F32)
    for r in range(0, n, 8):
        w_x = jnp.where((lane == width - 1) & end_col, zero, wx[r : r + 8, :])
        w_y = wy[r : r + 8, :]
        if r == n - 8:
            w_y = jnp.where((row == 7) & end_row, zero, w_y)
        fx = w_x * gx[r : r + 8, :]
        fy = w_y * gy[r : r + 8, :]
        a = an[r : r + 8, :]
        before_x = jnp.where(lane == 0, zero, left_of(fx))
        before_y = jnp.where(row == 0, jnp.broadcast_to(carry, fy.shape), pltpu.roll(fy, 1, 0))
        carry = fy[7:8, :]
        st(r_o, r, a * pr[r : r + 8, :] + before_x - fx + before_y - fy)
        st(wx_o, r, w_x)
        st(wy_o, r, w_y)
        st(an_o, r, a)
        fx_o[r : r + 8, :] = jnp.broadcast_to(fx[:, width - 1 : width], (8, 128))
    st(fy_o, 0, jnp.broadcast_to(carry, (8, width)))


def edge_rows(has_outer, r_t, wx_t, wy_t, an_t, fx_t, fy_t, *refs):
    inner, refs = refs[0], refs[1:]
    outer = None
    if has_outer:
        outer, refs = refs[0], refs[1:]
    msg_in, msg_out, r_o, wx_o, wy_o, an_o, fy_o, g_o, cr_o, cd_o, ca_o, u_s, t_s, tops = refs
    own, n, _ = r_t.shape
    ext = (own + 1) * 128
    row_odd, odd, _, _ = position()
    lane = lanes((8, 128))
    zero = F32(0.0)

    def halo(r, c):
        x = inner[r : r + 8, c : c + 128]
        y = outer[r : r + 8, c : c + 128] if has_outer else jnp.zeros_like(x)
        before, after = jnp.where(odd, x, y), jnp.where(odd, y, x)
        first = jnp.where(lane < HC, after, left_of(before, HC))
        second = jnp.where(lane < HC, left_of(after, HC), before)
        return first, second

    for r in range(0, n, 8):
        src_h, wx_h = halo(r, 0)
        wy_h, an_h = halo(r, 128)
        incoming = jnp.broadcast_to(src_h[:, HC : HC + 1], (8, 128))
        src_h = jnp.where(lane == 0, src_h + fx_t[r : r + 8, :], jnp.where(lane == HC, zero, src_h))
        for out, tile, h in ((r_o, r_t, src_h), (wx_o, wx_t, wx_h), (wy_o, wy_t, wy_h), (an_o, an_t, an_h)):
            for j in range(own):
                x = tile[j, r : r + 8, :]
                if out is r_o and j == 0:
                    x = jnp.where(lane == 0, x + incoming, x)
                out[j, r : r + 8, :] = x
            out[own, r : r + 8, :] = h
    for j in range(own):
        fy_o[j] = fy_t[j]
    fy_o[own] = halo(n, 0)[0]

    lo, hi = 16, n - 32
    for base in (lo, hi):
        for r in range(base - 8, base + 24, 8):
            w_x, w_y = ld(wx_o, r), ld(wy_o, r)
            diag = ld(an_o, r) + w_x + left_of(w_x) + w_y + ld(wy_o, r - 1)
            st(u_s, r, jnp.where(diag > zero, ld(r_o, r) / diag, zero))
        for r in range(base, base + 16, 8):
            st(t_s, r, apply_a(u_s, wx_o, wy_o, an_o, r))
    four = lanes((4, ext)) % 4
    packed_s = []
    for base in (lo, hi):
        s = group_sum(four_rows(t_s, base, 4))
        keep = jnp.where(four == rows((4, ext)), s, zero)
        packed_s.append((keep[0:1] + keep[1:2]) + (keep[2:3] + keep[3:4]))
    packed = []
    four = lanes((8, ext)) % 4
    for k, c in enumerate(range(lo, n - lo, 32)):
        c_r = group_sum(jnp.where(four == 3, four_rows(wx_o, c, 8), zero))
        c_d = group_sum(ld(wy_o, c + 3, 8, 4))
        c_a = group_sum(four_rows(an_o, c, 8))
        g = group_sum(four_rows(r_o, c, 8))
        packed.append(jnp.where(four < 2, jnp.where(four == 0, g, c_r), jnp.where(four == 2, c_d, c_a)))
        for out, x in ((g_o, g), (cr_o, c_r), (cd_o, c_d), (ca_o, c_a)):
            st(out, 8 * k, x)

    top, bottom = tops.at[0], tops.at[1]
    for k, ref in enumerate((r_o, wx_o, wy_o, an_o)):
        top[:, k * HR : (k + 1) * HR, :] = ref[:, 0:HR, :]
        bottom[:, k * HR : (k + 1) * HR, :] = ref[:, n - HR : n, :]
    st(top, HR - 1, packed_s[0])
    st(bottom, 0, packed_s[1])
    st(bottom, HR, ld(cd_o, cd_o.shape[1] - 9, 1))
    st(bottom, 3 * HR, ld(fy_o, 0, 1))
    st(top, 4 * HR, packed[0])
    st(bottom, 4 * HR, packed[-1])

    @pl.when(row_odd)
    def _():
        msg_in[...] = top[...]
        msg_out[...] = bottom[...]

    @pl.when(jnp.logical_not(row_odd))
    def _():
        msg_in[...] = bottom[...]
        msg_out[...] = top[...]


def inverse_diagonal(wx, wy, an, di):
    for r in range(8, wx.shape[1], 8):
        w_x, w_y = ld(wx, r), ld(wy, r)
        diag = ld(an, r) + w_x + left_of(w_x) + w_y + ld(wy, r - 1)
        st(di, r, jnp.where(diag > F32(0.0), F32(1.0) / diag, F32(0.0)))


def apply_a(v, w_x, w_y, an, r):
    x = ld(v, r)
    flow = ld(w_x, r) * (x - right_of(x))
    down = ld(w_y, r) * (x - ld(v, r + 1))
    up = ld(w_y, r - 1) * (x - ld(v, r - 1))
    return (ld(an, r) * x + (flow - left_of(flow))) + (down + up)


def basis(r_i, wx_i, wy_i, an_i, fy_i, g_i, cr_i, cd_i, ca_i, di_i, msg_in, msg_out, mom, p0, p1, p2, q0, q1, q2, r0,
         R, WX, WY, AN, DI, SP, PA, PB, QA, C_L, C_R, C_D, C_A, C_I, EA, EB, GC):
    blocks, n, _ = r_i.shape
    ext = blocks * 128
    fine = n + 2 * FG
    coarse = fine // 4 + 12
    zero = F32(0.0)
    odd, _, _, _ = position()
    own_blocks = blocks - 1
    B = GUARD

    def sides(a, b):
        x, y = ld(msg_in, a, b - a), ld(msg_out, a, b - a)
        return jnp.where(odd, x, y), jnp.where(odd, y, x)

    zeros = jnp.zeros((B, ext), F32)
    for ref in (R, WX, WY, AN, PA, PB):
        st(ref, 0, zeros)
        st(ref, B + fine, zeros)
    for k, (ref, own) in enumerate(((R, r_i), (WX, wx_i), (WY, wy_i), (AN, an_i))):
        up, down = sides(k * HR, (k + 1) * HR)
        st(ref, B, zeros[: FG - HR])
        st(ref, B + FG + n + HR, zeros[: FG - HR])
        st(ref, B + FG - HR, up)
        st(ref, B + FG + n, down)
        for r in range(0, n, 8):
            st(ref, B + FG + r, ld(own, r))
    flux_up, _ = sides(3 * HR, 3 * HR + 1)
    st(R, B + FG, ld(R, B + FG, 1) + flux_up)
    st(R, B + FG + n, ld(R, B + FG + n, 1) + ld(fy_i, 0, 1))

    for r in range(8, n, 8):
        st(DI, B + FG + r, ld(di_i, r))
    for r in [*range(B, B + FG + 8, 8), *range(B + FG + n, B + fine, 8)]:
        w_x, w_y = ld(WX, r), ld(WY, r)
        diag = ld(AN, r) + w_x + left_of(w_x) + w_y + ld(WY, r - 1)
        st(DI, r, jnp.where(diag > zero, F32(1.0) / diag, zero))

    for ref in (EA, EB, C_D):
        st(ref, 0, zeros)
        st(ref, B + coarse, zeros)
    up, down = sides(4 * HR, 4 * HR + 8)
    four = lanes((8, ext)) % 4
    for k, ref in enumerate((GC, C_R, C_D, C_A)):
        st(ref, B, group_sum(jnp.where(four == k, up, zero)))
        st(ref, B + coarse - 8, group_sum(jnp.where(four == k, down, zero)))
    beyond, _ = sides(HR, HR + 1)
    st(C_D, B - 1, beyond)
    for ref, own in ((GC, g_i), (C_R, cr_i), (C_D, cd_i), (C_A, ca_i)):
        for r in range(0, own.shape[1], 8):
            st(ref, B + 16 + r, ld(own, r))
    for c in (8, coarse - 16):
        f = B + 4 * c - 24
        st(GC, B + c, group_sum(four_rows(R, f, 8)))
        st(C_R, B + c, group_sum(jnp.where(four == 3, four_rows(WX, f, 8), zero)))
        st(C_D, B + c, group_sum(ld(WY, f + 3, 8, 4)))
        st(C_A, B + c, group_sum(four_rows(AN, f, 8)))
    for c in range(B, B + coarse, 8):
        c_r = ld(C_R, c)
        c_l = left_of(c_r, 4)
        total = ld(C_A, c) + c_l + c_r + ld(C_D, c - 1) + ld(C_D, c)
        st(C_L, c, c_l)
        st(C_I, c, jnp.where(total > zero, F32(DAMP) / total, zero))

    def smooth(lo, hi):
        for c in range(lo, hi, 8):
            st(EA, B + c, ld(C_I, B + c) * ld(GC, B + c))
        if lo > 0:
            st(EA, B + lo - 8, zeros)
            st(EB, B + lo - 8, zeros)
        if hi < coarse:
            st(EA, B + hi, zeros)
            st(EB, B + hi, zeros)
        old, new = EA, EB
        for turn in range(3):
            for c in range(B + lo, B + hi, 8):
                e = ld(old, c)
                beside = ld(C_L, c) * left_of(e, 4) + ld(C_R, c) * right_of(e, 4)
                beside = beside + (ld(C_D, c - 1) * ld(old, c - 1) + ld(C_D, c) * ld(old, c + 1))
                st(new, c, F32(1.0 - DAMP) * e + ld(C_I, c) * (ld(GC, c) + beside))
            old, new = new, old
        first, last = max(lo, 6), min(hi, coarse - 6)
        count = last - first
        for k in range(4):
            st(SP, B + 4 * (first - 6) + k, ld(EB, B + first, count), 4)

    def restrict(q):
        for c in range(8, coarse - 8, 8):
            st(GC, B + c, group_sum(four_rows(q, B + 4 * c - 24, 8)))

    smooth(0, coarse)
    for r in range(B, B + fine, 8):
        st(PA, r, ld(DI, r) * ld(R, r) + ld(SP, r))
    for r in range(B, B + fine, 8):
        st(QA, r, apply_a(PA, WX, WY, AN, r))
    restrict(QA)
    s_up, _ = sides(0, 1)
    _, s_down = sides(HR - 1, HR)
    for c, s, off in ((0, s_up, 4), (coarse - 8, s_down, 0)):
        part = jnp.where(four == rows((8, ext)) - off, jnp.broadcast_to(s, (8, ext)), zero)
        c = B + c
        e = ld(EB, c)
        image = ld(C_A, c) * e + ld(C_L, c) * (e - left_of(e, 4)) + ld(C_R, c) * (e - right_of(e, 4))
        image = image + ld(C_D, c - 1) * (e - ld(EB, c - 1))
        image = image + ld(C_D, c) * (e - ld(EB, c + 1))
        st(GC, c, group_sum(part) + image)
    for r in range(0, n, 8):
        f = B + FG + r
        for out, ref in ((p0, PA), (q0, QA), (r0, R)):
            out[:, r : r + 8, :] = ref[:own_blocks, f : f + 8, :]
    smooth(0, coarse)
    for r in range(B, B + fine, 8):
        st(PB, r, (ld(DI, r) * ld(QA, r) + ld(SP, r)) - F32(SHIFT) * ld(PA, r))
    for r in range(B + 8, B + fine - 8, 8):
        st(QA, r, apply_a(PB, WX, WY, AN, r))
    restrict(QA)
    for r in range(0, n, 8):
        f = B + FG + r
        for out, ref in ((p1, PB), (q1, QA)):
            out[:, r : r + 8, :] = ref[:own_blocks, f : f + 8, :]
    smooth(8, coarse - 8)
    for r in range(B + FG - 8, B + FG + n + 8, 8):
        st(PA, r, (ld(DI, r) * ld(QA, r) + ld(SP, r)) - F32(SHIFT) * ld(PB, r))
    acc = [jnp.zeros((8, 128), F32) for _ in range(9)]
    for r in range(0, n, 8):
        f = B + FG + r
        image = apply_a(PA, WX, WY, AN, f)
        sums = [[] for _ in acc]
        for j in range(own_blocks):
            z2, i2 = PA[j, f : f + 8, :], image[:, j * 128 : (j + 1) * 128]
            p2[j, r : r + 8, :] = z2
            q2[j, r : r + 8, :] = i2
            z0, z1, i0, i1, res = [x[j, r : r + 8, :] for x in (p0, p1, q0, q1, r0)]
            pairs = ((z0, i0), (z1, i0), (z1, i1), (z2, i0), (z2, i1), (z2, i2), (z0, res), (z1, res), (z2, res))
            for k, (x, y) in enumerate(pairs):
                sums[k].append(x * y)
        for k, parts in enumerate(sums):
            acc[k] = acc[k] + tree(parts)
    lane = lanes((8, 128))
    line = jnp.zeros((8, 128), F32)
    for k in range(9):
        total = jnp.sum(jnp.sum(acc[k], axis=0, keepdims=True), axis=1, keepdims=True)
        line = jnp.where(lane == k, jnp.broadcast_to(total, (8, 128)), line)
    for j in range(mom.shape[0]):
        mom[j] = line


def combine(mom, p0, p1, p2, q0, q1, q2, r0, heights, residual):
    blocks, n, _ = p0.shape
    tot = tree([mom[j] for j in range(mom.shape[0])])
    m = [jnp.broadcast_to(tot[:, k : k + 1], (8, 128)) for k in range(9)]
    g00, g10, g11, g20, g21, g22, b0, b1, b2 = m
    l10, l20 = g10 / g00, g20 / g00
    d1 = g11 - l10 * g10
    t21 = g21 - l20 * g10
    l21 = t21 / d1
    d2 = g22 - l20 * g20 - l21 * t21
    y1 = b1 - l10 * b0
    y2 = b2 - l20 * b0 - l21 * y1
    x2 = y2 / d2
    x1 = y1 / d1 - l21 * x2
    x0 = b0 / g00 - l10 * x1 - l20 * x2
    for r in range(0, n, 8):
        for j in range(blocks):
            at = (slice(r, r + 8), slice(j * 128, (j + 1) * 128))
            z0, z1, z2, i0, i1, i2, res = [x[j, r : r + 8, :] for x in (p0, p1, p2, q0, q1, q2, r0)]
            heights[at] = x0 * z0 + x1 * z1 + x2 * z2
            residual[at] = res - (x0 * i0 + x1 * i1 + x2 * i2)


def swap(x, axis, size, inner):
    if inner:
        pairs = [(i, i ^ 1) for i in range(size) if i ^ 1 < size]
    else:
        pairs = [(i, j) for i in range(size) for j in [((i + 1) ^ 1) - 1] if 0 <= j < size]
    return lax.ppermute(x, axis, pairs)


def local(nrow, ncol, gx, gy, wx, wy, an, pr):
    n, width = gx.shape
    ext = width + 2 * HC
    fields = tuple(pltpu.with_memory_space_constraint(f, pltpu.HBM) for f in (gx, gy, wx, wy, an, pr))
    nb = ext // 128
    shape = lambda *dims: jax.ShapeDtypeStruct(dims, F32)
    params = pltpu.CompilerParams(vmem_limit_bytes=48 * 1024 * 1024)

    def call(kernel, name, args, outs, scratch=(), us=1, fetches=0):
        sems = [pltpu.SemaphoreType.DMA((fetches,))] if fetches else []
        return pl.pallas_call(
            kernel,
            in_specs=[HBM if fetches else VMEM] * len(args),
            out_specs=[VMEM] * len(outs),
            out_shape=outs,
            scratch_shapes=[pltpu.VMEM(dims, F32) for dims in scratch] + sems,
            compiler_params=params,
            cost_estimate=pl.CostEstimate(flops=us * 2_000_000, bytes_accessed=us * 2_000_000, transcendentals=0),
            name=name,
        )(*args)

    halos = []
    for inner in (True, False) if ncol > 2 else (True,):
        (edge,) = call(functools.partial(edge_columns, inner), "edge_columns", fields, [shape(n + 8, 256)], [(n, 128)] * 6, 1, 6)
        halos.append(swap(edge, "col", ncol, inner))
    tile = shape(nb - 1, n, 128)
    own = call(tile_fields, "tile_fields", fields, [tile] * 4 + [shape(n, 128), shape(nb - 1, 8, 128)], [(n, width)] * 6, 1, 6)
    depth = 4 * HR + 8
    lo = 16
    far = shape(nb, (n - 2 * lo) // 4, 128)
    msg = shape(nb, depth, 128)
    field = shape(nb, n, 128)
    to_in, to_out, r_e, wx_e, wy_e, an_e, *rest = call(
        functools.partial(edge_rows, len(halos) > 1),
        "edge_rows",
        (*own, *halos),
        [msg, msg] + [field] * 4 + [shape(nb, 8, 128)] + [far] * 4,
        [(nb, n, 128), (nb, n, 128), (2, nb, depth, 128)],
    )
    from_out = swap(to_out, "row", nrow, False)
    from_in = swap(to_in, "row", nrow, True)
    (di,) = call(inverse_diagonal, "inverse_diagonal", (wx_e, wy_e, an_e), [field])
    fine = n + 2 * FG
    coarse = fine // 4 + 12
    mom, *vectors = call(
        basis,
        "basis",
        (r_e, wx_e, wy_e, an_e, *rest, di, from_in, from_out),
        [shape(nrow * ncol, 8, 128)] + [tile] * 7,
        [(nb, fine + 2 * GUARD, 128)] * 9 + [(nb, coarse + 2 * GUARD, 128)] * 8,
    )
    mom = lax.all_to_all(mom, ("row", "col"), 0, 0, tiled=True)
    out = shape(n, width)
    return tuple(call(combine, "combine", (mom, *vectors), [out, out]))


def solution(mesh):
    spec = P("row", "col")
    return jax.shard_map(
        functools.partial(local, mesh.shape["row"], mesh.shape["col"]),
        mesh=mesh,
        in_specs=(spec,) * 6,
        out_specs=(spec, spec),
        check_vma=False,
    )
```

```python
import functools

import jax
import jax.numpy as jnp
from jax import lax
from jax.experimental import pallas as pl
from jax.experimental.pallas import tpu as pltpu
from jax.sharding import PartitionSpec as P

DAMP = 2.0 / 3.0
SHIFT = 1.0
HC = 64
HR = 20
FG = 24
GUARD = 8
VMEM = pl.BlockSpec(memory_space=pltpu.VMEM)
HBM = pl.BlockSpec(memory_space=pltpu.HBM)
F32 = jnp.float32


def lanes(shape):
    return lax.broadcasted_iota(jnp.int32, shape, 1)


def rows(shape):
    return lax.broadcasted_iota(jnp.int32, shape, 0)


def roll_right(x, k=1):
    return pltpu.roll(x, k, 1)


def roll_left(x, k=1):
    return pltpu.roll(x, x.shape[1] - k, 1)


def group_sum(x):
    lane = lanes(x.shape)
    x = x + jnp.where(lane % 2 == 0, roll_left(x), roll_right(x))
    return x + jnp.where(lane % 4 < 2, roll_left(x, 2), roll_right(x, 2))


def split(x):
    return [x[:, j : j + 128] for j in range(0, x.shape[1], 128)]


def join(parts):
    return jnp.concatenate(parts, axis=1)


class Wide:
    def __init__(self, width):
        self.coarse_blocks = width // 128 + 1

    left, right = staticmethod(roll_right), staticmethod(roll_left)
    total = staticmethod(group_sum)
    spread = take = staticmethod(lambda x: x)
    steps_in = steps_out = ()

    def coarse_left(self, e):
        return roll_right(e, 4)

    def coarse_right(self, e):
        return roll_left(e, 4)

    def last_column(self, x):
        return group_sum(jnp.where(lanes(x.shape) % 4 == 3, x, F32(0.0)))

    def pack(self, a, b, c, d):
        four = lanes(a.shape) % 4
        return jnp.where(four < 2, jnp.where(four == 0, a, b), jnp.where(four == 2, c, d))

    def unpack(self, m, k):
        return group_sum(jnp.where(lanes(m.shape) % 4 == k, m, F32(0.0)))


class Planes:
    coarse_blocks = 2

    def left(self, x):
        a, b, c, d, h = split(x)
        first = lanes(h.shape) == 0
        d, h = roll_right(d), roll_right(h)
        return join([jnp.where(first, h, d), a, b, c, jnp.where(first, d, h)])

    def right(self, x):
        a, b, c, d, h = split(x)
        last = lanes(h.shape) == 127
        a, h = roll_left(a), roll_left(h)
        return join([b, c, d, jnp.where(last, h, a), jnp.where(last, a, h)])

    def coarse_left(self, e):
        o, h = split(e)
        lane = lanes(h.shape)
        end = jnp.broadcast_to(o[:, 127:128], h.shape)
        return join([jnp.where(lane == 0, roll_right(h), roll_right(o)), jnp.where(lane < 4, end, roll_right(h, 4))])

    def coarse_right(self, e):
        o, h = split(e)
        lane = lanes(h.shape)
        end = jnp.broadcast_to(o[:, 0:1], h.shape)
        return join([jnp.where(lane == 127, roll_left(h), roll_left(o)), jnp.where(lane >= 124, end, roll_left(h, 4))])

    def total(self, x):
        a, b, c, d, h = split(x)
        return join([(a + b) + (c + d), group_sum(h)])

    def last_column(self, x):
        h = x[:, 512:640]
        return join([x[:, 384:512], group_sum(jnp.where(lanes(h.shape) % 4 == 3, h, F32(0.0)))])

    def spread(self, e):
        o, h = split(e)
        return join([o, o, o, o, h])

    def take(self, x):
        return join([x[:, 0:128], x[:, 512:640]])

    def pack(self, *fields):
        own, halo = zip(*[split(f) for f in fields])
        a, b, c, d = halo
        four = lanes(a.shape) % 4
        mixed = jnp.where(four < 2, jnp.where(four == 0, a, b), jnp.where(four == 2, c, d))
        return join([*own, mixed])

    def unpack(self, m, k):
        h = m[:, 512:640]
        return join([m[:, k * 128 : k * 128 + 128], group_sum(jnp.where(lanes(h.shape) % 4 == k, h, F32(0.0)))])

    def gather_in(self, parts):
        lane = lanes(parts[0].shape)
        index = (lane % 32) * 4 + lane // 32
        return [jnp.take_along_axis(p, index, axis=1) for p in parts]

    def gather_out(self, parts):
        lane = lanes(parts[0].shape)
        index = (lane % 4) * 32 + lane // 4
        return [jnp.take_along_axis(p, index, axis=1) for p in parts]

    def swap_halves(self, parts):
        a, b, c, d = parts
        low = lanes(a.shape) < 64
        return [
            jnp.where(low, a, roll_right(c, 64)),
            jnp.where(low, b, roll_right(d, 64)),
            jnp.where(low, roll_right(a, 64), c),
            jnp.where(low, roll_right(b, 64), d),
        ]

    def swap_quarters(self, parts):
        a, b, c, d = parts
        low = lanes(a.shape) % 64 < 32
        return [
            jnp.where(low, a, roll_right(b, 32)),
            jnp.where(low, roll_left(a, 32), b),
            jnp.where(low, c, roll_right(d, 32)),
            jnp.where(low, roll_left(c, 32), d),
        ]

    @property
    def steps_in(self):
        return self.gather_in, self.swap_halves, self.swap_quarters

    @property
    def steps_out(self):
        return self.swap_halves, self.swap_quarters, self.gather_out


def layout(blocks):
    return Planes() if blocks == 5 else Wide(128 * (blocks - 1))


def ld(ref, start, count=8, step=1):
    rows_of = pl.ds(start, count, stride=step) if step > 1 else slice(start, start + count)
    return jnp.concatenate([ref[j, rows_of, :] for j in range(ref.shape[0])], axis=1)


def st(ref, start, value, step=1):
    count = value.shape[0]
    rows_of = pl.ds(start, count, stride=step) if step > 1 else slice(start, start + count)
    for j in range(ref.shape[0]):
        ref[j, rows_of, :] = value[:, j * 128 : (j + 1) * 128]


def tree(parts):
    while len(parts) > 1:
        parts = [sum(parts[j + 1 : j + 2], parts[j]) for j in range(0, len(parts), 2)]
    return parts[0]


def four_rows(ref, start, count):
    parts = [ld(ref, start + k, count, 4) for k in range(4)]
    return (parts[0] + parts[1]) + (parts[2] + parts[3])


def position():
    row, col = lax.axis_index("row"), lax.axis_index("col")
    end_row = row == lax.axis_size("row") - 1
    end_col = col == lax.axis_size("col") - 1
    return lax.rem(row, 2) == 1, lax.rem(col, 2) == 1, end_row, end_col


def reorder(steps, sources, targets, spare):
    pairs = list(zip(sources, spare))
    for k, step in enumerate(steps):
        for (x, y), target in zip(pairs, targets):
            x, y = (y, x) if k % 2 else (x, y)
            y = target if k == len(steps) - 1 else y
            for r in range(0, x.shape[1], 8):
                for j, block in enumerate(step([x[j, r : r + 8, :] for j in range(x.shape[0])])):
                    y[j, r : r + 8, :] = block
    if not steps:
        for x, target in zip(sources, targets):
            target[...] = x[...]


def fetch(sources, targets, sems):
    copies = [pltpu.make_async_copy(x, y, sems.at[k]) for k, (x, y) in enumerate(zip(sources, targets))]
    for copy in copies:
        copy.start()
    for copy in copies:
        copy.wait()


def edge_columns(inner, *refs):
    fields, (out, *held, sems) = refs[:6], refs[6:]
    n, width = fields[0].shape
    _, col_odd, end_row, _ = position()
    last = jnp.logical_not(col_odd) if inner else col_odd
    offset = pl.multiple_of(jnp.where(last, width - 128, 0), 128)
    row, lane = rows((8, 128)), lanes((8, 128))
    zero = F32(0.0)
    fetch([f.at[:, pl.ds(offset, 128)] for f in fields], held, sems)

    def pair(x, y):
        low = jnp.where(lane < HC, x, roll_right(y, HC))
        high = jnp.where(lane < HC, roll_right(x, HC), y)
        return jnp.where(last, high, low)

    carry = jnp.zeros((1, 128), F32)
    for r in range(0, n, 8):
        g_x, g_y, w_x, w_y, a, p = [f[r : r + 8, :] for f in held]
        if r == n - 8:
            w_y = jnp.where((row == 7) & end_row, zero, w_y)
        fx = w_x * g_x
        fy = w_y * g_y
        before_x = jnp.where(lane == 0, zero, roll_right(fx))
        before_y = jnp.where(row == 0, jnp.broadcast_to(carry, fy.shape), pltpu.roll(fy, 1, 0))
        carry = fy[7:8, :]
        src = a * p + before_x - fx + before_y - fy
        edge = jnp.broadcast_to(fx[:, 127:128], fx.shape)
        out[r : r + 8, 0:128] = jnp.where((lane == 0) & last, edge, pair(src, w_x))
        out[r : r + 8, 128:256] = pair(w_y, a)
    tail = jnp.broadcast_to(carry, (8, 128))
    tail = pair(tail, tail)
    out[n : n + 8, 0:128] = tail
    out[n : n + 8, 128:256] = tail


def tile_fields(*refs):
    fields, (r_o, wx_o, wy_o, an_o, fx_o, fy_o, *held, raw, spare, tail, sems) = refs[:6], refs[6:]
    gx, gy, wx, wy, an, pr = held
    n, width = gx.shape
    form = layout(width // 128 + 1)
    fetch(fields, held, sems)
    _, _, end_row, end_col = position()
    row, lane = rows((8, width)), lanes((8, width))
    zero = F32(0.0)
    carry = jnp.zeros((1, width), F32)
    for r in range(0, n, 8):
        w_x = jnp.where((lane == width - 1) & end_col, zero, wx[r : r + 8, :])
        w_y = wy[r : r + 8, :]
        if r == n - 8:
            w_y = jnp.where((row == 7) & end_row, zero, w_y)
        fx = w_x * gx[r : r + 8, :]
        fy = w_y * gy[r : r + 8, :]
        a = an[r : r + 8, :]
        before_x = jnp.where(lane == 0, zero, roll_right(fx))
        before_y = jnp.where(row == 0, jnp.broadcast_to(carry, fy.shape), pltpu.roll(fy, 1, 0))
        carry = fy[7:8, :]
        src = a * pr[r : r + 8, :] + before_x - fx + before_y - fy
        for k, x in enumerate((src, w_x, w_y, a)):
            st(raw.at[k], r, x)
        fx_o[r : r + 8, :] = jnp.broadcast_to(fx[:, width - 1 : width], (8, 128))
    st(tail.at[0], 0, jnp.broadcast_to(carry, (8, width)))
    pick = lambda ref: [ref.at[k] for k in range(4)]
    reorder(form.steps_in, [*pick(raw), tail.at[0]], [r_o, wx_o, wy_o, an_o, fy_o], [*pick(spare), tail.at[1]])


def edge_rows(has_outer, r_t, wx_t, wy_t, an_t, fx_t, fy_t, *refs):
    inner, refs = refs[0], refs[1:]
    outer = None
    if has_outer:
        outer, refs = refs[0], refs[1:]
    msg_in, msg_out, r_o, wx_o, wy_o, an_o, fy_o, g_o, cr_o, cd_o, ca_o, u_s, t_s, f_s, tops = refs
    own, n, _ = r_t.shape
    form = layout(own + 1)
    row_odd, odd, _, _ = position()
    lane = lanes((8, 128))
    zero = F32(0.0)

    def halo(r, c):
        x = inner[r : r + 8, c : c + 128]
        y = outer[r : r + 8, c : c + 128] if has_outer else jnp.zeros_like(x)
        before, after = jnp.where(odd, x, y), jnp.where(odd, y, x)
        first = jnp.where(lane < HC, after, roll_right(before, HC))
        second = jnp.where(lane < HC, roll_right(after, HC), before)
        return first, second

    for r in range(0, n, 8):
        src_h, wx_h = halo(r, 0)
        wy_h, an_h = halo(r, 128)
        incoming = jnp.broadcast_to(src_h[:, HC : HC + 1], (8, 128))
        src_h = jnp.where(lane == 0, src_h + fx_t[r : r + 8, :], jnp.where(lane == HC, zero, src_h))
        for out, tile, h in ((r_o, r_t, src_h), (wx_o, wx_t, wx_h), (wy_o, wy_t, wy_h), (an_o, an_t, an_h)):
            for j in range(own):
                x = tile[j, r : r + 8, :]
                if out is r_o and j == 0:
                    x = jnp.where(lane == 0, x + incoming, x)
                out[j, r : r + 8, :] = x
            out[own, r : r + 8, :] = h
    for j in range(own):
        fy_o[j] = fy_t[j]
    fy_o[own] = halo(n, 0)[0]

    lo, hi = 16, n - 32
    for base in (lo, hi):
        for r in range(base - 8, base + 24, 8):
            w_x, w_y = ld(wx_o, r), ld(wy_o, r)
            diag = ld(an_o, r) + w_x + form.left(w_x) + w_y + ld(wy_o, r - 1)
            st(u_s, r, jnp.where(diag > zero, ld(r_o, r) / diag, zero))
    for base in (lo, hi):
        flows(form, u_s, wx_o, f_s, range(base, base + 16, 8))
    for base in (lo, hi):
        for r in range(base, base + 16, 8):
            st(t_s, r, apply_a(u_s, form.left, f_s, wy_o, an_o, r))
    packed_s = []
    for base in (lo, hi):
        sums = form.total(four_rows(t_s, base, 4))
        packed_s.append(form.pack(*[sums[k : k + 1] for k in range(4)]))
    packed = []
    for k, c in enumerate(range(lo, n - lo, 32)):
        c_r = form.last_column(four_rows(wx_o, c, 8))
        c_d = form.total(ld(wy_o, c + 3, 8, 4))
        c_a = form.total(four_rows(an_o, c, 8))
        g = form.total(four_rows(r_o, c, 8))
        packed.append(form.pack(g, c_r, c_d, c_a))
        for out, x in ((g_o, g), (cr_o, c_r), (cd_o, c_d), (ca_o, c_a)):
            st(out, 8 * k, x)

    top, bottom = tops.at[0], tops.at[1]
    for k, ref in enumerate((r_o, wx_o, wy_o, an_o)):
        top[:, k * HR : (k + 1) * HR, :] = ref[:, 0:HR, :]
        bottom[:, k * HR : (k + 1) * HR, :] = ref[:, n - HR : n, :]
    st(top, HR - 1, packed_s[0])
    st(bottom, 0, packed_s[1])
    st(bottom, HR, form.spread(ld(cd_o, cd_o.shape[1] - 9, 1)))
    st(bottom, 3 * HR, ld(fy_o, 0, 1))
    st(top, 4 * HR, packed[0])
    st(bottom, 4 * HR, packed[-1])

    @pl.when(row_odd)
    def _():
        msg_in[...] = top[...]
        msg_out[...] = bottom[...]

    @pl.when(jnp.logical_not(row_odd))
    def _():
        msg_in[...] = bottom[...]
        msg_out[...] = top[...]


def inverse_diagonal(wx, wy, an, di):
    form = layout(wx.shape[0])
    for r in range(8, wx.shape[1], 8):
        w_x, w_y = ld(wx, r), ld(wy, r)
        diag = ld(an, r) + w_x + form.left(w_x) + w_y + ld(wy, r - 1)
        st(di, r, jnp.where(diag > F32(0.0), F32(1.0) / diag, F32(0.0)))


def flows(form, v, w_x, flow, starts):
    for r in starts:
        x = ld(v, r)
        st(flow, r, ld(w_x, r) * (x - form.right(x)))


def apply_a(v, flow_left, flow, w_y, an, r):
    x = ld(v, r)
    down = ld(w_y, r) * (x - ld(v, r + 1))
    up = ld(w_y, r - 1) * (x - ld(v, r - 1))
    return (ld(an, r) * x + (ld(flow, r) - flow_left(ld(flow, r)))) + (down + up)


def basis(r_i, wx_i, wy_i, an_i, fy_i, g_i, cr_i, cd_i, ca_i, di_i, msg_in, msg_out, mom, p0, p1, p2, q0, q1, q2, r0,
         R, WX, WY, AN, DI, SP, PA, PB, QA, FL, C_L, C_R, C_D, C_A, C_I, EA, EB, GC):
    blocks, n, _ = r_i.shape
    form = layout(blocks)
    fine = n + 2 * FG
    coarse = fine // 4 + 12
    zero = F32(0.0)
    odd, _, _, _ = position()
    own_blocks = blocks - 1
    B = GUARD

    def sides(a, b):
        x, y = ld(msg_in, a, b - a), ld(msg_out, a, b - a)
        return jnp.where(odd, x, y), jnp.where(odd, y, x)

    zeros = jnp.zeros((B, blocks * 128), F32)
    coarse_zeros = jnp.zeros((B, form.coarse_blocks * 128), F32)
    for ref in (R, WX, WY, AN, PA, PB):
        st(ref, 0, zeros)
        st(ref, B + fine, zeros)
    for k, (ref, own) in enumerate(((R, r_i), (WX, wx_i), (WY, wy_i), (AN, an_i))):
        up, down = sides(k * HR, (k + 1) * HR)
        st(ref, B, zeros[: FG - HR])
        st(ref, B + FG + n + HR, zeros[: FG - HR])
        st(ref, B + FG - HR, up)
        st(ref, B + FG + n, down)
        for r in range(0, n, 8):
            st(ref, B + FG + r, ld(own, r))
    flux_up, _ = sides(3 * HR, 3 * HR + 1)
    st(R, B + FG, ld(R, B + FG, 1) + flux_up)
    st(R, B + FG + n, ld(R, B + FG + n, 1) + ld(fy_i, 0, 1))

    for r in range(8, n, 8):
        st(DI, B + FG + r, ld(di_i, r))
    for r in [*range(B, B + FG + 8, 8), *range(B + FG + n, B + fine, 8)]:
        w_x, w_y = ld(WX, r), ld(WY, r)
        diag = ld(AN, r) + w_x + form.left(w_x) + w_y + ld(WY, r - 1)
        st(DI, r, jnp.where(diag > zero, F32(1.0) / diag, zero))

    for ref in (EA, EB, C_D):
        st(ref, 0, coarse_zeros)
        st(ref, B + coarse, coarse_zeros)
    up, down = sides(4 * HR, 4 * HR + 8)
    for k, ref in enumerate((GC, C_R, C_D, C_A)):
        st(ref, B, form.unpack(up, k))
        st(ref, B + coarse - 8, form.unpack(down, k))
    beyond, _ = sides(HR, HR + 1)
    st(C_D, B - 1, form.take(beyond))
    for ref, own in ((GC, g_i), (C_R, cr_i), (C_D, cd_i), (C_A, ca_i)):
        for r in range(0, own.shape[1], 8):
            st(ref, B + 16 + r, ld(own, r))
    for c in (8, coarse - 16):
        f = B + 4 * c - 24
        st(GC, B + c, form.total(four_rows(R, f, 8)))
        st(C_R, B + c, form.last_column(four_rows(WX, f, 8)))
        st(C_D, B + c, form.total(ld(WY, f + 3, 8, 4)))
        st(C_A, B + c, form.total(four_rows(AN, f, 8)))
    for c in range(B, B + coarse, 8):
        c_r = ld(C_R, c)
        c_l = form.coarse_left(c_r)
        total = ld(C_A, c) + c_l + c_r + ld(C_D, c - 1) + ld(C_D, c)
        st(C_L, c, c_l)
        st(C_I, c, jnp.where(total > zero, F32(DAMP) / total, zero))

    def smooth(lo, hi):
        for c in range(lo, hi, 8):
            st(EA, B + c, ld(C_I, B + c) * ld(GC, B + c))
        if lo > 0:
            st(EA, B + lo - 8, coarse_zeros)
            st(EB, B + lo - 8, coarse_zeros)
        if hi < coarse:
            st(EA, B + hi, coarse_zeros)
            st(EB, B + hi, coarse_zeros)
        old, new = EA, EB
        for turn in range(3):
            for c in range(B + lo, B + hi, 8):
                e = ld(old, c)
                beside = ld(C_L, c) * form.coarse_left(e) + ld(C_R, c) * form.coarse_right(e)
                beside = beside + (ld(C_D, c - 1) * ld(old, c - 1) + ld(C_D, c) * ld(old, c + 1))
                st(new, c, F32(1.0 - DAMP) * e + ld(C_I, c) * (ld(GC, c) + beside))
            old, new = new, old
        first, last = max(lo, 6), min(hi, coarse - 6)
        count = last - first
        for k in range(4):
            st(SP, B + 4 * (first - 6) + k, form.spread(ld(EB, B + first, count)), 4)

    def restrict(q):
        for c in range(8, coarse - 8, 8):
            st(GC, B + c, form.total(four_rows(q, B + 4 * c - 24, 8)))

    smooth(0, coarse)
    for r in range(B, B + fine, 8):
        st(PA, r, ld(DI, r) * ld(R, r) + ld(SP, r))
    flows(form, PA, WX, FL, range(B, B + fine, 8))
    for r in range(B, B + fine, 8):
        st(QA, r, apply_a(PA, form.left, FL, WY, AN, r))
    restrict(QA)
    s_up, _ = sides(0, 1)
    _, s_down = sides(HR - 1, HR)
    for c, s, off in ((0, s_up, 4), (coarse - 8, s_down, 0)):
        c = B + c
        e = ld(EB, c)
        part = jnp.zeros_like(e)
        for k in range(4):
            part = jnp.where(rows(e.shape) == off + k, jnp.broadcast_to(form.unpack(s, k), e.shape), part)
        image = ld(C_A, c) * e + ld(C_L, c) * (e - form.coarse_left(e)) + ld(C_R, c) * (e - form.coarse_right(e))
        image = image + ld(C_D, c - 1) * (e - ld(EB, c - 1))
        image = image + ld(C_D, c) * (e - ld(EB, c + 1))
        st(GC, c, part + image)
    for r in range(0, n, 8):
        f = B + FG + r
        for out, ref in ((p0, PA), (q0, QA), (r0, R)):
            out[:, r : r + 8, :] = ref[:own_blocks, f : f + 8, :]
    smooth(0, coarse)
    for r in range(B, B + fine, 8):
        st(PB, r, (ld(DI, r) * ld(QA, r) + ld(SP, r)) - F32(SHIFT) * ld(PA, r))
    flows(form, PB, WX, FL, range(B + 8, B + fine - 8, 8))
    for r in range(B + 8, B + fine - 8, 8):
        st(QA, r, apply_a(PB, form.left, FL, WY, AN, r))
    restrict(QA)
    for r in range(0, n, 8):
        f = B + FG + r
        for out, ref in ((p1, PB), (q1, QA)):
            out[:, r : r + 8, :] = ref[:own_blocks, f : f + 8, :]
    smooth(8, coarse - 8)
    for r in range(B + FG - 8, B + FG + n + 8, 8):
        st(PA, r, (ld(DI, r) * ld(QA, r) + ld(SP, r)) - F32(SHIFT) * ld(PB, r))
    flows(form, PA, WX, FL, range(B + FG, B + FG + n, 8))
    acc = [jnp.zeros((8, 128), F32) for _ in range(9)]
    for r in range(0, n, 8):
        f = B + FG + r
        image = apply_a(PA, form.left, FL, WY, AN, f)
        sums = [[] for _ in acc]
        for j in range(own_blocks):
            z2, i2 = PA[j, f : f + 8, :], image[:, j * 128 : (j + 1) * 128]
            p2[j, r : r + 8, :] = z2
            q2[j, r : r + 8, :] = i2
            z0, z1, i0, i1, res = [x[j, r : r + 8, :] for x in (p0, p1, q0, q1, r0)]
            pairs = ((z0, i0), (z1, i0), (z1, i1), (z2, i0), (z2, i1), (z2, i2), (z0, res), (z1, res), (z2, res))
            for k, (x, y) in enumerate(pairs):
                sums[k].append(x * y)
        for k, parts in enumerate(sums):
            acc[k] = acc[k] + tree(parts)
    lane = lanes((8, 128))
    line = jnp.zeros((8, 128), F32)
    for k in range(9):
        total = jnp.sum(jnp.sum(acc[k], axis=0, keepdims=True), axis=1, keepdims=True)
        line = jnp.where(lane == k, jnp.broadcast_to(total, (8, 128)), line)
    for j in range(mom.shape[0]):
        mom[j] = line


def combine(mom, p0, p1, p2, q0, q1, q2, r0, heights, residual, work):
    blocks, n, _ = p0.shape
    form = layout(blocks + 1)
    tot = tree([mom[j] for j in range(mom.shape[0])])
    m = [jnp.broadcast_to(tot[:, k : k + 1], (8, 128)) for k in range(9)]
    g00, g10, g11, g20, g21, g22, b0, b1, b2 = m
    l10, l20 = g10 / g00, g20 / g00
    d1 = g11 - l10 * g10
    t21 = g21 - l20 * g10
    l21 = t21 / d1
    d2 = g22 - l20 * g20 - l21 * t21
    y1 = b1 - l10 * b0
    y2 = b2 - l20 * b0 - l21 * y1
    x2 = y2 / d2
    x1 = y1 / d1 - l21 * x2
    x0 = b0 / g00 - l10 * x1 - l20 * x2
    sums, spare, done = [[work.at[k], work.at[k + 1]] for k in (0, 2, 4)]
    for r in range(0, n, 8):
        for j in range(blocks):
            z0, z1, z2, i0, i1, i2, res = [x[j, r : r + 8, :] for x in (p0, p1, p2, q0, q1, q2, r0)]
            sums[0][j, r : r + 8, :] = x0 * z0 + x1 * z1 + x2 * z2
            sums[1][j, r : r + 8, :] = res - (x0 * i0 + x1 * i1 + x2 * i2)
    reorder(form.steps_out, sums, done, spare)
    for r in range(0, n, 8):
        heights[r : r + 8, :] = ld(done[0], r)
        residual[r : r + 8, :] = ld(done[1], r)


def swap(x, axis, size, inner):
    if inner:
        pairs = [(i, i ^ 1) for i in range(size) if i ^ 1 < size]
    else:
        pairs = [(i, j) for i in range(size) for j in [((i + 1) ^ 1) - 1] if 0 <= j < size]
    return lax.ppermute(x, axis, pairs)


def local(nrow, ncol, gx, gy, wx, wy, an, pr):
    n, width = gx.shape
    ext = width + 2 * HC
    fields = tuple(pltpu.with_memory_space_constraint(f, pltpu.HBM) for f in (gx, gy, wx, wy, an, pr))
    nb = ext // 128
    shape = lambda *dims: jax.ShapeDtypeStruct(dims, F32)
    params = pltpu.CompilerParams(vmem_limit_bytes=48 * 1024 * 1024)

    def call(kernel, name, args, outs, scratch=(), us=1, fetches=0):
        sems = [pltpu.SemaphoreType.DMA((fetches,))] if fetches else []
        return pl.pallas_call(
            kernel,
            in_specs=[HBM if fetches else VMEM] * len(args),
            out_specs=[VMEM] * len(outs),
            out_shape=outs,
            scratch_shapes=[pltpu.VMEM(dims, F32) for dims in scratch] + sems,
            compiler_params=params,
            cost_estimate=pl.CostEstimate(flops=us * 2_000_000, bytes_accessed=us * 2_000_000, transcendentals=0),
            name=name,
        )(*args)

    halos = []
    for inner in (True, False) if ncol > 2 else (True,):
        (edge,) = call(functools.partial(edge_columns, inner), "edge_columns", fields, [shape(n + 8, 256)], [(n, 128)] * 6, 1, 6)
        halos.append(swap(edge, "col", ncol, inner))
    tile = shape(nb - 1, n, 128)
    own = call(tile_fields, "tile_fields", fields, [tile] * 4 + [shape(n, 128), shape(nb - 1, 8, 128)], [(n, width)] * 6 + [(4, nb - 1, n, 128)] * 2 + [(2, nb - 1, 8, 128)], 1, 6)
    depth = 4 * HR + 8
    lo = 16
    cb = layout(nb).coarse_blocks
    far = shape(cb, (n - 2 * lo) // 4, 128)
    msg = shape(nb, depth, 128)
    field = shape(nb, n, 128)
    to_in, to_out, r_e, wx_e, wy_e, an_e, *rest = call(
        functools.partial(edge_rows, len(halos) > 1),
        "edge_rows",
        (*own, *halos),
        [msg, msg] + [field] * 4 + [shape(nb, 8, 128)] + [far] * 4,
        [(nb, n, 128)] * 3 + [(2, nb, depth, 128)],
    )
    from_out = swap(to_out, "row", nrow, False)
    from_in = swap(to_in, "row", nrow, True)
    (di,) = call(inverse_diagonal, "inverse_diagonal", (wx_e, wy_e, an_e), [field])
    fine = n + 2 * FG
    coarse = fine // 4 + 12
    mom, *vectors = call(
        basis,
        "basis",
        (r_e, wx_e, wy_e, an_e, *rest, di, from_in, from_out),
        [shape(nrow * ncol, 8, 128)] + [tile] * 7,
        [(nb, fine + 2 * GUARD, 128)] * 10 + [(cb, coarse + 2 * GUARD, 128)] * 8,
    )
    mom = lax.all_to_all(mom, ("row", "col"), 0, 0, tiled=True)
    out = shape(n, width)
    return tuple(call(combine, "combine", (mom, *vectors), [out, out], [(6, nb - 1, n, 128)]))


def solution(mesh):
    spec = P("row", "col")
    return jax.shard_map(
        functools.partial(local, mesh.shape["row"], mesh.shape["col"]),
        mesh=mesh,
        in_specs=(spec,) * 6,
        out_specs=(spec, spec),
        check_vma=False,
    )
```

```python
import functools

import jax
import jax.numpy as jnp
from jax import lax
from jax.experimental import pallas as pl
from jax.experimental.pallas import tpu as pltpu
from jax.sharding import PartitionSpec as P

DAMP = 2.0 / 3.0
SHIFT = 1.0
HC = 64
HR = 20
FG = 24
GUARD = 8
VMEM = pl.BlockSpec(memory_space=pltpu.VMEM)
HBM = pl.BlockSpec(memory_space=pltpu.HBM)
F32 = jnp.float32


def lanes(shape):
    return lax.broadcasted_iota(jnp.int32, shape, 1)


def rows(shape):
    return lax.broadcasted_iota(jnp.int32, shape, 0)


def roll_right(x, k=1):
    return pltpu.roll(x, k, 1)


def roll_left(x, k=1):
    return pltpu.roll(x, x.shape[1] - k, 1)


def group_sum(x):
    lane = lanes(x.shape)
    x = x + jnp.where(lane % 2 == 0, roll_left(x), roll_right(x))
    return x + jnp.where(lane % 4 < 2, roll_left(x, 2), roll_right(x, 2))


def split(x):
    return [x[:, j : j + 128] for j in range(0, x.shape[1], 128)]


def join(parts):
    return jnp.concatenate(parts, axis=1)


class Wide:
    def __init__(self, width):
        self.coarse_blocks = width // 128 + 1

    left, right = staticmethod(roll_right), staticmethod(roll_left)
    total = staticmethod(group_sum)
    spread = take = staticmethod(lambda x: x)
    steps_in = steps_out = ()

    def coarse_left(self, e):
        return roll_right(e, 4)

    def coarse_right(self, e):
        return roll_left(e, 4)

    def last_column(self, x):
        return group_sum(jnp.where(lanes(x.shape) % 4 == 3, x, F32(0.0)))

    def pack(self, a, b, c, d):
        four = lanes(a.shape) % 4
        return jnp.where(four < 2, jnp.where(four == 0, a, b), jnp.where(four == 2, c, d))

    def unpack(self, m, k):
        return group_sum(jnp.where(lanes(m.shape) % 4 == k, m, F32(0.0)))


class Planes:
    coarse_blocks = 2

    def left(self, x):
        a, b, c, d, h = split(x)
        first = lanes(h.shape) == 0
        d, h = roll_right(d), roll_right(h)
        return join([jnp.where(first, h, d), a, b, c, jnp.where(first, d, h)])

    def right(self, x):
        a, b, c, d, h = split(x)
        last = lanes(h.shape) == 127
        a, h = roll_left(a), roll_left(h)
        return join([b, c, d, jnp.where(last, h, a), jnp.where(last, a, h)])

    def coarse_left(self, e):
        o, h = split(e)
        lane = lanes(h.shape)
        end = jnp.broadcast_to(o[:, 127:128], h.shape)
        return join([jnp.where(lane == 0, roll_right(h), roll_right(o)), jnp.where(lane < 4, end, roll_right(h, 4))])

    def coarse_right(self, e):
        o, h = split(e)
        lane = lanes(h.shape)
        end = jnp.broadcast_to(o[:, 0:1], h.shape)
        return join([jnp.where(lane == 127, roll_left(h), roll_left(o)), jnp.where(lane >= 124, end, roll_left(h, 4))])

    def total(self, x):
        a, b, c, d, h = split(x)
        return join([(a + b) + (c + d), group_sum(h)])

    def last_column(self, x):
        h = x[:, 512:640]
        return join([x[:, 384:512], group_sum(jnp.where(lanes(h.shape) % 4 == 3, h, F32(0.0)))])

    def spread(self, e):
        o, h = split(e)
        return join([o, o, o, o, h])

    def take(self, x):
        return join([x[:, 0:128], x[:, 512:640]])

    def pack(self, *fields):
        own, halo = zip(*[split(f) for f in fields])
        a, b, c, d = halo
        four = lanes(a.shape) % 4
        mixed = jnp.where(four < 2, jnp.where(four == 0, a, b), jnp.where(four == 2, c, d))
        return join([*own, mixed])

    def unpack(self, m, k):
        h = m[:, 512:640]
        return join([m[:, k * 128 : k * 128 + 128], group_sum(jnp.where(lanes(h.shape) % 4 == k, h, F32(0.0)))])

    def gather_in(self, parts):
        lane = lanes(parts[0].shape)
        index = (lane % 32) * 4 + lane // 32
        return [jnp.take_along_axis(p, index, axis=1) for p in parts]

    def gather_out(self, parts):
        lane = lanes(parts[0].shape)
        index = (lane % 4) * 32 + lane // 4
        return [jnp.take_along_axis(p, index, axis=1) for p in parts]

    def swap_halves(self, parts):
        a, b, c, d = parts
        low = lanes(a.shape) < 64
        return [
            jnp.where(low, a, roll_right(c, 64)),
            jnp.where(low, b, roll_right(d, 64)),
            jnp.where(low, roll_right(a, 64), c),
            jnp.where(low, roll_right(b, 64), d),
        ]

    def swap_quarters(self, parts):
        a, b, c, d = parts
        low = lanes(a.shape) % 64 < 32
        return [
            jnp.where(low, a, roll_right(b, 32)),
            jnp.where(low, roll_left(a, 32), b),
            jnp.where(low, c, roll_right(d, 32)),
            jnp.where(low, roll_left(c, 32), d),
        ]

    @property
    def steps_in(self):
        return self.gather_in, self.swap_halves, self.swap_quarters

    @property
    def steps_out(self):
        return self.swap_halves, self.swap_quarters, self.gather_out


def layout(blocks):
    return Planes() if blocks == 5 else Wide(128 * (blocks - 1))


def ld(ref, start, count=8, step=1):
    rows_of = pl.ds(start, count, stride=step) if step > 1 else pl.ds(start, count)
    return jnp.concatenate([ref[j, rows_of, :] for j in range(ref.shape[0])], axis=1)


def st(ref, start, value, step=1):
    count = value.shape[0]
    rows_of = pl.ds(start, count, stride=step) if step > 1 else pl.ds(start, count)
    for j in range(ref.shape[0]):
        ref[j, rows_of, :] = value[:, j * 128 : (j + 1) * 128]


def tree(parts):
    while len(parts) > 1:
        parts = [sum(parts[j + 1 : j + 2], parts[j]) for j in range(0, len(parts), 2)]
    return parts[0]


def four_rows(ref, start, count):
    parts = [ld(ref, start + k, count, 4) for k in range(4)]
    return (parts[0] + parts[1]) + (parts[2] + parts[3])


def position():
    row, col = lax.axis_index("row"), lax.axis_index("col")
    end_row = row == lax.axis_size("row") - 1
    end_col = col == lax.axis_size("col") - 1
    return lax.rem(row, 2) == 1, lax.rem(col, 2) == 1, end_row, end_col


def reorder(steps, sources, targets, spare):
    pairs = list(zip(sources, spare))
    for k, step in enumerate(steps):
        for (x, y), target in zip(pairs, targets):
            x, y = (y, x) if k % 2 else (x, y)
            y = target if k == len(steps) - 1 else y
            for r in range(0, x.shape[1], 8):
                for j, block in enumerate(step([x[j, r : r + 8, :] for j in range(x.shape[0])])):
                    y[j, r : r + 8, :] = block
    if not steps:
        for x, target in zip(sources, targets):
            target[...] = x[...]


def fetch(sources, targets, sems):
    copies = [pltpu.make_async_copy(x, y, sems.at[k]) for k, (x, y) in enumerate(zip(sources, targets))]
    for copy in copies:
        copy.start()
    for copy in copies:
        copy.wait()


def edge_columns(inner, *refs):
    fields, (out, *held, sems) = refs[:6], refs[6:]
    n, width = fields[0].shape
    _, col_odd, end_row, _ = position()
    last = jnp.logical_not(col_odd) if inner else col_odd
    offset = pl.multiple_of(jnp.where(last, width - 128, 0), 128)
    row, lane = rows((8, 128)), lanes((8, 128))
    zero = F32(0.0)
    fetch([f.at[:, pl.ds(offset, 128)] for f in fields], held, sems)

    def pair(x, y):
        low = jnp.where(lane < HC, x, roll_right(y, HC))
        high = jnp.where(lane < HC, roll_right(x, HC), y)
        return jnp.where(last, high, low)

    carry = jnp.zeros((1, 128), F32)
    for r in range(0, n, 8):
        g_x, g_y, w_x, w_y, a, p = [f[r : r + 8, :] for f in held]
        if r == n - 8:
            w_y = jnp.where((row == 7) & end_row, zero, w_y)
        fx = w_x * g_x
        fy = w_y * g_y
        before_x = jnp.where(lane == 0, zero, roll_right(fx))
        before_y = jnp.where(row == 0, jnp.broadcast_to(carry, fy.shape), pltpu.roll(fy, 1, 0))
        carry = fy[7:8, :]
        src = a * p + before_x - fx + before_y - fy
        edge = jnp.broadcast_to(fx[:, 127:128], fx.shape)
        out[r : r + 8, 0:128] = jnp.where((lane == 0) & last, edge, pair(src, w_x))
        out[r : r + 8, 128:256] = pair(w_y, a)
    tail = jnp.broadcast_to(carry, (8, 128))
    tail = pair(tail, tail)
    out[n : n + 8, 0:128] = tail
    out[n : n + 8, 128:256] = tail


def tile_fields(*refs):
    fields, (r_o, wx_o, wy_o, an_o, fx_o, fy_o, *held, raw, spare, tail, sems) = refs[:6], refs[6:]
    gx, gy, wx, wy, an, pr = held
    n, width = gx.shape
    form = layout(width // 128 + 1)
    fetch(fields, held, sems)
    _, _, end_row, end_col = position()
    row, lane = rows((8, width)), lanes((8, width))
    zero = F32(0.0)
    carry = jnp.zeros((1, width), F32)
    for r in range(0, n, 8):
        w_x = jnp.where((lane == width - 1) & end_col, zero, wx[r : r + 8, :])
        w_y = wy[r : r + 8, :]
        if r == n - 8:
            w_y = jnp.where((row == 7) & end_row, zero, w_y)
        fx = w_x * gx[r : r + 8, :]
        fy = w_y * gy[r : r + 8, :]
        a = an[r : r + 8, :]
        before_x = jnp.where(lane == 0, zero, roll_right(fx))
        before_y = jnp.where(row == 0, jnp.broadcast_to(carry, fy.shape), pltpu.roll(fy, 1, 0))
        carry = fy[7:8, :]
        src = a * pr[r : r + 8, :] + before_x - fx + before_y - fy
        for k, x in enumerate((src, w_x, w_y, a)):
            st(raw.at[k], r, x)
        fx_o[r : r + 8, :] = jnp.broadcast_to(fx[:, width - 1 : width], (8, 128))
    st(tail.at[0], 0, jnp.broadcast_to(carry, (8, width)))
    pick = lambda ref: [ref.at[k] for k in range(4)]
    reorder(form.steps_in, [*pick(raw), tail.at[0]], [r_o, wx_o, wy_o, an_o, fy_o], [*pick(spare), tail.at[1]])


def edge_rows(has_outer, r_t, wx_t, wy_t, an_t, fx_t, fy_t, *refs):
    inner, refs = refs[0], refs[1:]
    outer = None
    if has_outer:
        outer, refs = refs[0], refs[1:]
    r_o, wx_o, wy_o, an_o, fy_o, *rest = refs
    own, n, _ = r_t.shape
    form = layout(own + 1)
    row_odd, odd, _, _ = position()
    lane = lanes((8, 128))
    zero = F32(0.0)

    def halo(r, c):
        x = inner[r : r + 8, c : c + 128]
        y = outer[r : r + 8, c : c + 128] if has_outer else jnp.zeros_like(x)
        before, after = jnp.where(odd, x, y), jnp.where(odd, y, x)
        first = jnp.where(lane < HC, after, roll_right(before, HC))
        second = jnp.where(lane < HC, roll_right(after, HC), before)
        return first, second

    for r in range(0, n, 8):
        src_h, wx_h = halo(r, 0)
        wy_h, an_h = halo(r, 128)
        incoming = jnp.broadcast_to(src_h[:, HC : HC + 1], (8, 128))
        src_h = jnp.where(lane == 0, src_h + fx_t[r : r + 8, :], jnp.where(lane == HC, zero, src_h))
        for out, tile, h in ((r_o, r_t, src_h), (wx_o, wx_t, wx_h), (wy_o, wy_t, wy_h), (an_o, an_t, an_h)):
            for j in range(own):
                x = tile[j, r : r + 8, :]
                if out is r_o and j == 0:
                    x = jnp.where(lane == 0, x + incoming, x)
                out[j, r : r + 8, :] = x
            out[own, r : r + 8, :] = h
    for j in range(own):
        fy_o[j] = fy_t[j]
    fy_o[own] = halo(n, 0)[0]

    message(form, row_odd, r_o, wx_o, wy_o, an_o, fy_o, *rest)


def near_rows(r_i, wx_i, wy_i, an_i, fy_i, di, *rest):
    form = layout(wx_i.shape[0])
    row_odd, _, _, _ = position()
    message(form, jnp.logical_not(row_odd), r_i, wx_i, wy_i, an_i, fy_i, *rest)
    for r in range(8, wx_i.shape[1], 8):
        w_x, w_y = ld(wx_i, r), ld(wy_i, r)
        diag = ld(an_i, r) + w_x + form.left(w_x) + w_y + ld(wy_i, r - 1)
        st(di, r, jnp.where(diag > F32(0.0), F32(1.0) / diag, F32(0.0)))


def message(form, bottom, r_o, wx_o, wy_o, an_o, fy_o, msg, g_o, cr_o, cd_o, ca_o, u_s, t_s, f_s):
    n = r_o.shape[1]
    zero = F32(0.0)

    def pick(low, high):
        return jnp.where(bottom, high, low)

    base = pl.multiple_of(pick(16, n - 32), 8)
    for r in range(0, 32, 8):
        at = pl.multiple_of(base - 8 + r, 8)
        w_x, w_y = ld(wx_o, at), ld(wy_o, at)
        diag = ld(an_o, at) + w_x + form.left(w_x) + w_y + ld(wy_o, base - 9 + r)
        st(u_s, 8 + r, jnp.where(diag > zero, ld(r_o, at) / diag, zero))
    for r in (0, 8):
        x = ld(u_s, 16 + r)
        st(f_s, r, ld(wx_o, pl.multiple_of(base + r, 8)) * (x - form.right(x)))
    for r in (0, 8):
        at = pl.multiple_of(base + r, 8)
        x, flow = ld(u_s, 16 + r), ld(f_s, r)
        down = ld(wy_o, at) * (x - ld(u_s, 17 + r))
        up = ld(wy_o, base + r - 1) * (x - ld(u_s, 15 + r))
        st(t_s, r, (ld(an_o, at) * x + (flow - form.left(flow))) + (down + up))
    sums = form.total(four_rows(t_s, 0, 4))
    c = pl.multiple_of(pick(16, n - 48), 8)
    coarse = (
        form.total(four_rows(r_o, c, 8)),
        form.last_column(four_rows(wx_o, c, 8)),
        form.total(ld(wy_o, c + 3, 8, 4)),
        form.total(four_rows(an_o, c, 8)),
    )
    for out, x in zip((g_o, cr_o, cd_o, ca_o), coarse):
        st(out, 0, x)
    start = pick(0, n - HR)
    for k, ref in enumerate((r_o, wx_o, wy_o, an_o)):
        for r in range(0, HR, 4):
            st(msg, k * HR + r, ld(ref, start + r, 4))
    outer = pick(HR - 1, 0)
    st(msg, outer, form.pack(*[sums[k : k + 1] for k in range(4)]))
    st(msg, HR + outer, form.spread(form.total(ld(wy_o, n - 49, 1))))
    st(msg, 3 * HR + outer, ld(fy_o, 0, 1))
    st(msg, 4 * HR, form.pack(*coarse))


def flows(form, v, w_x, flow, starts):
    for r in starts:
        x = ld(v, r)
        st(flow, r, ld(w_x, r) * (x - form.right(x)))


def apply_a(v, flow_left, flow, w_y, an, r):
    x = ld(v, r)
    down = ld(w_y, r) * (x - ld(v, r + 1))
    up = ld(w_y, r - 1) * (x - ld(v, r - 1))
    return (ld(an, r) * x + (ld(flow, r) - flow_left(ld(flow, r)))) + (down + up)


def basis(r_i, wx_i, wy_i, an_i, fy_i, g_a, cr_a, cd_a, ca_a, di_i, g_b, cr_b, cd_b, ca_b, msg_in, msg_out, mom, p0, p1, p2, q0, q1, q2, r0,
         R, WX, WY, AN, DI, SP, PA, PB, QA, FL, C_L, C_R, C_D, C_A, C_I, EA, EB, GC):
    blocks, n, _ = r_i.shape
    form = layout(blocks)
    fine = n + 2 * FG
    coarse = fine // 4 + 12
    zero = F32(0.0)
    odd, _, _, _ = position()
    own_blocks = blocks - 1
    B = GUARD

    def sides(a, b):
        x, y = ld(msg_in, a, b - a), ld(msg_out, a, b - a)
        return jnp.where(odd, x, y), jnp.where(odd, y, x)

    zeros = jnp.zeros((B, blocks * 128), F32)
    coarse_zeros = jnp.zeros((B, form.coarse_blocks * 128), F32)
    for ref in (R, WX, WY, AN, PA, PB):
        st(ref, 0, zeros)
        st(ref, B + fine, zeros)
    for k, (ref, own) in enumerate(((R, r_i), (WX, wx_i), (WY, wy_i), (AN, an_i))):
        up, down = sides(k * HR, (k + 1) * HR)
        st(ref, B, zeros[: FG - HR])
        st(ref, B + FG + n + HR, zeros[: FG - HR])
        st(ref, B + FG - HR, up)
        st(ref, B + FG + n, down)
        for r in range(0, n, 8):
            st(ref, B + FG + r, ld(own, r))
    flux_up, _ = sides(3 * HR, 3 * HR + 1)
    st(R, B + FG, ld(R, B + FG, 1) + flux_up)
    st(R, B + FG + n, ld(R, B + FG + n, 1) + ld(fy_i, 0, 1))

    for r in range(8, n, 8):
        st(DI, B + FG + r, ld(di_i, r))
    for r in [*range(B, B + FG + 8, 8), *range(B + FG + n, B + fine, 8)]:
        w_x, w_y = ld(WX, r), ld(WY, r)
        diag = ld(AN, r) + w_x + form.left(w_x) + w_y + ld(WY, r - 1)
        st(DI, r, jnp.where(diag > zero, F32(1.0) / diag, zero))

    for ref in (EA, EB, C_D):
        st(ref, 0, coarse_zeros)
        st(ref, B + coarse, coarse_zeros)
    up, down = sides(4 * HR, 4 * HR + 8)
    for k, ref in enumerate((GC, C_R, C_D, C_A)):
        st(ref, B, form.unpack(up, k))
        st(ref, B + coarse - 8, form.unpack(down, k))
    beyond, _ = sides(HR, HR + 1)
    st(C_D, B - 1, form.take(beyond))
    for ref, a, b in ((GC, g_a, g_b), (C_R, cr_a, cr_b), (C_D, cd_a, cd_b), (C_A, ca_a, ca_b)):
        x, y = ld(a, 0), ld(b, 0)
        st(ref, B + 16, jnp.where(odd, y, x))
        st(ref, B + 24, jnp.where(odd, x, y))
    for c in (8, coarse - 16):
        f = B + 4 * c - 24
        st(GC, B + c, form.total(four_rows(R, f, 8)))
        st(C_R, B + c, form.last_column(four_rows(WX, f, 8)))
        st(C_D, B + c, form.total(ld(WY, f + 3, 8, 4)))
        st(C_A, B + c, form.total(four_rows(AN, f, 8)))
    for c in range(B, B + coarse, 8):
        c_r = ld(C_R, c)
        c_l = form.coarse_left(c_r)
        total = ld(C_A, c) + c_l + c_r + ld(C_D, c - 1) + ld(C_D, c)
        st(C_L, c, c_l)
        st(C_I, c, jnp.where(total > zero, F32(DAMP) / total, zero))

    def smooth(lo, hi):
        for c in range(lo, hi, 8):
            st(EA, B + c, ld(C_I, B + c) * ld(GC, B + c))
        if lo > 0:
            st(EA, B + lo - 8, coarse_zeros)
            st(EB, B + lo - 8, coarse_zeros)
        if hi < coarse:
            st(EA, B + hi, coarse_zeros)
            st(EB, B + hi, coarse_zeros)
        old, new = EA, EB
        for turn in range(3):
            for c in range(B + lo, B + hi, 8):
                e = ld(old, c)
                beside = ld(C_L, c) * form.coarse_left(e) + ld(C_R, c) * form.coarse_right(e)
                beside = beside + (ld(C_D, c - 1) * ld(old, c - 1) + ld(C_D, c) * ld(old, c + 1))
                st(new, c, F32(1.0 - DAMP) * e + ld(C_I, c) * (ld(GC, c) + beside))
            old, new = new, old
        first, last = max(lo, 6), min(hi, coarse - 6)
        count = last - first
        for k in range(4):
            st(SP, B + 4 * (first - 6) + k, form.spread(ld(EB, B + first, count)), 4)

    def restrict(q):
        for c in range(8, coarse - 8, 8):
            st(GC, B + c, form.total(four_rows(q, B + 4 * c - 24, 8)))

    smooth(0, coarse)
    for r in range(B, B + fine, 8):
        st(PA, r, ld(DI, r) * ld(R, r) + ld(SP, r))
    flows(form, PA, WX, FL, range(B, B + fine, 8))
    for r in range(B, B + fine, 8):
        st(QA, r, apply_a(PA, form.left, FL, WY, AN, r))
    restrict(QA)
    s_up, _ = sides(0, 1)
    _, s_down = sides(HR - 1, HR)
    for c, s, off in ((0, s_up, 4), (coarse - 8, s_down, 0)):
        c = B + c
        e = ld(EB, c)
        part = jnp.zeros_like(e)
        for k in range(4):
            part = jnp.where(rows(e.shape) == off + k, jnp.broadcast_to(form.unpack(s, k), e.shape), part)
        image = ld(C_A, c) * e + ld(C_L, c) * (e - form.coarse_left(e)) + ld(C_R, c) * (e - form.coarse_right(e))
        image = image + ld(C_D, c - 1) * (e - ld(EB, c - 1))
        image = image + ld(C_D, c) * (e - ld(EB, c + 1))
        st(GC, c, part + image)
    for r in range(0, n, 8):
        f = B + FG + r
        for out, ref in ((p0, PA), (q0, QA), (r0, R)):
            out[:, r : r + 8, :] = ref[:own_blocks, f : f + 8, :]
    smooth(0, coarse)
    for r in range(B, B + fine, 8):
        st(PB, r, (ld(DI, r) * ld(QA, r) + ld(SP, r)) - F32(SHIFT) * ld(PA, r))
    flows(form, PB, WX, FL, range(B + 8, B + fine - 8, 8))
    for r in range(B + 8, B + fine - 8, 8):
        st(QA, r, apply_a(PB, form.left, FL, WY, AN, r))
    restrict(QA)
    for r in range(0, n, 8):
        f = B + FG + r
        for out, ref in ((p1, PB), (q1, QA)):
            out[:, r : r + 8, :] = ref[:own_blocks, f : f + 8, :]
    smooth(8, coarse - 8)
    for r in range(B + FG - 8, B + FG + n + 8, 8):
        st(PA, r, (ld(DI, r) * ld(QA, r) + ld(SP, r)) - F32(SHIFT) * ld(PB, r))
    flows(form, PA, WX, FL, range(B + FG, B + FG + n, 8))
    acc = [jnp.zeros((8, 128), F32) for _ in range(9)]
    for r in range(0, n, 8):
        f = B + FG + r
        image = apply_a(PA, form.left, FL, WY, AN, f)
        sums = [[] for _ in acc]
        for j in range(own_blocks):
            z2, i2 = PA[j, f : f + 8, :], image[:, j * 128 : (j + 1) * 128]
            p2[j, r : r + 8, :] = z2
            q2[j, r : r + 8, :] = i2
            z0, z1, i0, i1, res = [x[j, r : r + 8, :] for x in (p0, p1, q0, q1, r0)]
            pairs = ((z0, i0), (z1, i0), (z1, i1), (z2, i0), (z2, i1), (z2, i2), (z0, res), (z1, res), (z2, res))
            for k, (x, y) in enumerate(pairs):
                sums[k].append(x * y)
        for k, parts in enumerate(sums):
            acc[k] = acc[k] + tree(parts)
    lane = lanes((8, 128))
    line = jnp.zeros((8, 128), F32)
    for k in range(9):
        total = jnp.sum(jnp.sum(acc[k], axis=0, keepdims=True), axis=1, keepdims=True)
        line = jnp.where(lane == k, jnp.broadcast_to(total, (8, 128)), line)
    for j in range(mom.shape[0]):
        mom[j] = line[0:1]


def combine(mom, p0, p1, p2, q0, q1, q2, r0, heights, residual, work):
    blocks, n, _ = p0.shape
    form = layout(blocks + 1)
    tot = jnp.broadcast_to(tree([mom[j] for j in range(mom.shape[0])]), (8, 128))
    m = [jnp.broadcast_to(tot[:, k : k + 1], (8, 128)) for k in range(9)]
    g00, g10, g11, g20, g21, g22, b0, b1, b2 = m
    l10, l20 = g10 / g00, g20 / g00
    d1 = g11 - l10 * g10
    t21 = g21 - l20 * g10
    l21 = t21 / d1
    d2 = g22 - l20 * g20 - l21 * t21
    y1 = b1 - l10 * b0
    y2 = b2 - l20 * b0 - l21 * y1
    x2 = y2 / d2
    x1 = y1 / d1 - l21 * x2
    x0 = b0 / g00 - l10 * x1 - l20 * x2
    sums, spare, done = [[work.at[k], work.at[k + 1]] for k in (0, 2, 4)]
    for r in range(0, n, 8):
        for j in range(blocks):
            z0, z1, z2, i0, i1, i2, res = [x[j, r : r + 8, :] for x in (p0, p1, p2, q0, q1, q2, r0)]
            sums[0][j, r : r + 8, :] = x0 * z0 + x1 * z1 + x2 * z2
            sums[1][j, r : r + 8, :] = res - (x0 * i0 + x1 * i1 + x2 * i2)
    reorder(form.steps_out, sums, done, spare)
    for r in range(0, n, 8):
        heights[r : r + 8, :] = ld(done[0], r)
        residual[r : r + 8, :] = ld(done[1], r)


def swap(x, axis, size, inner):
    if inner:
        pairs = [(i, i ^ 1) for i in range(size) if i ^ 1 < size]
    else:
        pairs = [(i, j) for i in range(size) for j in [((i + 1) ^ 1) - 1] if 0 <= j < size]
    return lax.ppermute(x, axis, pairs)


def local(nrow, ncol, gx, gy, wx, wy, an, pr):
    n, width = gx.shape
    ext = width + 2 * HC
    fields = tuple(pltpu.with_memory_space_constraint(f, pltpu.HBM) for f in (gx, gy, wx, wy, an, pr))
    nb = ext // 128
    shape = lambda *dims: jax.ShapeDtypeStruct(dims, F32)
    params = pltpu.CompilerParams(vmem_limit_bytes=48 * 1024 * 1024)

    def call(kernel, name, args, outs, scratch=(), us=1, fetches=0):
        sems = [pltpu.SemaphoreType.DMA((fetches,))] if fetches else []
        return pl.pallas_call(
            kernel,
            in_specs=[HBM if fetches else VMEM] * len(args),
            out_specs=[VMEM] * len(outs),
            out_shape=outs,
            scratch_shapes=[pltpu.VMEM(dims, F32) for dims in scratch] + sems,
            compiler_params=params,
            cost_estimate=pl.CostEstimate(flops=us * 2_000_000, bytes_accessed=us * 2_000_000, transcendentals=0),
            name=name,
        )(*args)

    halos = []
    for inner in (True, False) if ncol > 2 else (True,):
        (edge,) = call(functools.partial(edge_columns, inner), "edge_columns", fields, [shape(n + 8, 256)], [(n, 128)] * 6, 1, 6)
        halos.append(swap(edge, "col", ncol, inner))
    tile = shape(nb - 1, n, 128)
    own = call(tile_fields, "tile_fields", fields, [tile] * 4 + [shape(n, 128), shape(nb - 1, 8, 128)], [(n, width)] * 6 + [(4, nb - 1, n, 128)] * 2 + [(2, nb - 1, 8, 128)], 1, 6)
    depth = 4 * HR + 8
    cb = layout(nb).coarse_blocks
    far = shape(cb, 8, 128)
    msg = shape(nb, depth, 128)
    field = shape(nb, n, 128)
    work = [(nb, 48, 128), (nb, 16, 128), (nb, 16, 128)]
    *fields, to_out, g_a, cr_a, cd_a, ca_a = call(
        functools.partial(edge_rows, len(halos) > 1),
        "edge_rows",
        (*own, *halos),
        [field] * 4 + [shape(nb, 8, 128), msg] + [far] * 4,
        work,
    )
    from_out = swap(to_out, "row", nrow, False)
    di, to_in, *far_b = call(near_rows, "near_rows", fields, [field, msg] + [far] * 4, work)
    from_in = swap(to_in, "row", nrow, True)
    fine = n + 2 * FG
    coarse = fine // 4 + 12
    mom, *vectors = call(
        basis,
        "basis",
        (*fields, g_a, cr_a, cd_a, ca_a, di, *far_b, from_in, from_out),
        [shape(nrow * ncol, 1, 128)] + [tile] * 7,
        [(nb, fine + 2 * GUARD, 128)] * 10 + [(cb, coarse + 2 * GUARD, 128)] * 8,
    )
    mom = lax.all_to_all(mom, ("row", "col"), 0, 0, tiled=True)
    out = shape(n, width)
    return tuple(call(combine, "combine", (mom, *vectors), [out, out], [(6, nb - 1, n, 128)]))


def solution(mesh):
    spec = P("row", "col")
    return jax.shard_map(
        functools.partial(local, mesh.shape["row"], mesh.shape["col"]),
        mesh=mesh,
        in_specs=(spec,) * 6,
        out_specs=(spec, spec),
        check_vma=False,
    )
```

```python
import functools

import jax
import jax.numpy as jnp
from jax import lax
from jax.experimental import pallas as pl
from jax.experimental.pallas import tpu as pltpu
from jax.sharding import PartitionSpec as P

DAMP = 2.0 / 3.0
SHIFT = 1.0
HC = 64
HR = 8
FAR = 12
DEPTH = 4 * HR + FAR - 1 + 5
GUARD = 8
VMEM = pl.BlockSpec(memory_space=pltpu.VMEM)
HBM = pl.BlockSpec(memory_space=pltpu.HBM)
F32 = jnp.float32


def lanes(shape):
    return lax.broadcasted_iota(jnp.int32, shape, 1)


def rows(shape):
    return lax.broadcasted_iota(jnp.int32, shape, 0)


def roll_right(x, k=1):
    return pltpu.roll(x, k, 1)


def roll_left(x, k=1):
    return pltpu.roll(x, x.shape[1] - k, 1)


def group_sum(x):
    lane = lanes(x.shape)
    x = x + jnp.where(lane % 2 == 0, roll_left(x), roll_right(x))
    return x + jnp.where(lane % 4 < 2, roll_left(x, 2), roll_right(x, 2))


def split(x):
    return [x[:, j : j + 128] for j in range(0, x.shape[1], 128)]


def join(parts):
    return jnp.concatenate(parts, axis=1)


class Wide:
    def __init__(self, width):
        self.coarse_blocks = width // 128 + 1

    left, right = staticmethod(roll_right), staticmethod(roll_left)
    total = staticmethod(group_sum)
    spread = take = staticmethod(lambda x: x)
    steps_in = steps_out = ()

    def coarse_left(self, e):
        return roll_right(e, 4)

    def coarse_right(self, e):
        return roll_left(e, 4)

    def last_column(self, x):
        return group_sum(jnp.where(lanes(x.shape) % 4 == 3, x, F32(0.0)))

    def pack(self, a, b, c, d):
        four = lanes(a.shape) % 4
        return jnp.where(four < 2, jnp.where(four == 0, a, b), jnp.where(four == 2, c, d))

    def unpack(self, m, k):
        return group_sum(jnp.where(lanes(m.shape) % 4 == k, m, F32(0.0)))

    def unpack_rows(self, m):
        return group_sum(jnp.where(lanes(m.shape) % 4 == rows(m.shape) % 4, m, F32(0.0)))

    def first_only(self, x):
        return jnp.where(lanes(x.shape) % 4 == 0, x, F32(0.0))

    def last_only(self, x):
        return jnp.where(lanes(x.shape) % 4 == 3, x, F32(0.0))


class Planes:
    coarse_blocks = 2

    def left(self, x):
        a, b, c, d, h = split(x)
        first = lanes(h.shape) == 0
        d, h = roll_right(d), roll_right(h)
        return join([jnp.where(first, h, d), a, b, c, jnp.where(first, d, h)])

    def right(self, x):
        a, b, c, d, h = split(x)
        last = lanes(h.shape) == 127
        a, h = roll_left(a), roll_left(h)
        return join([b, c, d, jnp.where(last, h, a), jnp.where(last, a, h)])

    def coarse_left(self, e):
        o, h = split(e)
        lane = lanes(h.shape)
        end = jnp.broadcast_to(o[:, 127:128], h.shape)
        return join([jnp.where(lane == 0, roll_right(h), roll_right(o)), jnp.where(lane < 4, end, roll_right(h, 4))])

    def coarse_right(self, e):
        o, h = split(e)
        lane = lanes(h.shape)
        end = jnp.broadcast_to(o[:, 0:1], h.shape)
        return join([jnp.where(lane == 127, roll_left(h), roll_left(o)), jnp.where(lane >= 124, end, roll_left(h, 4))])

    def total(self, x):
        a, b, c, d, h = split(x)
        return join([(a + b) + (c + d), group_sum(h)])

    def last_column(self, x):
        h = x[:, 512:640]
        return join([x[:, 384:512], group_sum(jnp.where(lanes(h.shape) % 4 == 3, h, F32(0.0)))])

    def spread(self, e):
        o, h = split(e)
        return join([o, o, o, o, h])

    def take(self, x):
        return join([x[:, 0:128], x[:, 512:640]])

    def pack(self, *fields):
        own, halo = zip(*[split(f) for f in fields])
        a, b, c, d = halo
        four = lanes(a.shape) % 4
        mixed = jnp.where(four < 2, jnp.where(four == 0, a, b), jnp.where(four == 2, c, d))
        return join([*own, mixed])

    def unpack(self, m, k):
        h = m[:, 512:640]
        return join([m[:, k * 128 : k * 128 + 128], group_sum(jnp.where(lanes(h.shape) % 4 == k, h, F32(0.0)))])

    def unpack_rows(self, m):
        a, b, c, d, h = split(m)
        key = rows(h.shape) % 4
        own = jnp.where(key < 2, jnp.where(key == 0, a, b), jnp.where(key == 2, c, d))
        return join([own, group_sum(jnp.where(lanes(h.shape) % 4 == key, h, F32(0.0)))])

    def first_only(self, x):
        a, _, _, _, h = split(x)
        none = jnp.zeros_like(h)
        return join([a, none, none, none, jnp.where(lanes(h.shape) % 4 == 0, h, none)])

    def last_only(self, x):
        _, _, _, d, h = split(x)
        none = jnp.zeros_like(h)
        return join([none, none, none, d, jnp.where(lanes(h.shape) % 4 == 3, h, none)])

    def gather_in(self, parts):
        lane = lanes(parts[0].shape)
        index = (lane % 32) * 4 + lane // 32
        return [jnp.take_along_axis(p, index, axis=1) for p in parts]

    def gather_out(self, parts):
        lane = lanes(parts[0].shape)
        index = (lane % 4) * 32 + lane // 4
        return [jnp.take_along_axis(p, index, axis=1) for p in parts]

    def swap_halves(self, parts):
        a, b, c, d = parts
        low = lanes(a.shape) < 64
        return [
            jnp.where(low, a, roll_right(c, 64)),
            jnp.where(low, b, roll_right(d, 64)),
            jnp.where(low, roll_right(a, 64), c),
            jnp.where(low, roll_right(b, 64), d),
        ]

    def swap_quarters(self, parts):
        a, b, c, d = parts
        low = lanes(a.shape) % 64 < 32
        return [
            jnp.where(low, a, roll_right(b, 32)),
            jnp.where(low, roll_left(a, 32), b),
            jnp.where(low, c, roll_right(d, 32)),
            jnp.where(low, roll_left(c, 32), d),
        ]

    @property
    def steps_in(self):
        return self.gather_in, self.swap_halves, self.swap_quarters

    @property
    def steps_out(self):
        return self.swap_halves, self.swap_quarters, self.gather_out


def layout(blocks):
    return Planes() if blocks == 5 else Wide(128 * (blocks - 1))


def ld(ref, start, count=8, step=1):
    rows_of = pl.ds(start, count, stride=step) if step > 1 else pl.ds(start, count)
    return jnp.concatenate([ref[j, rows_of, :] for j in range(ref.shape[0])], axis=1)


def st(ref, start, value, step=1):
    count = value.shape[0]
    rows_of = pl.ds(start, count, stride=step) if step > 1 else pl.ds(start, count)
    for j in range(ref.shape[0]):
        ref[j, rows_of, :] = value[:, j * 128 : (j + 1) * 128]


def tree(parts):
    while len(parts) > 1:
        parts = [sum(parts[j + 1 : j + 2], parts[j]) for j in range(0, len(parts), 2)]
    return parts[0]


def four_rows(ref, start, count):
    parts = [ld(ref, start + k, count, 4) for k in range(4)]
    return (parts[0] + parts[1]) + (parts[2] + parts[3])


def position():
    row, col = lax.axis_index("row"), lax.axis_index("col")
    end_row = row == lax.axis_size("row") - 1
    end_col = col == lax.axis_size("col") - 1
    return lax.rem(row, 2) == 1, lax.rem(col, 2) == 1, end_row, end_col


def reorder(steps, sources, targets, spare):
    pairs = list(zip(sources, spare))
    for k, step in enumerate(steps):
        for (x, y), target in zip(pairs, targets):
            x, y = (y, x) if k % 2 else (x, y)
            y = target if k == len(steps) - 1 else y
            for r in range(0, x.shape[1], 8):
                for j, block in enumerate(step([x[j, r : r + 8, :] for j in range(x.shape[0])])):
                    y[j, r : r + 8, :] = block
    if not steps:
        for x, target in zip(sources, targets):
            target[...] = x[...]


def fetch(sources, targets, sems):
    copies = [pltpu.make_async_copy(x, y, sems.at[k]) for k, (x, y) in enumerate(zip(sources, targets))]
    for copy in copies:
        copy.start()
    for copy in copies:
        copy.wait()


def edge_columns(inner, *refs):
    fields, (out, *held, sems) = refs[:6], refs[6:]
    n, width = fields[0].shape
    _, col_odd, end_row, _ = position()
    last = jnp.logical_not(col_odd) if inner else col_odd
    offset = pl.multiple_of(jnp.where(last, width - 128, 0), 128)
    row, lane = rows((8, 128)), lanes((8, 128))
    zero = F32(0.0)
    fetch([f.at[:, pl.ds(offset, 128)] for f in fields], held, sems)

    def pair(x, y):
        low = jnp.where(lane < HC, x, roll_right(y, HC))
        high = jnp.where(lane < HC, roll_right(x, HC), y)
        return jnp.where(last, high, low)

    carry = jnp.zeros((1, 128), F32)
    for r in range(0, n, 8):
        g_x, g_y, w_x, w_y, a, p = [f[r : r + 8, :] for f in held]
        if r == n - 8:
            w_y = jnp.where((row == 7) & end_row, zero, w_y)
        fx = w_x * g_x
        fy = w_y * g_y
        before_x = jnp.where(lane == 0, zero, roll_right(fx))
        before_y = jnp.where(row == 0, jnp.broadcast_to(carry, fy.shape), pltpu.roll(fy, 1, 0))
        carry = fy[7:8, :]
        src = a * p + before_x - fx + before_y - fy
        edge = jnp.broadcast_to(fx[:, 127:128], fx.shape)
        out[r : r + 8, 0:128] = jnp.where((lane == 0) & last, edge, pair(src, w_x))
        out[r : r + 8, 128:256] = pair(w_y, a)
    tail = jnp.broadcast_to(carry, (8, 128))
    tail = pair(tail, tail)
    out[n : n + 8, 0:128] = tail
    out[n : n + 8, 128:256] = tail


def tile_fields(*refs):
    fields, (r_o, wx_o, wy_o, an_o, fx_o, fy_o, *held, raw, spare, tail, sems) = refs[:6], refs[6:]
    gx, gy, wx, wy, an, pr = held
    n, width = gx.shape
    form = layout(width // 128 + 1)
    fetch(fields, held, sems)
    _, _, end_row, end_col = position()
    row, lane = rows((8, width)), lanes((8, width))
    zero = F32(0.0)
    carry = jnp.zeros((1, width), F32)
    for r in range(0, n, 8):
        w_x = jnp.where((lane == width - 1) & end_col, zero, wx[r : r + 8, :])
        w_y = wy[r : r + 8, :]
        if r == n - 8:
            w_y = jnp.where((row == 7) & end_row, zero, w_y)
        fx = w_x * gx[r : r + 8, :]
        fy = w_y * gy[r : r + 8, :]
        a = an[r : r + 8, :]
        before_x = jnp.where(lane == 0, zero, roll_right(fx))
        before_y = jnp.where(row == 0, jnp.broadcast_to(carry, fy.shape), pltpu.roll(fy, 1, 0))
        carry = fy[7:8, :]
        src = a * pr[r : r + 8, :] + before_x - fx + before_y - fy
        for k, x in enumerate((src, w_x, w_y, a)):
            st(raw.at[k], r, x)
        fx_o[r : r + 8, :] = jnp.broadcast_to(fx[:, width - 1 : width], (8, 128))
    st(tail.at[0], 0, jnp.broadcast_to(carry, (8, width)))
    pick = lambda ref: [ref.at[k] for k in range(4)]
    reorder(form.steps_in, [*pick(raw), tail.at[0]], [r_o, wx_o, wy_o, an_o, fy_o], [*pick(spare), tail.at[1]])


def edge_rows(has_outer, r_t, wx_t, wy_t, an_t, fx_t, fy_t, *refs):
    inner, refs = refs[0], refs[1:]
    outer = None
    if has_outer:
        outer, refs = refs[0], refs[1:]
    r_o, wx_o, wy_o, an_o, fy_o, *rest = refs
    own, n, _ = r_t.shape
    form = layout(own + 1)
    row_odd, odd, _, _ = position()
    lane = lanes((8, 128))
    zero = F32(0.0)

    def halo(r, c):
        x = inner[r : r + 8, c : c + 128]
        y = outer[r : r + 8, c : c + 128] if has_outer else jnp.zeros_like(x)
        before, after = jnp.where(odd, x, y), jnp.where(odd, y, x)
        first = jnp.where(lane < HC, after, roll_right(before, HC))
        second = jnp.where(lane < HC, roll_right(after, HC), before)
        return first, second

    for r in range(0, n, 8):
        src_h, wx_h = halo(r, 0)
        wy_h, an_h = halo(r, 128)
        incoming = jnp.broadcast_to(src_h[:, HC : HC + 1], (8, 128))
        src_h = jnp.where(lane == 0, src_h + fx_t[r : r + 8, :], jnp.where(lane == HC, zero, src_h))
        for out, tile, h in ((r_o, r_t, src_h), (wx_o, wx_t, wx_h), (wy_o, wy_t, wy_h), (an_o, an_t, an_h)):
            top = GUARD if out is wy_o else 0
            for j in range(own):
                x = tile[j, r : r + 8, :]
                if out is r_o and j == 0:
                    x = jnp.where(lane == 0, x + incoming, x)
                out[j, top + r : top + r + 8, :] = x
            out[own, top + r : top + r + 8, :] = h
    st(wy_o, 0, jnp.zeros((GUARD, (own + 1) * 128), F32))
    for j in range(own):
        fy_o[j] = fy_t[j]
    fy_o[own] = halo(n, 0)[0]

    message(form, row_odd, r_o, wx_o, wy_o, an_o, fy_o, *rest)


def near_rows(r_i, wx_i, wy_i, an_i, fy_i, di, *rest):
    form = layout(wx_i.shape[0])
    row_odd, _, _, _ = position()
    message(form, jnp.logical_not(row_odd), r_i, wx_i, wy_i, an_i, fy_i, *rest)
    for r in range(8, wx_i.shape[1], 8):
        w_x, w_y = ld(wx_i, r), ld(wy_i, GUARD + r)
        diag = ld(an_i, r) + w_x + form.left(w_x) + w_y + ld(wy_i, GUARD + r - 1)
        st(di, r, jnp.where(diag > F32(0.0), F32(1.0) / diag, F32(0.0)))


def message(form, bottom, r_o, wx_o, wy_o, an_o, fy_o, msg, g_o, cr_o, cd_o, ca_o, U, DI, V, FL, T, H, K):
    n = r_o.shape[1]
    zero = F32(0.0)
    G = GUARD

    def pick(low, high):
        return jnp.where(bottom, high, low)

    def align(x):
        return pl.multiple_of(x, 8)

    base = align(pick(0, n - 40))
    for r in range(0, 40, 8):
        at = align(base + r)
        w_x = ld(wx_o, at)
        diag = ld(an_o, at) + w_x + form.left(w_x) + ld(wy_o, align(at + G)) + ld(wy_o, base + (r + G - 1))
        inverse = jnp.where(diag > zero, F32(1.0) / diag, zero)
        st(DI, G + r, inverse)
        st(U, G + r, ld(r_o, at) * inverse)
    for source, image in ((U, T), (V, U)):
        for r in range(0, 40, 8):
            x = ld(source, G + r)
            st(FL, G + r, ld(wx_o, align(base + r)) * (x - form.right(x)))
        for r in range(0, 40, 8):
            at = align(base + r)
            x, flow = ld(source, G + r), ld(FL, G + r)
            down = ld(wy_o, align(at + G)) * (x - ld(source, G + r + 1))
            up = ld(wy_o, base + (r + G - 1)) * (x - ld(source, G + r - 1))
            y = (ld(an_o, at) * x + (flow - form.left(flow))) + (down + up)
            st(image, G + r, y)
            if image is T:
                st(V, G + r, ld(DI, G + r) * y)
    near = align(pick(0, 8))
    sums = form.total(four_rows(T, align(near + G), 8))
    sums_2 = form.total(four_rows(U, pick(0, 20) + G, 4))
    parts = {}

    def add(name, x):
        parts[name] = parts[name] + x if name in parts else x

    for k in range(4):
        at = base + (near + k)
        w_x = ld(wx_o, at, 8, 4)
        first, last = form.first_only(form.left(w_x)), form.last_only(w_x)
        a = ld(an_o, at, 8, 4) + first + last
        inverse = ld(DI, near + (G + k), 8, 4)
        sides = []
        if k == 0:
            w = ld(wy_o, at + (G - 1), 8, 4)
            sides.append(("u", w))
            a = a + w
        if k == 3:
            w = ld(wy_o, at + G, 8, 4)
            sides.append(("d", w))
            a = a + w
        weighted = inverse * a
        add("aa", weighted * a)
        for name, w in (("l", first), ("r", last)):
            add("a" + name, weighted * w)
            scaled = inverse * w
            add(name + name, scaled * w)
            for other, v in sides:
                add(name + other, scaled * v)
        for name, w in sides:
            add("a" + name, weighted * w)
            add(name + name, inverse * w * w)
    parts = {name: form.total(x) for name, x in parts.items()}
    for k, name in enumerate(("uu", "dd", "au", "ru", "lu")):
        st(H.at[k], G, parts[name])
    uu, au, ru, lu = [ld(H.at[k], G + 1) for k in (0, 2, 3, 4)]
    dd = ld(H.at[1], G - 1)
    centre = parts["aa"] + form.coarse_right(parts["ll"]) + form.coarse_left(parts["rr"]) + uu + dd
    east = -(parts["ar"] + form.coarse_right(parts["al"]))
    south = -(parts["ad"] + au)
    south_east = form.coarse_right(parts["ld"]) + ru
    south_west = form.coarse_left(parts["rd"]) + lu
    for k, x in enumerate((centre, east, south, south_east, south_west)):
        st(K.at[k], 0, x)

    c = align(pick(0, n - 4 * FAR))
    coarse = (
        form.total(four_rows(r_o, c, FAR)),
        form.last_column(four_rows(wx_o, c, FAR)),
        form.total(ld(wy_o, c + (G + 3), FAR, 4)),
        form.total(four_rows(an_o, c, FAR)),
    )
    for out, x in zip((g_o, cr_o, cd_o, ca_o), coarse):
        st(out, 0, x)
    start = align(pick(0, n - HR))
    for k, (ref, top) in enumerate(((r_o, 0), (wx_o, 0), (wy_o, G), (an_o, 0))):
        st(msg, k * HR, ld(ref, align(start + top), HR))
    outer, inner = pick(HR - 1, 0), pick(HR - 2, 1)
    st(msg, outer, form.pack(*[sums[k : k + 1] for k in range(4)]))
    st(msg, inner, form.pack(*[sums[k : k + 1] for k in range(4, 8)]))
    st(msg, HR + outer, form.spread(form.total(ld(wy_o, n - 4 * FAR - 1 + G, 1))))
    st(msg, HR + inner, form.pack(*[sums_2[k : k + 1] for k in range(4)]))
    st(msg, 3 * HR + outer, ld(fy_o, 0, 1))
    packed = form.pack(*coarse)
    st(msg, 4 * HR, jnp.where(bottom, packed[: FAR - 1], packed[1:]))
    for k in range(5):
        four = [ld(K.at[k], pick(0, 3) + i, 1) for i in range(4)]
        st(msg, 4 * HR + FAR - 1 + k, form.pack(*four))


def flows(form, v, w_x, flow, starts):
    for r in starts:
        x = ld(v, r)
        st(flow, r, ld(w_x, r) * (x - form.right(x)))


def apply_a(v, flow_left, flow, w_y, an, r):
    x = ld(v, r)
    down = ld(w_y, r) * (x - ld(v, r + 1))
    up = ld(w_y, r - 1) * (x - ld(v, r - 1))
    return (ld(an, r) * x + (ld(flow, r) - flow_left(ld(flow, r)))) + (down + up)


def basis(r_i, wx_i, wy_i, an_i, fy_i, g_a, cr_a, cd_a, ca_a, di_i, g_b, cr_b, cd_b, ca_b, msg_in, msg_out, mom, p0, p1, p2, q0, q1, q2, r0,
         R, WX, WY, AN, DI, SP, PA, PB, QA, FL, C_L, C_R, C_D, C_A, C_I, EA, EB, GC, KF, KV):
    blocks, n, _ = r_i.shape
    form = layout(blocks)
    fine = n + 2 * HR
    coarse = n // 4 + 2 * FAR
    zero = F32(0.0)
    odd, _, _, _ = position()
    own_blocks = blocks - 1
    B = GUARD

    def sides(a, b):
        x, y = ld(msg_in, a, b - a), ld(msg_out, a, b - a)
        return jnp.where(odd, x, y), jnp.where(odd, y, x)

    zeros = jnp.zeros((B, blocks * 128), F32)
    coarse_zeros = jnp.zeros((B, form.coarse_blocks * 128), F32)
    for ref in (R, WX, WY, AN, PA, PB):
        st(ref, 0, zeros)
        st(ref, B + fine, zeros)
    for k, (ref, own, top) in enumerate(((R, r_i, 0), (WX, wx_i, 0), (WY, wy_i, GUARD), (AN, an_i, 0))):
        up, down = sides(k * HR, (k + 1) * HR)
        st(ref, B, up)
        st(ref, B + HR + n, down)
        for r in range(0, n, 8):
            st(ref, B + HR + r, ld(own, top + r))
    flux_up, _ = sides(3 * HR, 3 * HR + 1)
    st(R, B + HR, ld(R, B + HR, 1) + flux_up)
    st(R, B + HR + n, ld(R, B + HR + n, 1) + ld(fy_i, 0, 1))

    for r in range(8, n, 8):
        st(DI, B + HR + r, ld(di_i, r))
    for r in [*range(B, B + HR + 8, 8), *range(B + HR + n, B + fine, 8)]:
        w_x, w_y = ld(WX, r), ld(WY, r)
        diag = ld(AN, r) + w_x + form.left(w_x) + w_y + ld(WY, r - 1)
        st(DI, r, jnp.where(diag > zero, F32(1.0) / diag, zero))

    for ref in (EA, EB, C_D):
        st(ref, 0, coarse_zeros)
        st(ref, B + coarse, coarse_zeros)
    up, down = sides(4 * HR, 4 * HR + FAR - 1)
    for k, (ref, a, b) in enumerate(((GC, g_a, g_b), (C_R, cr_a, cr_b), (C_D, cd_a, cd_b), (C_A, ca_a, ca_b))):
        st(ref, B, form.unpack(up, k))
        st(ref, B + coarse - FAR + 1, form.unpack(down, k))
        x, y = ld(a, 0, FAR), ld(b, 0, FAR)
        st(ref, B + FAR, jnp.where(odd, y, x))
        st(ref, B + 2 * FAR, jnp.where(odd, x, y))
    st(GC, B + FAR, ld(GC, B + FAR, 1) + form.total(flux_up))
    beyond, _ = sides(HR, HR + 1)
    st(C_D, B - 1, form.take(beyond))
    for c in (FAR - 1, coarse - FAR):
        f = B + 4 * c - 40
        st(GC, B + c, form.total(four_rows(R, f, 1)))
        st(C_R, B + c, form.last_column(four_rows(WX, f, 1)))
        st(C_D, B + c, form.total(ld(WY, f + 3, 1)))
        st(C_A, B + c, form.total(four_rows(AN, f, 1)))
    for c in range(B, B + coarse, 8):
        c_r = ld(C_R, c)
        c_l = form.coarse_left(c_r)
        total = ld(C_A, c) + c_l + c_r + ld(C_D, c - 1) + ld(C_D, c)
        st(C_L, c, c_l)
        st(C_I, c, jnp.where(total > zero, F32(DAMP) / total, zero))

    def smooth(lo, hi):
        for c in range(lo, hi, 8):
            st(EA, B + c, ld(C_I, B + c) * ld(GC, B + c))
        if lo > 0:
            st(EA, B + lo - 8, coarse_zeros)
            st(EB, B + lo - 8, coarse_zeros)
        if hi < coarse:
            st(EA, B + hi, coarse_zeros)
            st(EB, B + hi, coarse_zeros)
        old, new = EA, EB
        for turn in range(3):
            for c in range(B + lo, B + hi, 8):
                e = ld(old, c)
                beside = ld(C_L, c) * form.coarse_left(e) + ld(C_R, c) * form.coarse_right(e)
                beside = beside + (ld(C_D, c - 1) * ld(old, c - 1) + ld(C_D, c) * ld(old, c + 1))
                st(new, c, F32(1.0 - DAMP) * e + ld(C_I, c) * (ld(GC, c) + beside))
            old, new = new, old
        for k in range(4):
            st(SP, B + k, form.spread(ld(EB, B + 10, fine // 4)), 4)

    def restrict(q):
        for c in range(FAR - 1, coarse - FAR + 1, 8):
            count = min(8, coarse - FAR + 1 - c)
            st(GC, B + c, form.total(four_rows(q, B + 4 * c - 40, count)))

    def coarse_image(c, count):
        e = ld(EB, B + c, count)
        c_l, c_r = ld(C_L, B + c, count), ld(C_R, B + c, count)
        image = ld(C_A, B + c, count) * e + c_l * (e - form.coarse_left(e)) + c_r * (e - form.coarse_right(e))
        image = image + ld(C_D, B + c - 1, count) * (e - ld(EB, B + c - 1, count))
        return image + ld(C_D, B + c, count) * (e - ld(EB, B + c + 1, count))

    def stretch(a, b):
        shape = (8, a.shape[1])
        return form.unpack_rows(jnp.where(rows(shape) < 4, jnp.broadcast_to(a, shape), jnp.broadcast_to(b, shape)))

    def second_sums(side, c, sums):
        for k in range(5):
            at = 4 * HR + FAR - 1 + k
            row = sides(at, at + 1)[side]
            st(KF.at[k], 8, form.unpack_rows(jnp.broadcast_to(row, (4, row.shape[1]))))
        centre, east, south, south_east, south_west = [ld(KF.at[k], 8, 4) for k in range(5)]
        north, north_west, north_east = [ld(KF.at[k], 7, 4) for k in (2, 3, 4)]
        e, below, above = [ld(EB, B + c + d, 4) for d in (0, 1, -1)]
        image = centre * e + east * form.coarse_right(e) + form.coarse_left(east * e)
        image = image + south * below + north * above
        image = image + south_east * form.coarse_right(below) + form.coarse_left(north_west * above)
        image = image + south_west * form.coarse_left(below) + form.coarse_right(north_east * above)
        st(KV.at[side], 0, image + form.unpack_rows(jnp.broadcast_to(sums, (4, sums.shape[1]))))

    smooth(0, coarse)
    for r in range(B, B + fine, 8):
        st(PA, r, ld(DI, r) * ld(R, r) + ld(SP, r))
    flows(form, PA, WX, FL, range(B, B + fine, 8))
    for r in range(B, B + fine, 8):
        st(QA, r, apply_a(PA, form.left, FL, WY, AN, r))
    restrict(QA)
    far_up, _ = sides(0, 1)
    near_up, _ = sides(1, 2)
    _, near_down = sides(HR - 1, HR)
    _, far_down = sides(HR - 2, HR - 1)
    up = stretch(far_up, near_up)
    down = stretch(near_down, far_down)
    image = coarse_image(0, FAR - 1)
    st(GC, B, image[0:4])
    st(GC, B + 4, image[4:] + up[0 : FAR - 5])
    image = coarse_image(coarse - FAR + 1, FAR - 1)
    st(GC, B + coarse - FAR + 1, image[0:7] + down[1:])
    st(GC, B + coarse - 4, image[7:])
    second_sums(0, 7, sides(HR + 1, HR + 2)[0])
    second_sums(1, coarse - FAR, sides(2 * HR - 2, 2 * HR - 1)[1])
    for r in range(0, n, 8):
        f = B + HR + r
        for out, ref in ((p0, PA), (q0, QA), (r0, R)):
            out[:, r : r + 8, :] = ref[:own_blocks, f : f + 8, :]
    smooth(0, coarse)
    for r in range(B, B + fine, 8):
        st(PB, r, (ld(DI, r) * ld(QA, r) + ld(SP, r)) - F32(SHIFT) * ld(PA, r))
    flows(form, PB, WX, FL, range(B, B + fine, 8))
    for r in range(B, B + fine, 8):
        st(QA, r, apply_a(PB, form.left, FL, WY, AN, r))
    restrict(QA)
    for c, side, first in ((8, 0, 1), (coarse - FAR + 1, 1, 1)):
        image = coarse_image(c, 3) + ld(KV.at[side], first, 3)
        st(GC, B + c, image - F32(SHIFT) * ld(GC, B + c, 3))
    for r in range(0, n, 8):
        f = B + HR + r
        for out, ref in ((p1, PB), (q1, QA)):
            out[:, r : r + 8, :] = ref[:own_blocks, f : f + 8, :]
    smooth(8, coarse - 8)
    for r in range(B + HR - 8, B + HR + n + 8, 8):
        st(PA, r, (ld(DI, r) * ld(QA, r) + ld(SP, r)) - F32(SHIFT) * ld(PB, r))
    flows(form, PA, WX, FL, range(B + HR, B + HR + n, 8))
    acc = [jnp.zeros((8, 128), F32) for _ in range(9)]
    for r in range(0, n, 8):
        f = B + HR + r
        image = apply_a(PA, form.left, FL, WY, AN, f)
        sums = [[] for _ in acc]
        for j in range(own_blocks):
            z2, i2 = PA[j, f : f + 8, :], image[:, j * 128 : (j + 1) * 128]
            p2[j, r : r + 8, :] = z2
            q2[j, r : r + 8, :] = i2
            z0, z1, i0, i1, res = [x[j, r : r + 8, :] for x in (p0, p1, q0, q1, r0)]
            pairs = ((z0, i0), (z1, i0), (z1, i1), (z2, i0), (z2, i1), (z2, i2), (z0, res), (z1, res), (z2, res))
            for k, (x, y) in enumerate(pairs):
                sums[k].append(x * y)
        for k, parts in enumerate(sums):
            acc[k] = acc[k] + tree(parts)
    lane = lanes((8, 128))
    line = jnp.zeros((8, 128), F32)
    for k in range(9):
        total = jnp.sum(jnp.sum(acc[k], axis=0, keepdims=True), axis=1, keepdims=True)
        line = jnp.where(lane == k, jnp.broadcast_to(total, (8, 128)), line)
    for j in range(mom.shape[0]):
        mom[j] = line[0:1]


def combine(mom, p0, p1, p2, q0, q1, q2, r0, heights, residual, work):
    blocks, n, _ = p0.shape
    form = layout(blocks + 1)
    tot = jnp.broadcast_to(tree([mom[j] for j in range(mom.shape[0])]), (8, 128))
    m = [jnp.broadcast_to(tot[:, k : k + 1], (8, 128)) for k in range(9)]
    g00, g10, g11, g20, g21, g22, b0, b1, b2 = m
    l10, l20 = g10 / g00, g20 / g00
    d1 = g11 - l10 * g10
    t21 = g21 - l20 * g10
    l21 = t21 / d1
    d2 = g22 - l20 * g20 - l21 * t21
    y1 = b1 - l10 * b0
    y2 = b2 - l20 * b0 - l21 * y1
    x2 = y2 / d2
    x1 = y1 / d1 - l21 * x2
    x0 = b0 / g00 - l10 * x1 - l20 * x2
    sums, spare, done = [[work.at[k], work.at[k + 1]] for k in (0, 2, 4)]
    for r in range(0, n, 8):
        for j in range(blocks):
            z0, z1, z2, i0, i1, i2, res = [x[j, r : r + 8, :] for x in (p0, p1, p2, q0, q1, q2, r0)]
            sums[0][j, r : r + 8, :] = x0 * z0 + x1 * z1 + x2 * z2
            sums[1][j, r : r + 8, :] = res - (x0 * i0 + x1 * i1 + x2 * i2)
    reorder(form.steps_out, sums, done, spare)
    for r in range(0, n, 8):
        heights[r : r + 8, :] = ld(done[0], r)
        residual[r : r + 8, :] = ld(done[1], r)


def swap(x, axis, size, inner):
    if inner:
        pairs = [(i, i ^ 1) for i in range(size) if i ^ 1 < size]
    else:
        pairs = [(i, j) for i in range(size) for j in [((i + 1) ^ 1) - 1] if 0 <= j < size]
    return lax.ppermute(x, axis, pairs)


def local(nrow, ncol, gx, gy, wx, wy, an, pr):
    n, width = gx.shape
    ext = width + 2 * HC
    fields = tuple(pltpu.with_memory_space_constraint(f, pltpu.HBM) for f in (gx, gy, wx, wy, an, pr))
    nb = ext // 128
    shape = lambda *dims: jax.ShapeDtypeStruct(dims, F32)
    params = pltpu.CompilerParams(vmem_limit_bytes=48 * 1024 * 1024)

    def call(kernel, name, args, outs, scratch=(), us=1, fetches=0):
        sems = [pltpu.SemaphoreType.DMA((fetches,))] if fetches else []
        return pl.pallas_call(
            kernel,
            in_specs=[HBM if fetches else VMEM] * len(args),
            out_specs=[VMEM] * len(outs),
            out_shape=outs,
            scratch_shapes=[pltpu.VMEM(dims, F32) for dims in scratch] + sems,
            compiler_params=params,
            cost_estimate=pl.CostEstimate(flops=us * 2_000_000, bytes_accessed=us * 2_000_000, transcendentals=0),
            name=name,
        )(*args)

    halos = []
    for inner in (True, False) if ncol > 2 else (True,):
        (edge,) = call(functools.partial(edge_columns, inner), "edge_columns", fields, [shape(n + 8, 256)], [(n, 128)] * 6, 1, 6)
        halos.append(swap(edge, "col", ncol, inner))
    tile = shape(nb - 1, n, 128)
    own = call(tile_fields, "tile_fields", fields, [tile] * 4 + [shape(n, 128), shape(nb - 1, 8, 128)], [(n, width)] * 6 + [(4, nb - 1, n, 128)] * 2 + [(2, nb - 1, 8, 128)], 1, 6)
    cb = layout(nb).coarse_blocks
    far = shape(cb, FAR, 128)
    msg = shape(nb, DEPTH, 128)
    field = shape(nb, n, 128)
    work = [(nb, 40 + 2 * GUARD, 128)] * 5 + [(5, cb, 24, 128), (5, cb, 8, 128)]
    *fields, to_out, g_a, cr_a, cd_a, ca_a = call(
        functools.partial(edge_rows, len(halos) > 1),
        "edge_rows",
        (*own, *halos),
        [field, field, shape(nb, GUARD + n, 128), field, shape(nb, 8, 128), msg] + [far] * 4,
        work,
    )
    from_out = swap(to_out, "row", nrow, False)
    di, to_in, *far_b = call(near_rows, "near_rows", fields, [field, msg] + [far] * 4, work)
    from_in = swap(to_in, "row", nrow, True)
    fine = n + 2 * HR
    coarse = n // 4 + 2 * FAR
    mom, *vectors = call(
        basis,
        "basis",
        (*fields, g_a, cr_a, cd_a, ca_a, di, *far_b, from_in, from_out),
        [shape(nrow * ncol, 1, 128)] + [tile] * 7,
        [(nb, fine + 2 * GUARD, 128)] * 10 + [(cb, coarse + 2 * GUARD, 128)] * 8 + [(5, cb, 16, 128), (2, cb, 8, 128)],
    )
    mom = lax.all_to_all(mom, ("row", "col"), 0, 0, tiled=True)
    out = shape(n, width)
    return tuple(call(combine, "combine", (mom, *vectors), [out, out], [(6, nb - 1, n, 128)]))


def solution(mesh):
    spec = P("row", "col")
    return jax.shard_map(
        functools.partial(local, mesh.shape["row"], mesh.shape["col"]),
        mesh=mesh,
        in_specs=(spec,) * 6,
        out_specs=(spec, spec),
        check_vma=False,
    )
```

```python
import functools

import jax
import jax.numpy as jnp
from jax import lax
from jax.experimental import pallas as pl
from jax.experimental.pallas import tpu as pltpu
from jax.sharding import PartitionSpec as P

DAMP = 2.0 / 3.0
SHIFT = 1.0
HC = 64
HR = 8
FAR = 12
DEPTH = 4 * HR + FAR - 1 + 5
GUARD = 8
VMEM = pl.BlockSpec(memory_space=pltpu.VMEM)
HBM = pl.BlockSpec(memory_space=pltpu.HBM)
F32 = jnp.float32


def lanes(shape):
    return lax.broadcasted_iota(jnp.int32, shape, 1)


def rows(shape):
    return lax.broadcasted_iota(jnp.int32, shape, 0)


def roll_right(x, k=1):
    return pltpu.roll(x, k, 1)


def roll_left(x, k=1):
    return pltpu.roll(x, x.shape[1] - k, 1)


def group_sum(x):
    four = lanes(x.shape) % 4
    one = jnp.where(four < 3, roll_left(x), roll_right(x, 3))
    two = jnp.where(four < 2, roll_left(x, 2), roll_right(x, 2))
    three = jnp.where(four < 1, roll_left(x, 3), roll_right(x))
    return (x + two) + (one + three)


def split(x):
    return [x[:, j : j + 128] for j in range(0, x.shape[1], 128)]


def join(parts):
    return jnp.concatenate(parts, axis=1)


class Wide:
    def __init__(self, width):
        self.coarse_blocks = width // 128 + 1

    left, right = staticmethod(roll_right), staticmethod(roll_left)
    total = staticmethod(group_sum)
    spread = take = staticmethod(lambda x: x)
    steps_in = steps_out = (lambda parts: parts,)

    def coarse_left(self, e):
        return roll_right(e, 4)

    def coarse_right(self, e):
        return roll_left(e, 4)

    def last_column(self, x):
        return group_sum(jnp.where(lanes(x.shape) % 4 == 3, x, F32(0.0)))

    def pack(self, a, b, c, d):
        four = lanes(a.shape) % 4
        return jnp.where(four < 2, jnp.where(four == 0, a, b), jnp.where(four == 2, c, d))

    def unpack(self, m, k):
        return group_sum(jnp.where(lanes(m.shape) % 4 == k, m, F32(0.0)))

    def unpack_rows(self, m):
        return group_sum(jnp.where(lanes(m.shape) % 4 == rows(m.shape) % 4, m, F32(0.0)))

    def first_only(self, x):
        return jnp.where(lanes(x.shape) % 4 == 0, x, F32(0.0))

    def last_only(self, x):
        return jnp.where(lanes(x.shape) % 4 == 3, x, F32(0.0))


class Planes:
    coarse_blocks = 2

    def left(self, x):
        a, b, c, d, h = split(x)
        first = lanes(h.shape) == 0
        d, h = roll_right(d), roll_right(h)
        return join([jnp.where(first, h, d), a, b, c, jnp.where(first, d, h)])

    def right(self, x):
        a, b, c, d, h = split(x)
        last = lanes(h.shape) == 127
        a, h = roll_left(a), roll_left(h)
        return join([b, c, d, jnp.where(last, h, a), jnp.where(last, a, h)])

    def coarse_left(self, e):
        o, h = split(e)
        lane = lanes(h.shape)
        end = jnp.broadcast_to(o[:, 127:128], h.shape)
        return join([jnp.where(lane == 0, roll_right(h), roll_right(o)), jnp.where(lane < 4, end, roll_right(h, 4))])

    def coarse_right(self, e):
        o, h = split(e)
        lane = lanes(h.shape)
        end = jnp.broadcast_to(o[:, 0:1], h.shape)
        return join([jnp.where(lane == 127, roll_left(h), roll_left(o)), jnp.where(lane >= 124, end, roll_left(h, 4))])

    def total(self, x):
        a, b, c, d, h = split(x)
        return join([(a + b) + (c + d), group_sum(h)])

    def last_column(self, x):
        h = x[:, 512:640]
        return join([x[:, 384:512], group_sum(jnp.where(lanes(h.shape) % 4 == 3, h, F32(0.0)))])

    def spread(self, e):
        o, h = split(e)
        return join([o, o, o, o, h])

    def take(self, x):
        return join([x[:, 0:128], x[:, 512:640]])

    def pack(self, *fields):
        own, halo = zip(*[split(f) for f in fields])
        a, b, c, d = halo
        four = lanes(a.shape) % 4
        mixed = jnp.where(four < 2, jnp.where(four == 0, a, b), jnp.where(four == 2, c, d))
        return join([*own, mixed])

    def unpack(self, m, k):
        h = m[:, 512:640]
        return join([m[:, k * 128 : k * 128 + 128], group_sum(jnp.where(lanes(h.shape) % 4 == k, h, F32(0.0)))])

    def unpack_rows(self, m):
        a, b, c, d, h = split(m)
        key = rows(h.shape) % 4
        own = jnp.where(key < 2, jnp.where(key == 0, a, b), jnp.where(key == 2, c, d))
        return join([own, group_sum(jnp.where(lanes(h.shape) % 4 == key, h, F32(0.0)))])

    def first_only(self, x):
        a, _, _, _, h = split(x)
        none = jnp.zeros_like(h)
        return join([a, none, none, none, jnp.where(lanes(h.shape) % 4 == 0, h, none)])

    def last_only(self, x):
        _, _, _, d, h = split(x)
        none = jnp.zeros_like(h)
        return join([none, none, none, d, jnp.where(lanes(h.shape) % 4 == 3, h, none)])

    def gather_in(self, parts):
        lane = lanes(parts[0].shape)
        index = (lane % 32) * 4 + lane // 32
        return [jnp.take_along_axis(p, index, axis=1) for p in parts]

    def gather_out(self, parts):
        lane = lanes(parts[0].shape)
        index = (lane % 4) * 32 + lane // 4
        return [jnp.take_along_axis(p, index, axis=1) for p in parts]

    def swap_halves(self, parts):
        a, b, c, d = parts
        low = lanes(a.shape) < 64
        return [
            jnp.where(low, a, roll_right(c, 64)),
            jnp.where(low, b, roll_right(d, 64)),
            jnp.where(low, roll_right(a, 64), c),
            jnp.where(low, roll_right(b, 64), d),
        ]

    def swap_quarters(self, parts):
        a, b, c, d = parts
        low = lanes(a.shape) % 64 < 32
        return [
            jnp.where(low, a, roll_right(b, 32)),
            jnp.where(low, roll_left(a, 32), b),
            jnp.where(low, c, roll_right(d, 32)),
            jnp.where(low, roll_left(c, 32), d),
        ]

    @property
    def steps_in(self):
        return self.gather_in, self.swap_halves, self.swap_quarters

    @property
    def steps_out(self):
        return self.swap_halves, self.swap_quarters, self.gather_out


class Rows:
    def __init__(self, own, ends):
        self.own, self.ends = own, ends

    def chunk(self, start):
        start -= GUARD + HR
        if 0 <= start < self.own.shape[1]:
            return ld(self.own, start)
        return ld(self.ends.at[int(start >= 0)], 0)


def layout(blocks):
    return Planes() if blocks == 5 else Wide(128 * (blocks - 1))


def ld(ref, start, count=8, step=1):
    rows_of = pl.ds(start, count, stride=step) if step > 1 else pl.ds(start, count)
    return jnp.concatenate([ref[j, rows_of, :] for j in range(ref.shape[0])], axis=1)


def st(ref, start, value, step=1):
    count = value.shape[0]
    rows_of = pl.ds(start, count, stride=step) if step > 1 else pl.ds(start, count)
    for j in range(ref.shape[0]):
        ref[j, rows_of, :] = value[:, j * 128 : (j + 1) * 128]


def tree(parts):
    while len(parts) > 1:
        parts = [sum(parts[j + 1 : j + 2], parts[j]) for j in range(0, len(parts), 2)]
    return parts[0]


def four_rows(ref, start, count):
    parts = [ld(ref, start + k, count, 4) for k in range(4)]
    return (parts[0] + parts[1]) + (parts[2] + parts[3])


def position():
    row, col = lax.axis_index("row"), lax.axis_index("col")
    end_row = row == lax.axis_size("row") - 1
    end_col = col == lax.axis_size("col") - 1
    return lax.rem(row, 2) == 1, lax.rem(col, 2) == 1, end_row, end_col


def reorder(steps, sources, targets, spare):
    pairs = list(zip(sources, spare))
    for k, step in enumerate(steps):
        for (x, y), target in zip(pairs, targets):
            x, y = (y, x) if k % 2 else (x, y)
            y = target if k == len(steps) - 1 else y
            for r in range(0, x.shape[1], 8):
                for j, block in enumerate(step([x[j, r : r + 8, :] for j in range(x.shape[0])])):
                    if len(y.shape) == 2:
                        y[r : r + 8, j * 128 : j * 128 + 128] = block
                    else:
                        y[j, r : r + 8, :] = block


def fetch(sources, targets, sems):
    copies = [pltpu.make_async_copy(x, y, sems.at[k]) for k, (x, y) in enumerate(zip(sources, targets))]
    for copy in copies:
        copy.start()
    for copy in copies:
        copy.wait()


def edge_columns(inner, *refs):
    fields, (out, *held, sems) = refs[:6], refs[6:]
    n, width = fields[0].shape
    _, col_odd, end_row, _ = position()
    last = jnp.logical_not(col_odd) if inner else col_odd
    offset = pl.multiple_of(jnp.where(last, width - 128, 0), 128)
    row, lane = rows((8, 128)), lanes((8, 128))
    zero = F32(0.0)
    fetch([f.at[:, pl.ds(offset, 128)] for f in fields], held, sems)

    def pair(x, y):
        low = jnp.where(lane < HC, x, roll_right(y, HC))
        high = jnp.where(lane < HC, roll_right(x, HC), y)
        return jnp.where(last, high, low)

    carry = jnp.zeros((1, 128), F32)
    for r in range(0, n, 8):
        g_x, g_y, w_x, w_y, a, p = [f[r : r + 8, :] for f in held]
        if r == n - 8:
            w_y = jnp.where((row == 7) & end_row, zero, w_y)
        fx = w_x * g_x
        fy = w_y * g_y
        before_x = jnp.where(lane == 0, zero, roll_right(fx))
        before_y = jnp.where(row == 0, jnp.broadcast_to(carry, fy.shape), pltpu.roll(fy, 1, 0))
        carry = fy[7:8, :]
        src = a * p + before_x - fx + before_y - fy
        edge = jnp.broadcast_to(fx[:, 127:128], fx.shape)
        out[r : r + 8, 0:128] = jnp.where((lane == 0) & last, edge, pair(src, w_x))
        out[r : r + 8, 128:256] = pair(w_y, a)
    tail = jnp.broadcast_to(carry, (8, 128))
    tail = pair(tail, tail)
    out[n : n + 8, 0:128] = tail
    out[n : n + 8, 128:256] = tail


def tile_fields(*refs):
    fields, (r_o, wx_o, wy_o, an_o, fx_o, fy_o, *held, raw, spare, tail, sems) = refs[:6], refs[6:]
    gx, gy, wx, wy, an, pr = held
    n, width = gx.shape
    form = layout(width // 128 + 1)
    fetch(fields, held, sems)
    _, _, end_row, end_col = position()
    row, lane = rows((8, width)), lanes((8, width))
    zero = F32(0.0)
    carry = jnp.zeros((1, width), F32)
    for r in range(0, n, 8):
        w_x = jnp.where((lane == width - 1) & end_col, zero, wx[r : r + 8, :])
        w_y = wy[r : r + 8, :]
        if r == n - 8:
            w_y = jnp.where((row == 7) & end_row, zero, w_y)
        fx = w_x * gx[r : r + 8, :]
        fy = w_y * gy[r : r + 8, :]
        a = an[r : r + 8, :]
        before_x = jnp.where(lane == 0, zero, roll_right(fx))
        before_y = jnp.where(row == 0, jnp.broadcast_to(carry, fy.shape), pltpu.roll(fy, 1, 0))
        carry = fy[7:8, :]
        src = a * pr[r : r + 8, :] + before_x - fx + before_y - fy
        for k, x in enumerate((src, w_x, w_y, a)):
            st(raw.at[k], r, x)
        fx_o[r : r + 8, :] = jnp.broadcast_to(fx[:, width - 1 : width], (8, 128))
    st(tail.at[0], 0, jnp.broadcast_to(carry, (8, width)))
    pick = lambda ref: [ref.at[k] for k in range(4)]
    reorder(form.steps_in, [*pick(raw), tail.at[0]], [r_o, wx_o, wy_o, an_o, fy_o], [*pick(spare), tail.at[1]])


def edge_rows(has_outer, r_t, wx_t, wy_t, an_t, fx_t, fy_t, *refs):
    inner, refs = refs[0], refs[1:]
    outer = None
    if has_outer:
        outer, refs = refs[0], refs[1:]
    r_o, wx_o, wy_o, an_o, fy_o, *rest = refs
    own, n, _ = r_t.shape
    form = layout(own + 1)
    row_odd, odd, _, _ = position()
    lane = lanes((8, 128))
    zero = F32(0.0)

    def halo(r, c):
        x = inner[r : r + 8, c : c + 128]
        y = outer[r : r + 8, c : c + 128] if has_outer else jnp.zeros_like(x)
        before, after = jnp.where(odd, x, y), jnp.where(odd, y, x)
        first = jnp.where(lane < HC, after, roll_right(before, HC))
        second = jnp.where(lane < HC, roll_right(after, HC), before)
        return first, second

    for r in range(0, n, 8):
        src_h, wx_h = halo(r, 0)
        wy_h, an_h = halo(r, 128)
        incoming = jnp.broadcast_to(src_h[:, HC : HC + 1], (8, 128))
        src_h = jnp.where(lane == 0, src_h + fx_t[r : r + 8, :], jnp.where(lane == HC, zero, src_h))
        for out, tile, h in ((r_o, r_t, src_h), (wx_o, wx_t, wx_h), (wy_o, wy_t, wy_h), (an_o, an_t, an_h)):
            top = GUARD if out is wy_o else 0
            for j in range(own):
                x = tile[j, r : r + 8, :]
                if out is r_o and j == 0:
                    x = jnp.where(lane == 0, x + incoming, x)
                out[j, top + r : top + r + 8, :] = x
            out[own, top + r : top + r + 8, :] = h
    st(wy_o, 0, jnp.zeros((GUARD, (own + 1) * 128), F32))
    for j in range(own):
        fy_o[j] = fy_t[j]
    fy_o[own] = halo(n, 0)[0]

    message(form, row_odd, r_o, wx_o, wy_o, an_o, fy_o, *rest)


def near_rows(r_i, wx_i, wy_i, an_i, fy_i, di, wl, *rest):
    form = layout(wx_i.shape[0])
    row_odd, _, _, _ = position()
    message(form, jnp.logical_not(row_odd), r_i, wx_i, wy_i, an_i, fy_i, *rest)
    for r in range(0, wx_i.shape[1], 8):
        w_x, w_y = ld(wx_i, r), ld(wy_i, GUARD + r)
        w_l = form.left(w_x)
        st(wl, r, w_l)
        diag = ld(an_i, r) + w_x + w_l + w_y + ld(wy_i, GUARD + r - 1)
        st(di, r, jnp.where(diag > F32(0.0), F32(1.0) / diag, F32(0.0)))


def message(form, bottom, r_o, wx_o, wy_o, an_o, fy_o, msg, g_o, cr_o, cd_o, ca_o, U, DI, V, WL, T, H, K):
    n = r_o.shape[1]
    zero = F32(0.0)
    G = GUARD

    def pick(low, high):
        return jnp.where(bottom, high, low)

    def align(x):
        return pl.multiple_of(x, 8)

    base = align(pick(0, n - 40))
    for r in range(0, 40, 8):
        at = align(base + r)
        w_x = ld(wx_o, at)
        w_l = form.left(w_x)
        st(WL, G + r, w_l)
        diag = ld(an_o, at) + w_x + w_l + ld(wy_o, align(at + G)) + ld(wy_o, base + (r + G - 1))
        inverse = jnp.where(diag > zero, F32(1.0) / diag, zero)
        st(DI, G + r, inverse)
        st(U, G + r, ld(r_o, at) * inverse)
    for source, image in ((U, T), (V, U)):
        for r in range(0, 40, 8):
            at = align(base + r)
            x = ld(source, G + r)
            beside = ld(WL, G + r) * (x - form.left(x)) + ld(wx_o, at) * (x - form.right(x))
            down = ld(wy_o, align(at + G)) * (x - ld(source, G + r + 1))
            up = ld(wy_o, base + (r + G - 1)) * (x - ld(source, G + r - 1))
            y = (ld(an_o, at) * x + beside) + (down + up)
            st(image, G + r, y)
            if image is T:
                st(V, G + r, ld(DI, G + r) * y)
    near = align(pick(0, 8))
    sums = form.total(four_rows(T, align(near + G), 8))
    sums_2 = form.total(four_rows(U, pick(0, 20) + G, 4))
    parts = {}

    def add(name, x):
        parts[name] = parts[name] + x if name in parts else x

    for k in range(4):
        at = base + (near + k)
        w_x = ld(wx_o, at, 8, 4)
        first, last = form.first_only(ld(WL, near + (G + k), 8, 4)), form.last_only(w_x)
        a = ld(an_o, at, 8, 4) + first + last
        inverse = ld(DI, near + (G + k), 8, 4)
        sides = []
        if k == 0:
            w = ld(wy_o, at + (G - 1), 8, 4)
            sides.append(("u", w))
            a = a + w
        if k == 3:
            w = ld(wy_o, at + G, 8, 4)
            sides.append(("d", w))
            a = a + w
        weighted = inverse * a
        add("aa", weighted * a)
        for name, w in (("l", first), ("r", last)):
            add("a" + name, weighted * w)
            scaled = inverse * w
            add(name + name, scaled * w)
            for other, v in sides:
                add(name + other, scaled * v)
        for name, w in sides:
            add("a" + name, weighted * w)
            add(name + name, inverse * w * w)
    parts = {name: form.total(x) for name, x in parts.items()}
    for k, name in enumerate(("uu", "dd", "au", "ru", "lu")):
        st(H.at[k], G, parts[name])
    uu, au, ru, lu = [ld(H.at[k], G + 1) for k in (0, 2, 3, 4)]
    dd = ld(H.at[1], G - 1)
    centre = parts["aa"] + form.coarse_right(parts["ll"]) + form.coarse_left(parts["rr"]) + uu + dd
    east = -(parts["ar"] + form.coarse_right(parts["al"]))
    south = -(parts["ad"] + au)
    south_east = form.coarse_right(parts["ld"]) + ru
    south_west = form.coarse_left(parts["rd"]) + lu
    for k, x in enumerate((centre, east, south, south_east, south_west)):
        st(K.at[k], 0, x)

    c = align(pick(0, n - 4 * FAR))
    coarse = (
        form.total(four_rows(r_o, c, FAR)),
        form.last_column(four_rows(wx_o, c, FAR)),
        form.total(ld(wy_o, c + (G + 3), FAR, 4)),
        form.total(four_rows(an_o, c, FAR)),
    )
    for out, x in zip((g_o, cr_o, cd_o, ca_o), coarse):
        st(out, 0, x)
    start = align(pick(0, n - HR))
    for k, (ref, top) in enumerate(((r_o, 0), (wx_o, 0), (wy_o, G), (an_o, 0))):
        st(msg, k * HR, ld(ref, align(start + top), HR))
    outer, inner = pick(HR - 1, 0), pick(HR - 2, 1)
    st(msg, outer, form.pack(*[sums[k : k + 1] for k in range(4)]))
    st(msg, inner, form.pack(*[sums[k : k + 1] for k in range(4, 8)]))
    st(msg, HR + outer, form.spread(form.total(ld(wy_o, n - 4 * FAR - 1 + G, 1))))
    st(msg, HR + inner, form.pack(*[sums_2[k : k + 1] for k in range(4)]))
    st(msg, 3 * HR + outer, ld(fy_o, 0, 1))
    packed = form.pack(*coarse)
    st(msg, 4 * HR, jnp.where(bottom, packed[: FAR - 1], packed[1:]))
    for k in range(5):
        four = [ld(K.at[k], pick(0, 3) + i, 1) for i in range(4)]
        st(msg, 4 * HR + FAR - 1 + k, form.pack(*four))


def apply_a(form, v, w_l, w_r, w_y, an, r):
    x = ld(v, r)
    down = ld(w_y, r) * (x - ld(v, r + 1))
    up = ld(w_y, r - 1) * (x - ld(v, r - 1))
    beside = w_l.chunk(r) * (x - form.left(x)) + w_r.chunk(r) * (x - form.right(x))
    return (an.chunk(r) * x + beside) + (down + up)


def basis(r_i, wx_i, wy_i, an_i, fy_i, g_a, cr_a, cd_a, ca_a, di_i, wl_i, g_b, cr_b, cd_b, ca_b, msg_in, msg_out, mom, p0, p1, p2, q0, q1, q2, r0,
         ENDS, WY, PA, PB, QA, C_L, C_R, C_D, C_A, C_I, EA, EB, GC, KF, KV):
    blocks, n, _ = r_i.shape
    form = layout(blocks)
    fine = n + 2 * HR
    coarse = n // 4 + 2 * FAR
    zero = F32(0.0)
    odd, _, _, _ = position()
    own_blocks = blocks - 1
    B = GUARD

    def sides(a, b):
        x, y = ld(msg_in, a, b - a), ld(msg_out, a, b - a)
        return jnp.where(odd, x, y), jnp.where(odd, y, x)

    zeros = jnp.zeros((B, blocks * 128), F32)
    coarse_zeros = jnp.zeros((B, form.coarse_blocks * 128), F32)
    R, WX, AN, DI, WL = [Rows(own, ENDS.at[k]) for k, own in enumerate((r_i, wx_i, an_i, di_i, wl_i))]
    for ref in (WY, PA, PB):
        st(ref, 0, zeros)
        st(ref, B + fine, zeros)
    for k, ends in ((0, ENDS.at[0]), (1, ENDS.at[1]), (3, ENDS.at[2])):
        for end, x in enumerate(sides(k * HR, (k + 1) * HR)):
            st(ends.at[end], 0, x)
    up, down = sides(2 * HR, 3 * HR)
    st(WY, B, up)
    st(WY, B + HR + n, down)
    for r in range(0, n, 8):
        st(WY, B + HR + r, ld(wy_i, GUARD + r))
    flux_up, _ = sides(3 * HR, 3 * HR + 1)
    first_rows = ld(r_i, 0) + jnp.where(rows(zeros.shape) == 0, jnp.broadcast_to(flux_up, zeros.shape), zero)
    below = ENDS.at[0, 1]
    st(below, 0, ld(below, 0, 1) + ld(fy_i, 0, 1))

    for end in (0, 1):
        st(ENDS.at[4, end], 0, form.left(ld(ENDS.at[1, end], 0)))

    def inverse(r):
        diag = AN.chunk(r) + WX.chunk(r) + WL.chunk(r) + ld(WY, r) + ld(WY, r - 1)
        return jnp.where(diag > zero, F32(1.0) / diag, zero)

    st(ENDS.at[3, 0], 0, inverse(B))
    st(ENDS.at[3, 1], 0, inverse(B + HR + n))
    first_inverse = inverse(B + HR)

    def read(field, r, first):
        return first if r == B + HR else field.chunk(r)

    for ref in (EA, EB, C_D):
        st(ref, 0, coarse_zeros)
        st(ref, B + coarse, coarse_zeros)
    up, down = sides(4 * HR, 4 * HR + FAR - 1)
    for k, (ref, a, b) in enumerate(((GC, g_a, g_b), (C_R, cr_a, cr_b), (C_D, cd_a, cd_b), (C_A, ca_a, ca_b))):
        st(ref, B, form.unpack(up, k))
        st(ref, B + coarse - FAR + 1, form.unpack(down, k))
        x, y = ld(a, 0, FAR), ld(b, 0, FAR)
        st(ref, B + FAR, jnp.where(odd, y, x))
        st(ref, B + 2 * FAR, jnp.where(odd, x, y))
    st(GC, B + FAR, ld(GC, B + FAR, 1) + form.total(flux_up))
    beyond, _ = sides(HR, HR + 1)
    st(C_D, B - 1, form.take(beyond))
    for c in (FAR - 1, coarse - FAR):
        f = B + 4 * c - 40
        end, at = (0, 4) if c < FAR else (1, 0)
        st(GC, B + c, form.total(four_rows(ENDS.at[0, end], at, 1)))
        st(C_R, B + c, form.last_column(four_rows(ENDS.at[1, end], at, 1)))
        st(C_D, B + c, form.total(ld(WY, f + 3, 1)))
        st(C_A, B + c, form.total(four_rows(ENDS.at[2, end], at, 1)))
    for c in range(B, B + coarse, 8):
        c_r = ld(C_R, c)
        c_l = form.coarse_left(c_r)
        total = ld(C_A, c) + c_l + c_r + ld(C_D, c - 1) + ld(C_D, c)
        st(C_L, c, c_l)
        inverse_c = jnp.where(total > zero, F32(DAMP) / total, zero)
        st(C_I, c, inverse_c)
        st(EA, c, inverse_c * ld(GC, c))

    def set_sums(c, g):
        st(GC, B + c, g)
        st(EA, B + c, ld(C_I, B + c, g.shape[0]) * g)

    def smooth(lo, hi):
        if lo > 0:
            st(EA, B + lo - 8, coarse_zeros)
            st(EB, B + lo - 8, coarse_zeros)
        if hi < coarse:
            st(EA, B + hi, coarse_zeros)
            st(EB, B + hi, coarse_zeros)
        old, new = EA, EB
        for turn in range(3):
            for c in range(B + lo, B + hi, 8):
                e = ld(old, c)
                beside = ld(C_L, c) * form.coarse_left(e) + ld(C_R, c) * form.coarse_right(e)
                beside = beside + (ld(C_D, c - 1) * ld(old, c - 1) + ld(C_D, c) * ld(old, c + 1))
                st(new, c, F32(1.0 - DAMP) * e + ld(C_I, c) * (ld(GC, c) + beside))
            old, new = new, old

    def coarse_part(r):
        at = B + 10 + (r - B) // 4
        shape = (8, form.coarse_blocks * 128)
        a, b = [jnp.broadcast_to(ld(EB, at + k, 1), shape) for k in (0, 1)]
        return form.spread(jnp.where(rows(shape) < 4, a, b))

    def direct(p, residual, before):
        for r in range(B, B + fine, 8):
            x = read(DI, r, first_inverse) * residual(r) + coarse_part(r)
            if before is not None:
                x = x - F32(SHIFT) * ld(before, r)
            st(p, r, x)

    def image_of(p, p_out, q_out):
        for r in range(B, B + fine, 8):
            q = apply_a(form, p, WL, WX, WY, AN, r)
            st(QA, r, q)
            at = r - B - HR
            if 0 <= at < n:
                for k in range(own_blocks):
                    p_out[k, at : at + 8, :] = p[k, r : r + 8, :]
                    q_out[k, at : at + 8, :] = q[:, k * 128 : k * 128 + 128]

    def restrict(q):
        for c in range(FAR - 1, coarse - FAR + 1, 8):
            count = min(8, coarse - FAR + 1 - c)
            set_sums(c, form.total(four_rows(q, B + 4 * c - 40, count)))

    def coarse_image(c, count):
        e = ld(EB, B + c, count)
        c_l, c_r = ld(C_L, B + c, count), ld(C_R, B + c, count)
        image = ld(C_A, B + c, count) * e + c_l * (e - form.coarse_left(e)) + c_r * (e - form.coarse_right(e))
        image = image + ld(C_D, B + c - 1, count) * (e - ld(EB, B + c - 1, count))
        return image + ld(C_D, B + c, count) * (e - ld(EB, B + c + 1, count))

    def stretch(a, b):
        shape = (8, a.shape[1])
        return form.unpack_rows(jnp.where(rows(shape) < 4, jnp.broadcast_to(a, shape), jnp.broadcast_to(b, shape)))

    def second_sums(side, c, sums):
        for k in range(5):
            at = 4 * HR + FAR - 1 + k
            row = sides(at, at + 1)[side]
            st(KF.at[k], 8, form.unpack_rows(jnp.broadcast_to(row, (4, row.shape[1]))))
        centre, east, south, south_east, south_west = [ld(KF.at[k], 8, 4) for k in range(5)]
        north, north_west, north_east = [ld(KF.at[k], 7, 4) for k in (2, 3, 4)]
        e, below, above = [ld(EB, B + c + d, 4) for d in (0, 1, -1)]
        image = centre * e + east * form.coarse_right(e) + form.coarse_left(east * e)
        image = image + south * below + north * above
        image = image + south_east * form.coarse_right(below) + form.coarse_left(north_west * above)
        image = image + south_west * form.coarse_left(below) + form.coarse_right(north_east * above)
        st(KV.at[side], 0, image + form.unpack_rows(jnp.broadcast_to(sums, (4, sums.shape[1]))))

    smooth(0, coarse)
    direct(PA, lambda r: read(R, r, first_rows), None)
    image_of(PA, p0, q0)
    for r in range(0, n, 8):
        for k in range(own_blocks):
            r0[k, r : r + 8, :] = first_rows[:, k * 128 : k * 128 + 128] if r == 0 else r_i[k, r : r + 8, :]
    restrict(QA)
    far_up, _ = sides(0, 1)
    near_up, _ = sides(1, 2)
    _, near_down = sides(HR - 1, HR)
    _, far_down = sides(HR - 2, HR - 1)
    up = stretch(far_up, near_up)
    down = stretch(near_down, far_down)
    image = coarse_image(0, FAR - 1)
    set_sums(0, image[0:4])
    set_sums(4, image[4:] + up[0 : FAR - 5])
    image = coarse_image(coarse - FAR + 1, FAR - 1)
    set_sums(coarse - FAR + 1, image[0:7] + down[1:])
    set_sums(coarse - 4, image[7:])
    second_sums(0, 7, sides(HR + 1, HR + 2)[0])
    second_sums(1, coarse - FAR, sides(2 * HR - 2, 2 * HR - 1)[1])
    smooth(0, coarse)
    direct(PB, lambda r: ld(QA, r), PA)
    image_of(PB, p1, q1)
    restrict(QA)
    for c, side, first in ((8, 0, 1), (coarse - FAR + 1, 1, 1)):
        image = coarse_image(c, 3) + ld(KV.at[side], first, 3)
        set_sums(c, image - F32(SHIFT) * ld(GC, B + c, 3))
    smooth(8, coarse - 8)
    direct(PA, lambda r: ld(QA, r), PB)
    acc = [jnp.zeros((8, 128), F32) for _ in range(9)]
    for r in range(0, n, 8):
        f = B + HR + r
        image = apply_a(form, PA, WL, WX, WY, AN, f)
        sums = [[] for _ in acc]
        for j in range(own_blocks):
            z2, i2 = PA[j, f : f + 8, :], image[:, j * 128 : (j + 1) * 128]
            p2[j, r : r + 8, :] = z2
            q2[j, r : r + 8, :] = i2
            z0, z1, i0, i1, res = [x[j, r : r + 8, :] for x in (p0, p1, q0, q1, r0)]
            pairs = ((z0, i0), (z1, i0), (z1, i1), (z2, i0), (z2, i1), (z2, i2), (z0, res), (z1, res), (z2, res))
            for k, (x, y) in enumerate(pairs):
                sums[k].append(x * y)
        for k, parts in enumerate(sums):
            acc[k] = acc[k] + tree(parts)
    lane = lanes((8, 128))
    line = jnp.zeros((8, 128), F32)
    for k in range(9):
        total = jnp.sum(jnp.sum(acc[k], axis=0, keepdims=True), axis=1, keepdims=True)
        line = jnp.where(lane == k, jnp.broadcast_to(total, (8, 128)), line)
    for j in range(mom.shape[0]):
        mom[j] = line[0:1]


def combine(mom, p0, p1, p2, q0, q1, q2, r0, heights, residual, work):
    blocks, n, _ = p0.shape
    form = layout(blocks + 1)
    tot = jnp.broadcast_to(tree([mom[j] for j in range(mom.shape[0])]), (8, 128))
    m = [jnp.broadcast_to(tot[:, k : k + 1], (8, 128)) for k in range(9)]
    g00, g10, g11, g20, g21, g22, b0, b1, b2 = m
    l10, l20 = g10 / g00, g20 / g00
    d1 = g11 - l10 * g10
    t21 = g21 - l20 * g10
    l21 = t21 / d1
    d2 = g22 - l20 * g20 - l21 * t21
    y1 = b1 - l10 * b0
    y2 = b2 - l20 * b0 - l21 * y1
    x2 = y2 / d2
    x1 = y1 / d1 - l21 * x2
    x0 = b0 / g00 - l10 * x1 - l20 * x2
    sums, spare = [[work.at[k], work.at[k + 1]] for k in (0, 2)]
    for r in range(0, n, 8):
        for j in range(blocks):
            z0, z1, z2, i0, i1, i2, res = [x[j, r : r + 8, :] for x in (p0, p1, p2, q0, q1, q2, r0)]
            sums[0][j, r : r + 8, :] = x0 * z0 + x1 * z1 + x2 * z2
            sums[1][j, r : r + 8, :] = res - (x0 * i0 + x1 * i1 + x2 * i2)
    reorder(form.steps_out, sums, [heights, residual], spare)


def swap(x, axis, size, inner):
    if inner:
        pairs = [(i, i ^ 1) for i in range(size) if i ^ 1 < size]
    else:
        pairs = [(i, j) for i in range(size) for j in [((i + 1) ^ 1) - 1] if 0 <= j < size]
    return lax.ppermute(x, axis, pairs)


def local(nrow, ncol, gx, gy, wx, wy, an, pr):
    n, width = gx.shape
    ext = width + 2 * HC
    fields = tuple(pltpu.with_memory_space_constraint(f, pltpu.HBM) for f in (gx, gy, wx, wy, an, pr))
    nb = ext // 128
    shape = lambda *dims: jax.ShapeDtypeStruct(dims, F32)
    params = pltpu.CompilerParams(vmem_limit_bytes=48 * 1024 * 1024)

    def call(kernel, name, args, outs, scratch=(), us=1, fetches=0):
        sems = [pltpu.SemaphoreType.DMA((fetches,))] if fetches else []
        return pl.pallas_call(
            kernel,
            in_specs=[HBM if fetches else VMEM] * len(args),
            out_specs=[VMEM] * len(outs),
            out_shape=outs,
            scratch_shapes=[pltpu.VMEM(dims, F32) for dims in scratch] + sems,
            compiler_params=params,
            cost_estimate=pl.CostEstimate(flops=us * 2_000_000, bytes_accessed=us * 2_000_000, transcendentals=0),
            name=name,
        )(*args)

    halos = []
    for inner in (True, False) if ncol > 2 else (True,):
        (edge,) = call(functools.partial(edge_columns, inner), "edge_columns", fields, [shape(n + 8, 256)], [(n, 128)] * 6, 1, 6)
        halos.append(swap(edge, "col", ncol, inner))
    tile = shape(nb - 1, n, 128)
    own = call(tile_fields, "tile_fields", fields, [tile] * 4 + [shape(n, 128), shape(nb - 1, 8, 128)], [(n, width)] * 6 + [(4, nb - 1, n, 128)] * 2 + [(2, nb - 1, 8, 128)], 1, 6)
    cb = layout(nb).coarse_blocks
    far = shape(cb, FAR, 128)
    msg = shape(nb, DEPTH, 128)
    field = shape(nb, n, 128)
    work = [(nb, 40 + 2 * GUARD, 128)] * 5 + [(5, cb, 24, 128), (5, cb, 8, 128)]
    *fields, to_out, g_a, cr_a, cd_a, ca_a = call(
        functools.partial(edge_rows, len(halos) > 1),
        "edge_rows",
        (*own, *halos),
        [field, field, shape(nb, GUARD + n, 128), field, shape(nb, 8, 128), msg] + [far] * 4,
        work,
    )
    from_out = swap(to_out, "row", nrow, False)
    di, wl, to_in, *far_b = call(near_rows, "near_rows", fields, [field, field, msg] + [far] * 4, work)
    from_in = swap(to_in, "row", nrow, True)
    fine = n + 2 * HR
    coarse = n // 4 + 2 * FAR
    mom, *vectors = call(
        basis,
        "basis",
        (*fields, g_a, cr_a, cd_a, ca_a, di, wl, *far_b, from_in, from_out),
        [shape(nrow * ncol, 1, 128)] + [tile] * 7,
        [(5, 2, nb, HR, 128)] + [(nb, fine + 2 * GUARD, 128)] * 4 + [(cb, coarse + 2 * GUARD, 128)] * 8 + [(5, cb, 16, 128), (2, cb, 8, 128)],
    )
    mom = lax.all_to_all(mom, ("row", "col"), 0, 0, tiled=True)
    out = shape(n, width)
    return tuple(call(combine, "combine", (mom, *vectors), [out, out], [(4, nb - 1, n, 128)]))


def solution(mesh):
    spec = P("row", "col")
    return jax.shard_map(
        functools.partial(local, mesh.shape["row"], mesh.shape["col"]),
        mesh=mesh,
        in_specs=(spec,) * 6,
        out_specs=(spec, spec),
        check_vma=False,
    )
```

```python
import functools

import jax
import jax.numpy as jnp
from jax import lax
from jax.experimental import pallas as pl
from jax.experimental.pallas import tpu as pltpu
from jax.sharding import PartitionSpec as P

DAMP = 2.0 / 3.0
SHIFT = 1.0
HC = 64
SENT = 48
HR = 8
FAR = 12
DEPTH = 4 * HR + FAR - 1 + 5
GUARD = 8
VMEM = pl.BlockSpec(memory_space=pltpu.VMEM)
HBM = pl.BlockSpec(memory_space=pltpu.HBM)
F32 = jnp.float32


def lanes(shape):
    return lax.broadcasted_iota(jnp.int32, shape, 1)


def rows(shape):
    return lax.broadcasted_iota(jnp.int32, shape, 0)


def roll_right(x, k=1):
    return pltpu.roll(x, k, 1)


def roll_left(x, k=1):
    return pltpu.roll(x, x.shape[1] - k, 1)


def group_sum(x):
    four = lanes(x.shape) % 4
    one = jnp.where(four < 3, roll_left(x), roll_right(x, 3))
    two = jnp.where(four < 2, roll_left(x, 2), roll_right(x, 2))
    three = jnp.where(four < 1, roll_left(x, 3), roll_right(x))
    return (x + two) + (one + three)


def split(x):
    return [x[:, j : j + 128] for j in range(0, x.shape[1], 128)]


def join(parts):
    return jnp.concatenate(parts, axis=1)


class Wide:
    def __init__(self, width):
        self.coarse_blocks = width // 128 + 1

    left, right = staticmethod(roll_right), staticmethod(roll_left)
    total = staticmethod(group_sum)
    spread = take = staticmethod(lambda x: x)
    steps_in = steps_out = (lambda parts: parts,)

    def coarse_left(self, e):
        return roll_right(e, 4)

    def coarse_right(self, e):
        return roll_left(e, 4)

    def last_column(self, x):
        return group_sum(jnp.where(lanes(x.shape) % 4 == 3, x, F32(0.0)))

    def pack(self, a, b, c, d):
        four = lanes(a.shape) % 4
        return jnp.where(four < 2, jnp.where(four == 0, a, b), jnp.where(four == 2, c, d))

    def unpack(self, m, k):
        return group_sum(jnp.where(lanes(m.shape) % 4 == k, m, F32(0.0)))

    def unpack_rows(self, m):
        return group_sum(jnp.where(lanes(m.shape) % 4 == rows(m.shape) % 4, m, F32(0.0)))

    def first_only(self, x):
        return jnp.where(lanes(x.shape) % 4 == 0, x, F32(0.0))

    def last_only(self, x):
        return jnp.where(lanes(x.shape) % 4 == 3, x, F32(0.0))


class Planes:
    coarse_blocks = 2

    def left(self, x):
        a, b, c, d, h = split(x)
        first = lanes(h.shape) == 0
        d, h = roll_right(d), roll_right(h)
        return join([jnp.where(first, h, d), a, b, c, jnp.where(first, d, h)])

    def right(self, x):
        a, b, c, d, h = split(x)
        last = lanes(h.shape) == 127
        a, h = roll_left(a), roll_left(h)
        return join([b, c, d, jnp.where(last, h, a), jnp.where(last, a, h)])

    def coarse_left(self, e):
        o, h = split(e)
        lane = lanes(h.shape)
        end = jnp.broadcast_to(o[:, 127:128], h.shape)
        return join([jnp.where(lane == 0, roll_right(h), roll_right(o)), jnp.where(lane < 4, end, roll_right(h, 4))])

    def coarse_right(self, e):
        o, h = split(e)
        lane = lanes(h.shape)
        end = jnp.broadcast_to(o[:, 0:1], h.shape)
        return join([jnp.where(lane == 127, roll_left(h), roll_left(o)), jnp.where(lane >= 124, end, roll_left(h, 4))])

    def total(self, x):
        a, b, c, d, h = split(x)
        return join([(a + b) + (c + d), group_sum(h)])

    def last_column(self, x):
        h = x[:, 512:640]
        return join([x[:, 384:512], group_sum(jnp.where(lanes(h.shape) % 4 == 3, h, F32(0.0)))])

    def spread(self, e):
        o, h = split(e)
        return join([o, o, o, o, h])

    def take(self, x):
        return join([x[:, 0:128], x[:, 512:640]])

    def pack(self, *fields):
        own, halo = zip(*[split(f) for f in fields])
        a, b, c, d = halo
        four = lanes(a.shape) % 4
        mixed = jnp.where(four < 2, jnp.where(four == 0, a, b), jnp.where(four == 2, c, d))
        return join([*own, mixed])

    def unpack(self, m, k):
        h = m[:, 512:640]
        return join([m[:, k * 128 : k * 128 + 128], group_sum(jnp.where(lanes(h.shape) % 4 == k, h, F32(0.0)))])

    def unpack_rows(self, m):
        a, b, c, d, h = split(m)
        key = rows(h.shape) % 4
        own = jnp.where(key < 2, jnp.where(key == 0, a, b), jnp.where(key == 2, c, d))
        return join([own, group_sum(jnp.where(lanes(h.shape) % 4 == key, h, F32(0.0)))])

    def first_only(self, x):
        a, _, _, _, h = split(x)
        none = jnp.zeros_like(h)
        return join([a, none, none, none, jnp.where(lanes(h.shape) % 4 == 0, h, none)])

    def last_only(self, x):
        _, _, _, d, h = split(x)
        none = jnp.zeros_like(h)
        return join([none, none, none, d, jnp.where(lanes(h.shape) % 4 == 3, h, none)])

    def gather_in(self, parts):
        lane = lanes(parts[0].shape)
        index = (lane % 32) * 4 + lane // 32
        return [jnp.take_along_axis(p, index, axis=1) for p in parts]

    def gather_out(self, parts):
        lane = lanes(parts[0].shape)
        index = (lane % 4) * 32 + lane // 4
        return [jnp.take_along_axis(p, index, axis=1) for p in parts]

    def swap_halves(self, parts):
        a, b, c, d = parts
        low = lanes(a.shape) < 64
        return [
            jnp.where(low, a, roll_right(c, 64)),
            jnp.where(low, b, roll_right(d, 64)),
            jnp.where(low, roll_right(a, 64), c),
            jnp.where(low, roll_right(b, 64), d),
        ]

    def swap_quarters(self, parts):
        a, b, c, d = parts
        low = lanes(a.shape) % 64 < 32
        return [
            jnp.where(low, a, roll_right(b, 32)),
            jnp.where(low, roll_left(a, 32), b),
            jnp.where(low, c, roll_right(d, 32)),
            jnp.where(low, roll_left(c, 32), d),
        ]

    @property
    def steps_in(self):
        return self.gather_in, self.swap_halves, self.swap_quarters

    @property
    def steps_out(self):
        return self.swap_halves, self.swap_quarters, self.gather_out


class Rows:
    def __init__(self, own, ends):
        self.own, self.ends = own, ends

    def chunk(self, start):
        start -= GUARD + HR
        if 0 <= start < self.own.shape[1]:
            return ld(self.own, start)
        return ld(self.ends.at[int(start >= 0)], 0)


def layout(blocks):
    return Planes() if blocks == 5 else Wide(128 * (blocks - 1))


def ld(ref, start, count=8, step=1):
    rows_of = pl.ds(start, count, stride=step) if step > 1 else pl.ds(start, count)
    return jnp.concatenate([ref[j, rows_of, :] for j in range(ref.shape[0])], axis=1)


def st(ref, start, value, step=1):
    count = value.shape[0]
    rows_of = pl.ds(start, count, stride=step) if step > 1 else pl.ds(start, count)
    for j in range(ref.shape[0]):
        ref[j, rows_of, :] = value[:, j * 128 : (j + 1) * 128]


def tree(parts):
    while len(parts) > 1:
        parts = [sum(parts[j + 1 : j + 2], parts[j]) for j in range(0, len(parts), 2)]
    return parts[0]


def four_rows(ref, start, count):
    parts = [ld(ref, start + k, count, 4) for k in range(4)]
    return (parts[0] + parts[1]) + (parts[2] + parts[3])


def position():
    row, col = lax.axis_index("row"), lax.axis_index("col")
    end_row = row == lax.axis_size("row") - 1
    end_col = col == lax.axis_size("col") - 1
    return lax.rem(row, 2) == 1, lax.rem(col, 2) == 1, end_row, end_col


def reorder(steps, sources, targets, spare):
    pairs = list(zip(sources, spare))
    for k, step in enumerate(steps):
        for (x, y), target in zip(pairs, targets):
            x, y = (y, x) if k % 2 else (x, y)
            y = target if k == len(steps) - 1 else y
            for r in range(0, x.shape[1], 8):
                for j, block in enumerate(step([x[j, r : r + 8, :] for j in range(x.shape[0])])):
                    if len(y.shape) == 2:
                        y[r : r + 8, j * 128 : j * 128 + 128] = block
                    else:
                        y[j, r : r + 8, :] = block


def fetch(sources, targets, sems):
    copies = [pltpu.make_async_copy(x, y, sems.at[k]) for k, (x, y) in enumerate(zip(sources, targets))]
    for copy in copies:
        copy.start()
    for copy in copies:
        copy.wait()


def edge_columns(inner, *refs):
    fields, (out, *held, sems) = refs[:6], refs[6:]
    n, width = fields[0].shape
    half = n // 2
    _, col_odd, end_row, _ = position()
    last = jnp.logical_not(col_odd) if inner else col_odd
    offset = pl.multiple_of(jnp.where(last, width - 128, 0), 128)
    row, lane = rows((8, 128)), lanes((8, 128))
    zero = F32(0.0)
    fetch([f.at[:, pl.ds(offset, 128)] for f in fields], held, sems)

    def to(x, target):
        return pltpu.roll(x, jnp.where(last, (target + SENT) % 128, target % 128), 1)

    def chunk(r, second):
        g_x, g_y, w_x, w_y, a, p = [f[r : r + 8, :] for f in held]
        if r == n - 8:
            w_y = jnp.where((row == 7) & end_row, zero, w_y)
        fx = w_x * g_x
        fy = w_y * g_y
        before = jnp.zeros((1, 128), F32) if r == 0 else held[3][r - 1 : r, :] * held[1][r - 1 : r, :]
        before_y = jnp.where(row == 0, jnp.broadcast_to(before, fy.shape), pltpu.roll(fy, 1, 0))
        src = to(a * p - fx + before_y - fy, 0)
        src = src + jnp.where((lane == 0) & jnp.logical_not(last), zero, to(fx, 1))
        flux = jnp.broadcast_to(fx[:, 127:128], fx.shape)
        right = jnp.where((lane == SENT) & last, flux, to(w_x, SENT))
        down = to(w_y, 2 * SENT)
        out[r : r + 8, :] = jnp.where(lane < SENT, src, jnp.where(lane < 2 * SENT, right, down))
        start = 80 if second else 16
        beyond = jnp.where((lane == start) & last, to(w_x, start + 1), zero)
        rest = jnp.where(lane < start, to(w_y, 32) if second else down, to(a, start) + beyond)
        return rest, fy[7:8, :]

    for r in range(0, half, 8):
        first, _ = chunk(r, False)
        second, tail = chunk(r + half, True)
        out[n + r : n + r + 8, :] = jnp.where(lane < HC, first, second)
    out[n + half :, :] = to(jnp.broadcast_to(tail, (8, 128)), 0)


def tile_fields(*refs):
    fields, (r_o, wx_o, wy_o, an_o, fx_o, fy_o, *held, raw, spare, tail, sems) = refs[:6], refs[6:]
    gx, gy, wx, wy, an, pr = held
    n, width = gx.shape
    form = layout(width // 128 + 1)
    fetch(fields, held, sems)
    _, _, end_row, end_col = position()
    row, lane = rows((8, width)), lanes((8, width))
    zero = F32(0.0)
    carry = jnp.zeros((1, width), F32)
    for r in range(0, n, 8):
        w_x = jnp.where((lane == width - 1) & end_col, zero, wx[r : r + 8, :])
        w_y = wy[r : r + 8, :]
        if r == n - 8:
            w_y = jnp.where((row == 7) & end_row, zero, w_y)
        fx = w_x * gx[r : r + 8, :]
        fy = w_y * gy[r : r + 8, :]
        a = an[r : r + 8, :]
        before_x = jnp.where(lane == 0, zero, roll_right(fx))
        before_y = jnp.where(row == 0, jnp.broadcast_to(carry, fy.shape), pltpu.roll(fy, 1, 0))
        carry = fy[7:8, :]
        src = a * pr[r : r + 8, :] + before_x - fx + before_y - fy
        for k, x in enumerate((src, w_x, w_y, a)):
            st(raw.at[k], r, x)
        fx_o[r : r + 8, :] = jnp.broadcast_to(fx[:, width - 1 : width], (8, 128))
    st(tail.at[0], 0, jnp.broadcast_to(carry, (8, width)))
    pick = lambda ref: [ref.at[k] for k in range(4)]
    reorder(form.steps_in, [*pick(raw), tail.at[0]], [r_o, wx_o, wy_o, an_o, fy_o], [*pick(spare), tail.at[1]])


def edge_rows(has_outer, r_t, wx_t, wy_t, an_t, fx_t, fy_t, *refs):
    inner, refs = refs[0], refs[1:]
    outer = None
    if has_outer:
        outer, refs = refs[0], refs[1:]
    r_o, wx_o, wy_o, an_o, fy_o, *rest = refs
    own, n, _ = r_t.shape
    form = layout(own + 1)
    row_odd, odd, _, _ = position()
    lane = lanes((8, 128))
    zero = F32(0.0)

    messages = [(inner, odd)] + ([(outer, jnp.logical_not(odd))] if has_outer else [])

    def placed(x, source, before):
        return pltpu.roll(x, jnp.where(before, (128 - SENT - source) % 128, -source % 128), 1)

    def within(x, before):
        start = jnp.where(before, 128 - SENT, 0)
        return jnp.where((lane >= start) & (lane < start + SENT), x, zero)

    def halo(m, before, r):
        half = n // 2
        main = m[r : r + 8, :]
        second = r >= half
        rest = m[n + r % half : n + r % half + 8, :]
        src = placed(main, 0, before)
        right = jnp.where(lane == 128 - SENT, zero, placed(main, SENT, before))
        if second:
            near = lane < jnp.where(before, 128 - SENT + 32, 32)
            down = jnp.where(near, placed(main, 2 * SENT, before), placed(rest, 32, before))
        else:
            down = placed(jnp.where(lane < 2 * SENT, rest, main), 2 * SENT, before)
        a = placed(rest, 80 if second else 16, before)
        flux = jnp.where(before, jnp.broadcast_to(main[:, SENT : SENT + 1], main.shape), zero)
        return [within(x, before) for x in (src, right, down, a)] + [flux]

    for r in range(0, n, 8):
        parts = [halo(m, before, r) for m, before in messages]
        src_h, wx_h, wy_h, an_h, incoming = [tree(list(x)) for x in zip(*parts)]
        src_h = jnp.where(lane == 0, src_h + fx_t[r : r + 8, :], src_h)
        for out, tile, h in ((r_o, r_t, src_h), (wx_o, wx_t, wx_h), (wy_o, wy_t, wy_h), (an_o, an_t, an_h)):
            top = GUARD if out is wy_o else 0
            for j in range(own):
                x = tile[j, r : r + 8, :]
                if out is r_o and j == 0:
                    x = jnp.where(lane == 0, x + incoming, x)
                out[j, top + r : top + r + 8, :] = x
            out[own, top + r : top + r + 8, :] = h
    st(wy_o, 0, jnp.zeros((GUARD, (own + 1) * 128), F32))
    for j in range(own):
        fy_o[j] = fy_t[j]
    tails = [within(placed(m[n + n // 2 :, :], 0, before), before) for m, before in messages]
    fy_o[own] = tree(tails)

    message(form, row_odd, r_o, wx_o, wy_o, an_o, fy_o, *rest)


def near_rows(r_i, wx_i, wy_i, an_i, fy_i, di, wl, *rest):
    form = layout(wx_i.shape[0])
    row_odd, _, _, _ = position()
    message(form, jnp.logical_not(row_odd), r_i, wx_i, wy_i, an_i, fy_i, *rest)
    for r in range(0, wx_i.shape[1], 8):
        w_x, w_y = ld(wx_i, r), ld(wy_i, GUARD + r)
        w_l = form.left(w_x)
        st(wl, r, w_l)
        diag = ld(an_i, r) + w_x + w_l + w_y + ld(wy_i, GUARD + r - 1)
        st(di, r, jnp.where(diag > F32(0.0), F32(1.0) / diag, F32(0.0)))


def message(form, bottom, r_o, wx_o, wy_o, an_o, fy_o, msg, g_o, cr_o, cd_o, ca_o, U, DI, V, WL, T, H, K):
    n = r_o.shape[1]
    zero = F32(0.0)
    G = GUARD

    def pick(low, high):
        return jnp.where(bottom, high, low)

    def align(x):
        return pl.multiple_of(x, 8)

    base = align(pick(0, n - 40))
    for r in range(0, 40, 8):
        at = align(base + r)
        w_x = ld(wx_o, at)
        w_l = form.left(w_x)
        st(WL, G + r, w_l)
        diag = ld(an_o, at) + w_x + w_l + ld(wy_o, align(at + G)) + ld(wy_o, base + (r + G - 1))
        inverse = jnp.where(diag > zero, F32(1.0) / diag, zero)
        st(DI, G + r, inverse)
        st(U, G + r, ld(r_o, at) * inverse)
    for source, image in ((U, T), (V, U)):
        for r in range(0, 40, 8):
            at = align(base + r)
            x = ld(source, G + r)
            beside = ld(WL, G + r) * (x - form.left(x)) + ld(wx_o, at) * (x - form.right(x))
            down = ld(wy_o, align(at + G)) * (x - ld(source, G + r + 1))
            up = ld(wy_o, base + (r + G - 1)) * (x - ld(source, G + r - 1))
            y = (ld(an_o, at) * x + beside) + (down + up)
            st(image, G + r, y)
            if image is T:
                st(V, G + r, ld(DI, G + r) * y)
    near = align(pick(0, 8))
    sums = form.total(four_rows(T, align(near + G), 8))
    sums_2 = form.total(four_rows(U, pick(0, 20) + G, 4))
    parts = {}

    def add(name, x):
        parts[name] = parts[name] + x if name in parts else x

    for k in range(4):
        at = base + (near + k)
        w_x = ld(wx_o, at, 8, 4)
        first, last = form.first_only(ld(WL, near + (G + k), 8, 4)), form.last_only(w_x)
        a = ld(an_o, at, 8, 4) + first + last
        inverse = ld(DI, near + (G + k), 8, 4)
        sides = []
        if k == 0:
            w = ld(wy_o, at + (G - 1), 8, 4)
            sides.append(("u", w))
            a = a + w
        if k == 3:
            w = ld(wy_o, at + G, 8, 4)
            sides.append(("d", w))
            a = a + w
        weighted = inverse * a
        add("aa", weighted * a)
        for name, w in (("l", first), ("r", last)):
            add("a" + name, weighted * w)
            scaled = inverse * w
            add(name + name, scaled * w)
            for other, v in sides:
                add(name + other, scaled * v)
        for name, w in sides:
            add("a" + name, weighted * w)
            add(name + name, inverse * w * w)
    parts = {name: form.total(x) for name, x in parts.items()}
    for k, name in enumerate(("uu", "dd", "au", "ru", "lu")):
        st(H.at[k], G, parts[name])
    uu, au, ru, lu = [ld(H.at[k], G + 1) for k in (0, 2, 3, 4)]
    dd = ld(H.at[1], G - 1)
    centre = parts["aa"] + form.coarse_right(parts["ll"]) + form.coarse_left(parts["rr"]) + uu + dd
    east = -(parts["ar"] + form.coarse_right(parts["al"]))
    south = -(parts["ad"] + au)
    south_east = form.coarse_right(parts["ld"]) + ru
    south_west = form.coarse_left(parts["rd"]) + lu
    for k, x in enumerate((centre, east, south, south_east, south_west)):
        st(K.at[k], 0, x)

    c = align(pick(0, n - 4 * FAR))
    coarse = (
        form.total(four_rows(r_o, c, FAR)),
        form.last_column(four_rows(wx_o, c, FAR)),
        form.total(ld(wy_o, c + (G + 3), FAR, 4)),
        form.total(four_rows(an_o, c, FAR)),
    )
    for out, x in zip((g_o, cr_o, cd_o, ca_o), coarse):
        st(out, 0, x)
    start = align(pick(0, n - HR))
    for k, (ref, top) in enumerate(((r_o, 0), (wx_o, 0), (wy_o, G), (an_o, 0))):
        st(msg, k * HR, ld(ref, align(start + top), HR))
    outer, inner = pick(HR - 1, 0), pick(HR - 2, 1)
    st(msg, outer, form.pack(*[sums[k : k + 1] for k in range(4)]))
    st(msg, inner, form.pack(*[sums[k : k + 1] for k in range(4, 8)]))
    st(msg, HR + outer, form.spread(form.total(ld(wy_o, n - 4 * FAR - 1 + G, 1))))
    st(msg, HR + inner, form.pack(*[sums_2[k : k + 1] for k in range(4)]))
    st(msg, 3 * HR + outer, ld(fy_o, 0, 1))
    packed = form.pack(*coarse)
    st(msg, 4 * HR, jnp.where(bottom, packed[: FAR - 1], packed[1:]))
    for k in range(5):
        four = [ld(K.at[k], pick(0, 3) + i, 1) for i in range(4)]
        st(msg, 4 * HR + FAR - 1 + k, form.pack(*four))


def apply_a(form, v, w_l, w_r, w_y, an, r):
    x = ld(v, r)
    down = ld(w_y, r) * (x - ld(v, r + 1))
    up = ld(w_y, r - 1) * (x - ld(v, r - 1))
    beside = w_l.chunk(r) * (x - form.left(x)) + w_r.chunk(r) * (x - form.right(x))
    return (an.chunk(r) * x + beside) + (down + up)


def basis(r_i, wx_i, wy_i, an_i, fy_i, g_a, cr_a, cd_a, ca_a, di_i, wl_i, g_b, cr_b, cd_b, ca_b, msg_in, msg_out, mom, p0, p1, p2, q0, q1, q2, r0,
         ENDS, WY, PA, PB, QA, C_L, C_R, C_D, C_A, C_I, EA, EB, GC, KF, KV):
    blocks, n, _ = r_i.shape
    form = layout(blocks)
    fine = n + 2 * HR
    coarse = n // 4 + 2 * FAR
    zero = F32(0.0)
    odd, _, _, _ = position()
    own_blocks = blocks - 1
    B = GUARD

    def sides(a, b):
        x, y = ld(msg_in, a, b - a), ld(msg_out, a, b - a)
        return jnp.where(odd, x, y), jnp.where(odd, y, x)

    zeros = jnp.zeros((B, blocks * 128), F32)
    coarse_zeros = jnp.zeros((B, form.coarse_blocks * 128), F32)
    R, WX, AN, DI, WL = [Rows(own, ENDS.at[k]) for k, own in enumerate((r_i, wx_i, an_i, di_i, wl_i))]
    for ref in (WY, PA, PB):
        st(ref, 0, zeros)
        st(ref, B + fine, zeros)
    for k, ends in ((0, ENDS.at[0]), (1, ENDS.at[1]), (3, ENDS.at[2])):
        for end, x in enumerate(sides(k * HR, (k + 1) * HR)):
            st(ends.at[end], 0, x)
    up, down = sides(2 * HR, 3 * HR)
    st(WY, B, up)
    st(WY, B + HR + n, down)
    for r in range(0, n, 8):
        st(WY, B + HR + r, ld(wy_i, GUARD + r))
    flux_up, _ = sides(3 * HR, 3 * HR + 1)
    first_rows = ld(r_i, 0) + jnp.where(rows(zeros.shape) == 0, jnp.broadcast_to(flux_up, zeros.shape), zero)
    below = ENDS.at[0, 1]
    st(below, 0, ld(below, 0, 1) + ld(fy_i, 0, 1))

    for end in (0, 1):
        st(ENDS.at[4, end], 0, form.left(ld(ENDS.at[1, end], 0)))

    def inverse(r):
        diag = AN.chunk(r) + WX.chunk(r) + WL.chunk(r) + ld(WY, r) + ld(WY, r - 1)
        return jnp.where(diag > zero, F32(1.0) / diag, zero)

    st(ENDS.at[3, 0], 0, inverse(B))
    st(ENDS.at[3, 1], 0, inverse(B + HR + n))
    first_inverse = inverse(B + HR)

    def read(field, r, first):
        return first if r == B + HR else field.chunk(r)

    for ref in (EA, EB, C_D):
        st(ref, 0, coarse_zeros)
        st(ref, B + coarse, coarse_zeros)
    up, down = sides(4 * HR, 4 * HR + FAR - 1)
    for k, (ref, a, b) in enumerate(((GC, g_a, g_b), (C_R, cr_a, cr_b), (C_D, cd_a, cd_b), (C_A, ca_a, ca_b))):
        st(ref, B, form.unpack(up, k))
        st(ref, B + coarse - FAR + 1, form.unpack(down, k))
        x, y = ld(a, 0, FAR), ld(b, 0, FAR)
        st(ref, B + FAR, jnp.where(odd, y, x))
        st(ref, B + 2 * FAR, jnp.where(odd, x, y))
    st(GC, B + FAR, ld(GC, B + FAR, 1) + form.total(flux_up))
    beyond, _ = sides(HR, HR + 1)
    st(C_D, B - 1, form.take(beyond))
    for c in (FAR - 1, coarse - FAR):
        f = B + 4 * c - 40
        end, at = (0, 4) if c < FAR else (1, 0)
        st(GC, B + c, form.total(four_rows(ENDS.at[0, end], at, 1)))
        st(C_R, B + c, form.last_column(four_rows(ENDS.at[1, end], at, 1)))
        st(C_D, B + c, form.total(ld(WY, f + 3, 1)))
        st(C_A, B + c, form.total(four_rows(ENDS.at[2, end], at, 1)))
    for c in range(B, B + coarse, 8):
        c_r = ld(C_R, c)
        c_l = form.coarse_left(c_r)
        total = ld(C_A, c) + c_l + c_r + ld(C_D, c - 1) + ld(C_D, c)
        st(C_L, c, c_l)
        inverse_c = jnp.where(total > zero, F32(DAMP) / total, zero)
        st(C_I, c, inverse_c)
        st(EA, c, inverse_c * ld(GC, c))

    def set_sums(c, g):
        st(GC, B + c, g)
        st(EA, B + c, ld(C_I, B + c, g.shape[0]) * g)

    def smooth(lo, hi):
        if lo > 0:
            st(EA, B + lo - 8, coarse_zeros)
            st(EB, B + lo - 8, coarse_zeros)
        if hi < coarse:
            st(EA, B + hi, coarse_zeros)
            st(EB, B + hi, coarse_zeros)
        old, new = EA, EB
        for turn in range(3):
            for c in range(B + lo, B + hi, 8):
                e = ld(old, c)
                beside = ld(C_L, c) * form.coarse_left(e) + ld(C_R, c) * form.coarse_right(e)
                beside = beside + (ld(C_D, c - 1) * ld(old, c - 1) + ld(C_D, c) * ld(old, c + 1))
                st(new, c, F32(1.0 - DAMP) * e + ld(C_I, c) * (ld(GC, c) + beside))
            old, new = new, old

    def coarse_part(r):
        at = B + 10 + (r - B) // 4
        shape = (8, form.coarse_blocks * 128)
        a, b = [jnp.broadcast_to(ld(EB, at + k, 1), shape) for k in (0, 1)]
        return form.spread(jnp.where(rows(shape) < 4, a, b))

    def direct(p, residual, before):
        for r in range(B, B + fine, 8):
            x = read(DI, r, first_inverse) * residual(r) + coarse_part(r)
            if before is not None:
                x = x - F32(SHIFT) * ld(before, r)
            st(p, r, x)

    def image_of(p, p_out, q_out):
        for r in range(B, B + fine, 8):
            q = apply_a(form, p, WL, WX, WY, AN, r)
            st(QA, r, q)
            at = r - B - HR
            if 0 <= at < n:
                for k in range(own_blocks):
                    p_out[k, at : at + 8, :] = p[k, r : r + 8, :]
                    q_out[k, at : at + 8, :] = q[:, k * 128 : k * 128 + 128]

    def restrict(q):
        for c in range(FAR - 1, coarse - FAR + 1, 8):
            count = min(8, coarse - FAR + 1 - c)
            set_sums(c, form.total(four_rows(q, B + 4 * c - 40, count)))

    def coarse_image(c, count):
        e = ld(EB, B + c, count)
        c_l, c_r = ld(C_L, B + c, count), ld(C_R, B + c, count)
        image = ld(C_A, B + c, count) * e + c_l * (e - form.coarse_left(e)) + c_r * (e - form.coarse_right(e))
        image = image + ld(C_D, B + c - 1, count) * (e - ld(EB, B + c - 1, count))
        return image + ld(C_D, B + c, count) * (e - ld(EB, B + c + 1, count))

    def stretch(a, b):
        shape = (8, a.shape[1])
        return form.unpack_rows(jnp.where(rows(shape) < 4, jnp.broadcast_to(a, shape), jnp.broadcast_to(b, shape)))

    def second_sums(side, c, sums):
        for k in range(5):
            at = 4 * HR + FAR - 1 + k
            row = sides(at, at + 1)[side]
            st(KF.at[k], 8, form.unpack_rows(jnp.broadcast_to(row, (4, row.shape[1]))))
        centre, east, south, south_east, south_west = [ld(KF.at[k], 8, 4) for k in range(5)]
        north, north_west, north_east = [ld(KF.at[k], 7, 4) for k in (2, 3, 4)]
        e, below, above = [ld(EB, B + c + d, 4) for d in (0, 1, -1)]
        image = centre * e + east * form.coarse_right(e) + form.coarse_left(east * e)
        image = image + south * below + north * above
        image = image + south_east * form.coarse_right(below) + form.coarse_left(north_west * above)
        image = image + south_west * form.coarse_left(below) + form.coarse_right(north_east * above)
        st(KV.at[side], 0, image + form.unpack_rows(jnp.broadcast_to(sums, (4, sums.shape[1]))))

    smooth(0, coarse)
    direct(PA, lambda r: read(R, r, first_rows), None)
    image_of(PA, p0, q0)
    for r in range(0, n, 8):
        for k in range(own_blocks):
            r0[k, r : r + 8, :] = first_rows[:, k * 128 : k * 128 + 128] if r == 0 else r_i[k, r : r + 8, :]
    restrict(QA)
    far_up, _ = sides(0, 1)
    near_up, _ = sides(1, 2)
    _, near_down = sides(HR - 1, HR)
    _, far_down = sides(HR - 2, HR - 1)
    up = stretch(far_up, near_up)
    down = stretch(near_down, far_down)
    image = coarse_image(0, FAR - 1)
    set_sums(0, image[0:4])
    set_sums(4, image[4:] + up[0 : FAR - 5])
    image = coarse_image(coarse - FAR + 1, FAR - 1)
    set_sums(coarse - FAR + 1, image[0:7] + down[1:])
    set_sums(coarse - 4, image[7:])
    second_sums(0, 7, sides(HR + 1, HR + 2)[0])
    second_sums(1, coarse - FAR, sides(2 * HR - 2, 2 * HR - 1)[1])
    smooth(0, coarse)
    direct(PB, lambda r: ld(QA, r), PA)
    image_of(PB, p1, q1)
    restrict(QA)
    for c, side, first in ((8, 0, 1), (coarse - FAR + 1, 1, 1)):
        image = coarse_image(c, 3) + ld(KV.at[side], first, 3)
        set_sums(c, image - F32(SHIFT) * ld(GC, B + c, 3))
    smooth(8, coarse - 8)
    direct(PA, lambda r: ld(QA, r), PB)
    acc = [jnp.zeros((8, 128), F32) for _ in range(9)]
    for r in range(0, n, 8):
        f = B + HR + r
        image = apply_a(form, PA, WL, WX, WY, AN, f)
        sums = [[] for _ in acc]
        for j in range(own_blocks):
            z2, i2 = PA[j, f : f + 8, :], image[:, j * 128 : (j + 1) * 128]
            p2[j, r : r + 8, :] = z2
            q2[j, r : r + 8, :] = i2
            z0, z1, i0, i1, res = [x[j, r : r + 8, :] for x in (p0, p1, q0, q1, r0)]
            pairs = ((z0, i0), (z1, i0), (z1, i1), (z2, i0), (z2, i1), (z2, i2), (z0, res), (z1, res), (z2, res))
            for k, (x, y) in enumerate(pairs):
                sums[k].append(x * y)
        for k, parts in enumerate(sums):
            acc[k] = acc[k] + tree(parts)
    lane = lanes((8, 128))
    line = jnp.zeros((8, 128), F32)
    for k in range(9):
        total = jnp.sum(jnp.sum(acc[k], axis=0, keepdims=True), axis=1, keepdims=True)
        line = jnp.where(lane == k, jnp.broadcast_to(total, (8, 128)), line)
    for j in range(mom.shape[0]):
        mom[j] = line[0:1]


def combine(mom, p0, p1, p2, q0, q1, q2, r0, heights, residual, work):
    blocks, n, _ = p0.shape
    form = layout(blocks + 1)
    tot = jnp.broadcast_to(tree([mom[j] for j in range(mom.shape[0])]), (8, 128))
    m = [jnp.broadcast_to(tot[:, k : k + 1], (8, 128)) for k in range(9)]
    g00, g10, g11, g20, g21, g22, b0, b1, b2 = m
    l10, l20 = g10 / g00, g20 / g00
    d1 = g11 - l10 * g10
    t21 = g21 - l20 * g10
    l21 = t21 / d1
    d2 = g22 - l20 * g20 - l21 * t21
    y1 = b1 - l10 * b0
    y2 = b2 - l20 * b0 - l21 * y1
    x2 = y2 / d2
    x1 = y1 / d1 - l21 * x2
    x0 = b0 / g00 - l10 * x1 - l20 * x2
    sums, spare = [[work.at[k], work.at[k + 1]] for k in (0, 2)]
    for r in range(0, n, 8):
        for j in range(blocks):
            z0, z1, z2, i0, i1, i2, res = [x[j, r : r + 8, :] for x in (p0, p1, p2, q0, q1, q2, r0)]
            sums[0][j, r : r + 8, :] = x0 * z0 + x1 * z1 + x2 * z2
            sums[1][j, r : r + 8, :] = res - (x0 * i0 + x1 * i1 + x2 * i2)
    reorder(form.steps_out, sums, [heights, residual], spare)


def swap(x, axis, size, inner):
    if inner:
        pairs = [(i, i ^ 1) for i in range(size) if i ^ 1 < size]
    else:
        pairs = [(i, j) for i in range(size) for j in [((i + 1) ^ 1) - 1] if 0 <= j < size]
    return lax.ppermute(x, axis, pairs)


def local(nrow, ncol, gx, gy, wx, wy, an, pr):
    n, width = gx.shape
    ext = width + 2 * HC
    fields = tuple(pltpu.with_memory_space_constraint(f, pltpu.HBM) for f in (gx, gy, wx, wy, an, pr))
    nb = ext // 128
    shape = lambda *dims: jax.ShapeDtypeStruct(dims, F32)
    params = pltpu.CompilerParams(vmem_limit_bytes=48 * 1024 * 1024)

    def call(kernel, name, args, outs, scratch=(), us=1, fetches=0):
        sems = [pltpu.SemaphoreType.DMA((fetches,))] if fetches else []
        return pl.pallas_call(
            kernel,
            in_specs=[HBM if fetches else VMEM] * len(args),
            out_specs=[VMEM] * len(outs),
            out_shape=outs,
            scratch_shapes=[pltpu.VMEM(dims, F32) for dims in scratch] + sems,
            compiler_params=params,
            cost_estimate=pl.CostEstimate(flops=us * 2_000_000, bytes_accessed=us * 2_000_000, transcendentals=0),
            name=name,
        )(*args)

    halos = []
    for inner in (True, False) if ncol > 2 else (True,):
        (edge,) = call(functools.partial(edge_columns, inner), "edge_columns", fields, [shape(n + n // 2 + 8, 128)], [(n, 128)] * 6, 1, 6)
        halos.append(swap(edge, "col", ncol, inner))
    tile = shape(nb - 1, n, 128)
    own = call(tile_fields, "tile_fields", fields, [tile] * 4 + [shape(n, 128), shape(nb - 1, 8, 128)], [(n, width)] * 6 + [(4, nb - 1, n, 128)] * 2 + [(2, nb - 1, 8, 128)], 1, 6)
    cb = layout(nb).coarse_blocks
    far = shape(cb, FAR, 128)
    msg = shape(nb, DEPTH, 128)
    field = shape(nb, n, 128)
    work = [(nb, 40 + 2 * GUARD, 128)] * 5 + [(5, cb, 24, 128), (5, cb, 8, 128)]
    *fields, to_out, g_a, cr_a, cd_a, ca_a = call(
        functools.partial(edge_rows, len(halos) > 1),
        "edge_rows",
        (*own, *halos),
        [field, field, shape(nb, GUARD + n, 128), field, shape(nb, 8, 128), msg] + [far] * 4,
        work,
    )
    from_out = swap(to_out, "row", nrow, False)
    di, wl, to_in, *far_b = call(near_rows, "near_rows", fields, [field, field, msg] + [far] * 4, work)
    from_in = swap(to_in, "row", nrow, True)
    fine = n + 2 * HR
    coarse = n // 4 + 2 * FAR
    mom, *vectors = call(
        basis,
        "basis",
        (*fields, g_a, cr_a, cd_a, ca_a, di, wl, *far_b, from_in, from_out),
        [shape(nrow * ncol, 1, 128)] + [tile] * 7,
        [(5, 2, nb, HR, 128)] + [(nb, fine + 2 * GUARD, 128)] * 4 + [(cb, coarse + 2 * GUARD, 128)] * 8 + [(5, cb, 16, 128), (2, cb, 8, 128)],
    )
    mom = lax.all_to_all(mom, ("row", "col"), 0, 0, tiled=True)
    out = shape(n, width)
    return tuple(call(combine, "combine", (mom, *vectors), [out, out], [(4, nb - 1, n, 128)]))


def solution(mesh):
    spec = P("row", "col")
    return jax.shard_map(
        functools.partial(local, mesh.shape["row"], mesh.shape["col"]),
        mesh=mesh,
        in_specs=(spec,) * 6,
        out_specs=(spec, spec),
        check_vma=False,
    )
```

```python
import functools

import jax
import jax.numpy as jnp
from jax import lax
from jax.experimental import pallas as pl
from jax.experimental.pallas import tpu as pltpu
from jax.sharding import PartitionSpec as P

DAMP = 2.0 / 3.0
SHIFT = 1.0
HC = 64
SENT = 48
HR = 8
FAR = 12
DEPTH = 4 * HR + FAR - 1 + 5
GUARD = 8
VMEM = pl.BlockSpec(memory_space=pltpu.VMEM)
HBM = pl.BlockSpec(memory_space=pltpu.HBM)
F32 = jnp.float32


def lanes(shape):
    return lax.broadcasted_iota(jnp.int32, shape, 1)


def rows(shape):
    return lax.broadcasted_iota(jnp.int32, shape, 0)


def roll_right(x, k=1):
    return pltpu.roll(x, k, 1)


def roll_left(x, k=1):
    return pltpu.roll(x, x.shape[1] - k, 1)


def group_sum(x):
    four = lanes(x.shape) % 4
    one = jnp.where(four < 3, roll_left(x), roll_right(x, 3))
    two = jnp.where(four < 2, roll_left(x, 2), roll_right(x, 2))
    three = jnp.where(four < 1, roll_left(x, 3), roll_right(x))
    return (x + two) + (one + three)


def split(x):
    return [x[:, j : j + 128] for j in range(0, x.shape[1], 128)]


def join(parts):
    return jnp.concatenate(parts, axis=1)


class Wide:
    def __init__(self, width):
        self.coarse_blocks = width // 128 + 1

    left, right = staticmethod(roll_right), staticmethod(roll_left)
    total = staticmethod(group_sum)
    spread = take = staticmethod(lambda x: x)
    steps_in = steps_out = (lambda parts: parts,)

    def coarse_left(self, e):
        return roll_right(e, 4)

    def coarse_right(self, e):
        return roll_left(e, 4)

    def last_column(self, x):
        return group_sum(jnp.where(lanes(x.shape) % 4 == 3, x, F32(0.0)))

    def pack(self, a, b, c, d):
        four = lanes(a.shape) % 4
        return jnp.where(four < 2, jnp.where(four == 0, a, b), jnp.where(four == 2, c, d))

    def unpack(self, m, k):
        return group_sum(jnp.where(lanes(m.shape) % 4 == k, m, F32(0.0)))

    def unpack_rows(self, m):
        return group_sum(jnp.where(lanes(m.shape) % 4 == rows(m.shape) % 4, m, F32(0.0)))

    def at_sides(self, w_l, d_l, w_r, d_r):
        return self.first_only(w_l * d_l) + self.last_only(w_r * d_r)

    def first_only(self, x):
        return jnp.where(lanes(x.shape) % 4 == 0, x, F32(0.0))

    def last_only(self, x):
        return jnp.where(lanes(x.shape) % 4 == 3, x, F32(0.0))


class Planes:
    coarse_blocks = 2

    def left(self, x):
        a, b, c, d, h = split(x)
        first = lanes(h.shape) == 0
        d, h = roll_right(d), roll_right(h)
        return join([jnp.where(first, h, d), a, b, c, jnp.where(first, d, h)])

    def right(self, x):
        a, b, c, d, h = split(x)
        last = lanes(h.shape) == 127
        a, h = roll_left(a), roll_left(h)
        return join([b, c, d, jnp.where(last, h, a), jnp.where(last, a, h)])

    def coarse_left(self, e):
        o, h = split(e)
        lane = lanes(h.shape)
        end = jnp.broadcast_to(o[:, 127:128], h.shape)
        return join([jnp.where(lane == 0, roll_right(h), roll_right(o)), jnp.where(lane < 4, end, roll_right(h, 4))])

    def coarse_right(self, e):
        o, h = split(e)
        lane = lanes(h.shape)
        end = jnp.broadcast_to(o[:, 0:1], h.shape)
        return join([jnp.where(lane == 127, roll_left(h), roll_left(o)), jnp.where(lane >= 124, end, roll_left(h, 4))])

    def total(self, x):
        a, b, c, d, h = split(x)
        return join([(a + b) + (c + d), group_sum(h)])

    def last_column(self, x):
        h = x[:, 512:640]
        return join([x[:, 384:512], group_sum(jnp.where(lanes(h.shape) % 4 == 3, h, F32(0.0)))])

    def spread(self, e):
        o, h = split(e)
        return join([o, o, o, o, h])

    def take(self, x):
        return join([x[:, 0:128], x[:, 512:640]])

    def pack(self, *fields):
        own, halo = zip(*[split(f) for f in fields])
        a, b, c, d = halo
        four = lanes(a.shape) % 4
        mixed = jnp.where(four < 2, jnp.where(four == 0, a, b), jnp.where(four == 2, c, d))
        return join([*own, mixed])

    def unpack(self, m, k):
        h = m[:, 512:640]
        return join([m[:, k * 128 : k * 128 + 128], group_sum(jnp.where(lanes(h.shape) % 4 == k, h, F32(0.0)))])

    def unpack_rows(self, m):
        a, b, c, d, h = split(m)
        key = rows(h.shape) % 4
        own = jnp.where(key < 2, jnp.where(key == 0, a, b), jnp.where(key == 2, c, d))
        return join([own, group_sum(jnp.where(lanes(h.shape) % 4 == key, h, F32(0.0)))])

    def at_sides(self, w_l, d_l, w_r, d_r):
        w_l, d_l, w_r, d_r = split(w_l), split(d_l), split(w_r), split(d_r)
        four = lanes(d_l[1].shape) % 4
        none = jnp.zeros_like(d_l[1])
        halo = jnp.where(four == 0, w_l[4] * d_l[1], jnp.where(four == 3, w_r[4] * d_r[1], none))
        return join([w_l[0] * d_l[0], none, none, w_r[3] * d_r[0], halo])

    def first_only(self, x):
        a, _, _, _, h = split(x)
        none = jnp.zeros_like(h)
        return join([a, none, none, none, jnp.where(lanes(h.shape) % 4 == 0, h, none)])

    def last_only(self, x):
        _, _, _, d, h = split(x)
        none = jnp.zeros_like(h)
        return join([none, none, none, d, jnp.where(lanes(h.shape) % 4 == 3, h, none)])

    def gather_in(self, parts):
        lane = lanes(parts[0].shape)
        index = (lane % 32) * 4 + lane // 32
        return [jnp.take_along_axis(p, index, axis=1) for p in parts]

    def gather_out(self, parts):
        lane = lanes(parts[0].shape)
        index = (lane % 4) * 32 + lane // 4
        return [jnp.take_along_axis(p, index, axis=1) for p in parts]

    def swap_halves(self, parts):
        a, b, c, d = parts
        low = lanes(a.shape) < 64
        return [
            jnp.where(low, a, roll_right(c, 64)),
            jnp.where(low, b, roll_right(d, 64)),
            jnp.where(low, roll_right(a, 64), c),
            jnp.where(low, roll_right(b, 64), d),
        ]

    def swap_quarters(self, parts):
        a, b, c, d = parts
        low = lanes(a.shape) % 64 < 32
        return [
            jnp.where(low, a, roll_right(b, 32)),
            jnp.where(low, roll_left(a, 32), b),
            jnp.where(low, c, roll_right(d, 32)),
            jnp.where(low, roll_left(c, 32), d),
        ]

    @property
    def steps_in(self):
        return self.gather_in, self.swap_halves, self.swap_quarters

    @property
    def steps_out(self):
        return self.swap_halves, self.swap_quarters, self.gather_out


class Rows:
    def __init__(self, own, ends):
        self.own, self.ends = own, ends

    def chunk(self, start):
        start -= GUARD + HR
        if 0 <= start < self.own.shape[1]:
            return ld(self.own, start)
        return ld(self.ends.at[int(start >= 0)], 0)


def layout(blocks):
    return Planes() if blocks == 5 else Wide(128 * (blocks - 1))


def ld(ref, start, count=8, step=1):
    rows_of = pl.ds(start, count, stride=step) if step > 1 else pl.ds(start, count)
    return jnp.concatenate([ref[j, rows_of, :] for j in range(ref.shape[0])], axis=1)


def st(ref, start, value, step=1):
    count = value.shape[0]
    rows_of = pl.ds(start, count, stride=step) if step > 1 else pl.ds(start, count)
    for j in range(ref.shape[0]):
        ref[j, rows_of, :] = value[:, j * 128 : (j + 1) * 128]


def tree(parts):
    while len(parts) > 1:
        parts = [sum(parts[j + 1 : j + 2], parts[j]) for j in range(0, len(parts), 2)]
    return parts[0]


def four_rows(ref, start, count):
    parts = [ld(ref, start + k, count, 4) for k in range(4)]
    return (parts[0] + parts[1]) + (parts[2] + parts[3])


def position():
    row, col = lax.axis_index("row"), lax.axis_index("col")
    end_row = row == lax.axis_size("row") - 1
    end_col = col == lax.axis_size("col") - 1
    return lax.rem(row, 2) == 1, lax.rem(col, 2) == 1, end_row, end_col


def reorder(steps, sources, targets, spare):
    pairs = list(zip(sources, spare))
    for k, step in enumerate(steps):
        for (x, y), target in zip(pairs, targets):
            x, y = (y, x) if k % 2 else (x, y)
            y = target if k == len(steps) - 1 else y
            for r in range(0, x.shape[1], 8):
                for j, block in enumerate(step([x[j, r : r + 8, :] for j in range(x.shape[0])])):
                    if len(y.shape) == 2:
                        y[r : r + 8, j * 128 : j * 128 + 128] = block
                    else:
                        y[j, r : r + 8, :] = block


def fetch(sources, targets, sems):
    copies = [pltpu.make_async_copy(x, y, sems.at[k]) for k, (x, y) in enumerate(zip(sources, targets))]
    for copy in copies:
        copy.start()
    for copy in copies:
        copy.wait()


def edge_columns(inner, *refs):
    fields, (out, *held, sems) = refs[:6], refs[6:]
    n, width = fields[0].shape
    half = n // 2
    _, col_odd, end_row, _ = position()
    last = jnp.logical_not(col_odd) if inner else col_odd
    offset = pl.multiple_of(jnp.where(last, width - 128, 0), 128)
    row, lane = rows((8, 128)), lanes((8, 128))
    zero = F32(0.0)
    fetch([f.at[:, pl.ds(offset, 128)] for f in fields], held, sems)

    def to(x, target):
        return pltpu.roll(x, jnp.where(last, (target + SENT) % 128, target % 128), 1)

    def chunk(r, second):
        g_x, g_y, w_x, w_y, a, p = [f[r : r + 8, :] for f in held]
        if r == n - 8:
            w_y = jnp.where((row == 7) & end_row, zero, w_y)
        fx = w_x * g_x
        fy = w_y * g_y
        before = jnp.zeros((1, 128), F32) if r == 0 else held[3][r - 1 : r, :] * held[1][r - 1 : r, :]
        before_y = jnp.where(row == 0, jnp.broadcast_to(before, fy.shape), pltpu.roll(fy, 1, 0))
        src = to(a * p - fx + before_y - fy, 0)
        src = src + jnp.where((lane == 0) & jnp.logical_not(last), zero, to(fx, 1))
        flux = jnp.broadcast_to(fx[:, 127:128], fx.shape)
        right = jnp.where((lane == SENT) & last, flux, to(w_x, SENT))
        down = to(w_y, 2 * SENT)
        out[r : r + 8, :] = jnp.where(lane < SENT, src, jnp.where(lane < 2 * SENT, right, down))
        start = 80 if second else 16
        beyond = jnp.where((lane == start) & last, to(w_x, start + 1), zero)
        rest = jnp.where(lane < start, to(w_y, 32) if second else down, to(a, start) + beyond)
        return rest, fy[7:8, :]

    for r in range(0, half, 8):
        first, _ = chunk(r, False)
        second, tail = chunk(r + half, True)
        out[n + r : n + r + 8, :] = jnp.where(lane < HC, first, second)
    out[n + half :, :] = to(jnp.broadcast_to(tail, (8, 128)), 0)


def tile_fields(*refs):
    fields, (r_o, wx_o, wy_o, an_o, fx_o, fy_o, *held, raw, spare, tail, sems) = refs[:6], refs[6:]
    gx, gy, wx, wy, an, pr = held
    n, width = gx.shape
    form = layout(width // 128 + 1)
    fetch(fields, held, sems)
    _, _, end_row, end_col = position()
    row, lane = rows((8, width)), lanes((8, width))
    zero = F32(0.0)
    carry = jnp.zeros((1, width), F32)
    for r in range(0, n, 8):
        w_x = jnp.where((lane == width - 1) & end_col, zero, wx[r : r + 8, :])
        w_y = wy[r : r + 8, :]
        if r == n - 8:
            w_y = jnp.where((row == 7) & end_row, zero, w_y)
        fx = w_x * gx[r : r + 8, :]
        fy = w_y * gy[r : r + 8, :]
        a = an[r : r + 8, :]
        before_x = jnp.where(lane == 0, zero, roll_right(fx))
        before_y = jnp.where(row == 0, jnp.broadcast_to(carry, fy.shape), pltpu.roll(fy, 1, 0))
        carry = fy[7:8, :]
        src = a * pr[r : r + 8, :] + before_x - fx + before_y - fy
        for k, x in enumerate((src, w_x, w_y, a)):
            st(raw.at[k], r, x)
        fx_o[r : r + 8, :] = jnp.broadcast_to(fx[:, width - 1 : width], (8, 128))
    st(tail.at[0], 0, jnp.broadcast_to(carry, (8, width)))
    pick = lambda ref: [ref.at[k] for k in range(4)]
    reorder(form.steps_in, [*pick(raw), tail.at[0]], [r_o, wx_o, wy_o, an_o, fy_o], [*pick(spare), tail.at[1]])


def edge_rows(has_outer, r_t, wx_t, wy_t, an_t, fx_t, fy_t, *refs):
    inner, refs = refs[0], refs[1:]
    outer = None
    if has_outer:
        outer, refs = refs[0], refs[1:]
    r_o, wx_o, wy_o, an_o, fy_o, *rest = refs
    own, n, _ = r_t.shape
    form = layout(own + 1)
    row_odd, odd, _, _ = position()
    lane = lanes((8, 128))
    zero = F32(0.0)

    messages = [(inner, odd)] + ([(outer, jnp.logical_not(odd))] if has_outer else [])

    def placed(x, source, before):
        return pltpu.roll(x, jnp.where(before, (128 - SENT - source) % 128, -source % 128), 1)

    def within(x, before):
        start = jnp.where(before, 128 - SENT, 0)
        return jnp.where((lane >= start) & (lane < start + SENT), x, zero)

    def halo(m, before, r):
        half = n // 2
        main = m[r : r + 8, :]
        second = r >= half
        rest = m[n + r % half : n + r % half + 8, :]
        src = placed(main, 0, before)
        right = jnp.where(lane == 128 - SENT, zero, placed(main, SENT, before))
        if second:
            near = lane < jnp.where(before, 128 - SENT + 32, 32)
            down = jnp.where(near, placed(main, 2 * SENT, before), placed(rest, 32, before))
        else:
            down = placed(jnp.where(lane < 2 * SENT, rest, main), 2 * SENT, before)
        a = placed(rest, 80 if second else 16, before)
        flux = jnp.where(before, jnp.broadcast_to(main[:, SENT : SENT + 1], main.shape), zero)
        return [within(x, before) for x in (src, right, down, a)] + [flux]

    for r in range(0, n, 8):
        parts = [halo(m, before, r) for m, before in messages]
        src_h, wx_h, wy_h, an_h, incoming = [tree(list(x)) for x in zip(*parts)]
        src_h = jnp.where(lane == 0, src_h + fx_t[r : r + 8, :], src_h)
        for out, tile, h in ((r_o, r_t, src_h), (wx_o, wx_t, wx_h), (wy_o, wy_t, wy_h), (an_o, an_t, an_h)):
            top = GUARD if out is wy_o else 0
            for j in range(own):
                x = tile[j, r : r + 8, :]
                if out is r_o and j == 0:
                    x = jnp.where(lane == 0, x + incoming, x)
                out[j, top + r : top + r + 8, :] = x
            out[own, top + r : top + r + 8, :] = h
    st(wy_o, 0, jnp.zeros((GUARD, (own + 1) * 128), F32))
    for j in range(own):
        fy_o[j] = fy_t[j]
    tails = [within(placed(m[n + n // 2 :, :], 0, before), before) for m, before in messages]
    fy_o[own] = tree(tails)

    message(form, row_odd, r_o, wx_o, wy_o, an_o, fy_o, *rest)


def near_rows(r_i, wx_i, wy_i, an_i, fy_i, di, wl, t_o, s_o, *rest):
    form = layout(wx_i.shape[0])
    row_odd, _, _, _ = position()
    *rest, U = rest
    message(form, jnp.logical_not(row_odd), r_i, wx_i, wy_i, an_i, fy_i, *rest)
    n, G = wx_i.shape[1], GUARD
    for r in range(0, wx_i.shape[1], 8):
        w_x, w_y = ld(wx_i, r), ld(wy_i, GUARD + r)
        w_l = form.left(w_x)
        st(wl, r, w_l)
        diag = ld(an_i, r) + w_x + w_l + w_y + ld(wy_i, GUARD + r - 1)
        inverse = jnp.where(diag > F32(0.0), F32(1.0) / diag, F32(0.0))
        st(di, r, inverse)
        st(U, G + r, inverse * ld(r_i, r))
    for r in range(0, n, 8):
        x = ld(U, G + r)
        down = ld(wy_i, G + r) * (x - ld(U, G + r + 1))
        up = ld(wy_i, G + r - 1) * (x - ld(U, G + r - 1))
        beside = ld(wl, r) * (x - form.left(x)) + ld(wx_i, r) * (x - form.right(x))
        st(t_o, r, (ld(an_i, r) * x + beside) + (down + up))
    for c in range(0, n // 4, 8):
        st(s_o, c, form.total(four_rows(t_o, 4 * c, 8)))


def message(form, bottom, r_o, wx_o, wy_o, an_o, fy_o, msg, g_o, cr_o, cd_o, ca_o, U, DI, V, WL, T, H, K):
    n = r_o.shape[1]
    zero = F32(0.0)
    G = GUARD

    def pick(low, high):
        return jnp.where(bottom, high, low)

    def align(x):
        return pl.multiple_of(x, 8)

    base = align(pick(0, n - 40))
    for r in range(0, 40, 8):
        at = align(base + r)
        w_x = ld(wx_o, at)
        w_l = form.left(w_x)
        st(WL, G + r, w_l)
        diag = ld(an_o, at) + w_x + w_l + ld(wy_o, align(at + G)) + ld(wy_o, base + (r + G - 1))
        inverse = jnp.where(diag > zero, F32(1.0) / diag, zero)
        st(DI, G + r, inverse)
        st(U, G + r, ld(r_o, at) * inverse)
    for source, image in ((U, T), (V, U)):
        for r in range(0, 40, 8):
            at = align(base + r)
            x = ld(source, G + r)
            beside = ld(WL, G + r) * (x - form.left(x)) + ld(wx_o, at) * (x - form.right(x))
            down = ld(wy_o, align(at + G)) * (x - ld(source, G + r + 1))
            up = ld(wy_o, base + (r + G - 1)) * (x - ld(source, G + r - 1))
            y = (ld(an_o, at) * x + beside) + (down + up)
            st(image, G + r, y)
            if image is T:
                st(V, G + r, ld(DI, G + r) * y)
    near = align(pick(0, 8))
    sums = form.total(four_rows(T, align(near + G), 8))
    sums_2 = form.total(four_rows(U, pick(0, 20) + G, 4))
    parts = {}

    def add(name, x):
        parts[name] = parts[name] + x if name in parts else x

    for k in range(4):
        at = base + (near + k)
        w_x = ld(wx_o, at, 8, 4)
        first, last = form.first_only(ld(WL, near + (G + k), 8, 4)), form.last_only(w_x)
        a = ld(an_o, at, 8, 4) + first + last
        inverse = ld(DI, near + (G + k), 8, 4)
        sides = []
        if k == 0:
            w = ld(wy_o, at + (G - 1), 8, 4)
            sides.append(("u", w))
            a = a + w
        if k == 3:
            w = ld(wy_o, at + G, 8, 4)
            sides.append(("d", w))
            a = a + w
        weighted = inverse * a
        add("aa", weighted * a)
        for name, w in (("l", first), ("r", last)):
            add("a" + name, weighted * w)
            scaled = inverse * w
            add(name + name, scaled * w)
            for other, v in sides:
                add(name + other, scaled * v)
        for name, w in sides:
            add("a" + name, weighted * w)
            add(name + name, inverse * w * w)
    parts = {name: form.total(x) for name, x in parts.items()}
    for k, name in enumerate(("uu", "dd", "au", "ru", "lu")):
        st(H.at[k], G, parts[name])
    uu, au, ru, lu = [ld(H.at[k], G + 1) for k in (0, 2, 3, 4)]
    dd = ld(H.at[1], G - 1)
    centre = parts["aa"] + form.coarse_right(parts["ll"]) + form.coarse_left(parts["rr"]) + uu + dd
    east = -(parts["ar"] + form.coarse_right(parts["al"]))
    south = -(parts["ad"] + au)
    south_east = form.coarse_right(parts["ld"]) + ru
    south_west = form.coarse_left(parts["rd"]) + lu
    for k, x in enumerate((centre, east, south, south_east, south_west)):
        st(K.at[k], 0, x)

    c = align(pick(0, n - 4 * FAR))
    coarse = (
        form.total(four_rows(r_o, c, FAR)),
        form.last_column(four_rows(wx_o, c, FAR)),
        form.total(ld(wy_o, c + (G + 3), FAR, 4)),
        form.total(four_rows(an_o, c, FAR)),
    )
    for out, x in zip((g_o, cr_o, cd_o, ca_o), coarse):
        st(out, 0, x)
    start = align(pick(0, n - HR))
    for k, (ref, top) in enumerate(((r_o, 0), (wx_o, 0), (wy_o, G), (an_o, 0))):
        st(msg, k * HR, ld(ref, align(start + top), HR))
    outer, inner = pick(HR - 1, 0), pick(HR - 2, 1)
    st(msg, outer, form.pack(*[sums[k : k + 1] for k in range(4)]))
    st(msg, inner, form.pack(*[sums[k : k + 1] for k in range(4, 8)]))
    st(msg, HR + outer, form.spread(form.total(ld(wy_o, n - 4 * FAR - 1 + G, 1))))
    st(msg, HR + inner, form.pack(*[sums_2[k : k + 1] for k in range(4)]))
    st(msg, 3 * HR + outer, ld(fy_o, 0, 1))
    packed = form.pack(*coarse)
    st(msg, 4 * HR, jnp.where(bottom, packed[: FAR - 1], packed[1:]))
    for k in range(5):
        four = [ld(K.at[k], pick(0, 3) + i, 1) for i in range(4)]
        st(msg, 4 * HR + FAR - 1 + k, form.pack(*four))


def apply_a(form, v, w_l, w_r, w_y, an, r):
    x = ld(v, r)
    down = ld(w_y, r) * (x - ld(v, r + 1))
    up = ld(w_y, r - 1) * (x - ld(v, r - 1))
    beside = w_l.chunk(r) * (x - form.left(x)) + w_r.chunk(r) * (x - form.right(x))
    return (an.chunk(r) * x + beside) + (down + up)


def basis(r_i, wx_i, wy_i, an_i, fy_i, g_a, cr_a, cd_a, ca_a, di_i, wl_i, t_i, s_i, g_b, cr_b, cd_b, ca_b, msg_in, msg_out, mom, PA, PB, PC, QA, QB, q2, r0,
         ENDS, WY, WM, T0, T1, T2, C_L, C_R, C_D, C_A, C_I, EA, EC, GC, SUM, E, D, KF, KV):
    blocks, n, _ = r_i.shape
    form = layout(blocks)
    fine = n + 2 * HR
    coarse = n // 4 + 2 * FAR
    zero = F32(0.0)
    odd, _, _, _ = position()
    own_blocks = blocks - 1
    B = GUARD

    def sides(a, b):
        x, y = ld(msg_in, a, b - a), ld(msg_out, a, b - a)
        return jnp.where(odd, x, y), jnp.where(odd, y, x)

    zeros = jnp.zeros((B, blocks * 128), F32)
    coarse_zeros = jnp.zeros((B, form.coarse_blocks * 128), F32)
    R, WX, AN, DI, WL = [Rows(own, ENDS.at[k]) for k, own in enumerate((r_i, wx_i, an_i, di_i, wl_i))]
    for ref in (WY, PA, PB, PC):
        st(ref, 0, zeros)
        st(ref, B + fine, zeros)
    for k, ends in ((0, ENDS.at[0]), (1, ENDS.at[1]), (3, ENDS.at[2])):
        for end, x in enumerate(sides(k * HR, (k + 1) * HR)):
            st(ends.at[end], 0, x)
    up, down = sides(2 * HR, 3 * HR)
    st(WY, B, up)
    st(WY, B + HR + n, down)
    for r in range(0, n, 8):
        st(WY, B + HR + r, ld(wy_i, GUARD + r))
    flux_up, _ = sides(3 * HR, 3 * HR + 1)
    first_rows = ld(r_i, 0) + jnp.where(rows(zeros.shape) == 0, jnp.broadcast_to(flux_up, zeros.shape), zero)
    below = ENDS.at[0, 1]
    st(below, 0, ld(below, 0, 1) + ld(fy_i, 0, 1))

    for end in (0, 1):
        st(ENDS.at[4, end], 0, form.left(ld(ENDS.at[1, end], 0)))

    def inverse(r):
        diag = AN.chunk(r) + WX.chunk(r) + WL.chunk(r) + ld(WY, r) + ld(WY, r - 1)
        return jnp.where(diag > zero, F32(1.0) / diag, zero)

    st(ENDS.at[3, 0], 0, inverse(B))
    st(ENDS.at[3, 1], 0, inverse(B + HR + n))
    first_inverse = inverse(B + HR)

    def read(field, r, first):
        return first if r == B + HR else field.chunk(r)

    for ref in (EA, EC, C_D, E.at[0], E.at[1], E.at[2]):
        st(ref, 0, coarse_zeros)
        st(ref, B + coarse, coarse_zeros)
    up, down = sides(4 * HR, 4 * HR + FAR - 1)
    for k, (ref, a, b) in enumerate(((GC, g_a, g_b), (C_R, cr_a, cr_b), (C_D, cd_a, cd_b), (C_A, ca_a, ca_b))):
        st(ref, B, form.unpack(up, k))
        st(ref, B + coarse - FAR + 1, form.unpack(down, k))
        x, y = ld(a, 0, FAR), ld(b, 0, FAR)
        st(ref, B + FAR, jnp.where(odd, y, x))
        st(ref, B + 2 * FAR, jnp.where(odd, x, y))
    st(GC, B + FAR, ld(GC, B + FAR, 1) + form.total(flux_up))
    beyond, _ = sides(HR, HR + 1)
    st(C_D, B - 1, form.take(beyond))
    for c in (FAR - 1, coarse - FAR):
        f = B + 4 * c - 40
        end, at = (0, 4) if c < FAR else (1, 0)
        st(GC, B + c, form.total(four_rows(ENDS.at[0, end], at, 1)))
        st(C_R, B + c, form.last_column(four_rows(ENDS.at[1, end], at, 1)))
        st(C_D, B + c, form.total(ld(WY, f + 3, 1)))
        st(C_A, B + c, form.total(four_rows(ENDS.at[2, end], at, 1)))
    for c in range(B, B + coarse, 8):
        c_r = ld(C_R, c)
        c_l = form.coarse_left(c_r)
        total = ld(C_A, c) + c_l + c_r + ld(C_D, c - 1) + ld(C_D, c)
        st(C_L, c, c_l)
        inverse_c = jnp.where(total > zero, F32(DAMP) / total, zero)
        st(C_I, c, inverse_c)
        st(EA, c, inverse_c * ld(GC, c))

    def set_sums(c, g):
        st(GC, B + c, g)
        st(EA, B + c, ld(C_I, B + c, g.shape[0]) * g)

    def smooth(turn, lo, hi):
        if lo > 0:
            st(EA, B + lo - 8, coarse_zeros)
            st(EC, B + lo - 8, coarse_zeros)
        if hi < coarse:
            st(EA, B + hi, coarse_zeros)
            st(EC, B + hi, coarse_zeros)
        for old, new in ((EA, EC), (EC, EA), (EA, E.at[turn])):
            for c in range(B + lo, B + hi, 8):
                e = ld(old, c)
                beside = ld(C_L, c) * form.coarse_left(e) + ld(C_R, c) * form.coarse_right(e)
                beside = beside + (ld(C_D, c - 1) * ld(old, c - 1) + ld(C_D, c) * ld(old, c + 1))
                st(new, c, F32(1.0 - DAMP) * e + ld(C_I, c) * (ld(GC, c) + beside))

    def differences(turn, lo, hi, with_sums):
        e_ref = E.at[turn]
        for c in range(B + lo, B + hi, 8):
            e = ld(e_ref, c)
            parts = (e - form.coarse_left(e), e - form.coarse_right(e), e - ld(e_ref, c - 1), e - ld(e_ref, c + 1))
            for k, x in enumerate(parts):
                st(D.at[turn, k], c, x)
            if with_sums:
                d_l, d_r, d_u, d_d = parts
                image = ld(C_A, c) * e + ld(C_L, c) * d_l + ld(C_R, c) * d_r
                g = ld(SUM, c) + (image + (ld(C_D, c - 1) * d_u + ld(C_D, c) * d_d))
                st(GC, c, g)
                st(EA, c, ld(C_I, c) * g)

    def lifted(turn, r):
        at = B + 10 + (r - B) // 4
        shape = (8, form.coarse_blocks * 128)
        row = rows(shape)

        def two(ref):
            a, b = [jnp.broadcast_to(ld(ref, at + k, 1), shape) for k in (0, 1)]
            return jnp.where(row < 4, a, b)

        e, d_l, d_r, d_u, d_d = two(E.at[turn]), *[two(D.at[turn, k]) for k in range(4)]
        e = form.spread(e)
        vertical = ld(WM, r) * form.spread(jnp.where(row % 4 == 0, d_u, d_d))
        return e, AN.chunk(r) * e + (form.at_sides(WL.chunk(r), d_l, WX.chunk(r), d_r) + vertical)

    def operate(v, t, chunks):
        for r in chunks:
            st(t, r, apply_a(form, v, WL, WX, WY, AN, r))

    def stretch(a, b):
        shape = (8, a.shape[1])
        return form.unpack_rows(jnp.where(rows(shape) < 4, jnp.broadcast_to(a, shape), jnp.broadcast_to(b, shape)))

    def second_sums(side, c, sums):
        for k in range(5):
            at = 4 * HR + FAR - 1 + k
            row = sides(at, at + 1)[side]
            st(KF.at[k], 8, form.unpack_rows(jnp.broadcast_to(row, (4, row.shape[1]))))
        centre, east, south, south_east, south_west = [ld(KF.at[k], 8, 4) for k in range(5)]
        north, north_west, north_east = [ld(KF.at[k], 7, 4) for k in (2, 3, 4)]
        e, below, above = [ld(E.at[0], B + c + d, 4) for d in (0, 1, -1)]
        image = centre * e + east * form.coarse_right(e) + form.coarse_left(east * e)
        image = image + south * below + north * above
        image = image + south_east * form.coarse_right(below) + form.coarse_left(north_west * above)
        image = image + south_west * form.coarse_left(below) + form.coarse_right(north_east * above)
        st(KV.at[side], 0, image + form.unpack_rows(jnp.broadcast_to(sums, (4, sums.shape[1]))))

    chunks = range(B, B + fine, 8)
    end = B + fine
    for r in (*chunks[:3], *chunks[-3:]):
        st(PA, r, read(DI, r, first_inverse) * read(R, r, first_rows))
    operate(PA, T0, (*chunks[:2], *chunks[-2:]))
    far_up, _ = sides(0, 1)
    near_up, _ = sides(1, 2)
    _, near_down = sides(HR - 1, HR)
    _, far_down = sides(HR - 2, HR - 1)
    st(SUM, B, coarse_zeros)
    st(SUM, B + coarse - 8, coarse_zeros)
    st(SUM, B + 4, stretch(far_up, near_up)[0:7])
    st(SUM, B + coarse - FAR + 1, stretch(near_down, far_down)[1:])
    st(SUM, B + FAR + 1, ld(s_i, 1, n // 4 - 2))
    st(SUM, B + FAR - 1, form.total(four_rows(T0, B + 4, 2)))
    st(SUM, B + coarse - FAR - 1, form.total(four_rows(T0, end - 12, 2)))
    for r in chunks:
        w_u, w_d = ld(WY, r - 1), ld(WY, r)
        row = rows(w_d.shape) % 4
        st(WM, r, jnp.where(row == 0, w_u, jnp.where(row == 3, w_d, zero)))

    smooth(0, 0, coarse)
    differences(0, 0, coarse, True)
    second_sums(0, 7, sides(HR + 1, HR + 2)[0])
    second_sums(1, coarse - FAR, sides(2 * HR - 2, 2 * HR - 1)[1])
    for r in chunks:
        e, image = lifted(0, r)
        inner = chunks[2] <= r < chunks[-2]
        p = read(DI, r, first_inverse) * read(R, r, first_rows) + e
        q = (ld(t_i, r - B - HR) if inner else ld(T0, r)) + image
        st(PA, r, p)
        st(QA, r, q)
        st(PB, r, read(DI, r, first_inverse) * q - F32(SHIFT) * p)
    st(r0, 0, first_rows)
    operate(PB, T1, chunks)
    for c, side in ((8, 0), (coarse - FAR + 1, 1)):
        st(SUM, B + c, ld(KV.at[side], 1, 3) - F32(SHIFT) * ld(GC, B + c, 3))
    for c in range(FAR - 1, coarse - FAR + 1, 8):
        st(SUM, B + c, form.total(four_rows(T1, B + 4 * c - 40, min(8, coarse - FAR + 1 - c))))
    smooth(1, 0, coarse)
    differences(1, 8, coarse - 8, True)
    for r in chunks:
        e, image = lifted(1, r)
        p = ld(PB, r) + e
        q = ld(T1, r) + image
        st(PB, r, p)
        st(QB, r, q)
        st(PC, r, read(DI, r, first_inverse) * q - F32(SHIFT) * p)
    operate(PC, T2, chunks[1:-1])
    smooth(2, 8, coarse - 8)
    differences(2, 8, coarse - 8, False)
    acc = [jnp.zeros((8, 128), F32) for _ in range(9)]
    for r in range(0, n, 8):
        f = B + HR + r
        e, image = lifted(2, f)
        image = ld(T2, f) + image
        st(PC, f, ld(PC, f) + e)
        sums = [[] for _ in acc]
        for j in range(own_blocks):
            i2 = image[:, j * 128 : (j + 1) * 128]
            q2[j, r : r + 8, :] = i2
            z0, z1, z2, i0, i1 = [x[j, f : f + 8, :] for x in (PA, PB, PC, QA, QB)]
            res = read(R, f, first_rows)[:, j * 128 : (j + 1) * 128]
            pairs = ((z0, i0), (z1, i0), (z1, i1), (z2, i0), (z2, i1), (z2, i2), (z0, res), (z1, res), (z2, res))
            for k, (x, y) in enumerate(pairs):
                sums[k].append(x * y)
        for k, parts in enumerate(sums):
            acc[k] = acc[k] + tree(parts)
    lane = lanes((8, 128))
    line = jnp.zeros((8, 128), F32)
    for k in range(9):
        total = jnp.sum(jnp.sum(acc[k], axis=0, keepdims=True), axis=1, keepdims=True)
        line = jnp.where(lane == k, jnp.broadcast_to(total, (8, 128)), line)
    for j in range(mom.shape[0]):
        mom[j] = line[0:1]


def combine(mom, p0, p1, p2, q0, q1, q2, r_first, r_i, heights, residual, work):
    blocks, n, _ = q2.shape
    skip = GUARD + HR
    form = layout(blocks + 1)
    tot = jnp.broadcast_to(tree([mom[j] for j in range(mom.shape[0])]), (8, 128))
    m = [jnp.broadcast_to(tot[:, k : k + 1], (8, 128)) for k in range(9)]
    g00, g10, g11, g20, g21, g22, b0, b1, b2 = m
    l10, l20 = g10 / g00, g20 / g00
    d1 = g11 - l10 * g10
    t21 = g21 - l20 * g10
    l21 = t21 / d1
    d2 = g22 - l20 * g20 - l21 * t21
    y1 = b1 - l10 * b0
    y2 = b2 - l20 * b0 - l21 * y1
    x2 = y2 / d2
    x1 = y1 / d1 - l21 * x2
    x0 = b0 / g00 - l10 * x1 - l20 * x2
    sums, spare = [[work.at[k], work.at[k + 1]] for k in (0, 2)]
    for r in range(0, n, 8):
        for j in range(blocks):
            z0, z1, z2, i0, i1 = [x[j, skip + r : skip + r + 8, :] for x in (p0, p1, p2, q0, q1)]
            i2, res = q2[j, r : r + 8, :], r_first[j] if r == 0 else r_i[j, r : r + 8, :]
            sums[0][j, r : r + 8, :] = x0 * z0 + x1 * z1 + x2 * z2
            sums[1][j, r : r + 8, :] = res - (x0 * i0 + x1 * i1 + x2 * i2)
    reorder(form.steps_out, sums, [heights, residual], spare)


def swap(x, axis, size, inner):
    if inner:
        pairs = [(i, i ^ 1) for i in range(size) if i ^ 1 < size]
    else:
        pairs = [(i, j) for i in range(size) for j in [((i + 1) ^ 1) - 1] if 0 <= j < size]
    return lax.ppermute(x, axis, pairs)


def local(nrow, ncol, gx, gy, wx, wy, an, pr):
    n, width = gx.shape
    ext = width + 2 * HC
    fields = tuple(pltpu.with_memory_space_constraint(f, pltpu.HBM) for f in (gx, gy, wx, wy, an, pr))
    nb = ext // 128
    shape = lambda *dims: jax.ShapeDtypeStruct(dims, F32)
    params = pltpu.CompilerParams(vmem_limit_bytes=48 * 1024 * 1024)

    def call(kernel, name, args, outs, scratch=(), us=1, fetches=0):
        sems = [pltpu.SemaphoreType.DMA((fetches,))] if fetches else []
        return pl.pallas_call(
            kernel,
            in_specs=[HBM if fetches else VMEM] * len(args),
            out_specs=[VMEM] * len(outs),
            out_shape=outs,
            scratch_shapes=[pltpu.VMEM(dims, F32) for dims in scratch] + sems,
            compiler_params=params,
            cost_estimate=pl.CostEstimate(flops=us * 2_000_000, bytes_accessed=us * 2_000_000, transcendentals=0),
            name=name,
        )(*args)

    halos = []
    for inner in (True, False) if ncol > 2 else (True,):
        (edge,) = call(functools.partial(edge_columns, inner), "edge_columns", fields, [shape(n + n // 2 + 8, 128)], [(n, 128)] * 6, 1, 6)
        halos.append(swap(edge, "col", ncol, inner))
    tile = shape(nb - 1, n, 128)
    own = call(tile_fields, "tile_fields", fields, [tile] * 4 + [shape(n, 128), shape(nb - 1, 8, 128)], [(n, width)] * 6 + [(4, nb - 1, n, 128)] * 2 + [(2, nb - 1, 8, 128)], 1, 6)
    cb = layout(nb).coarse_blocks
    far = shape(cb, FAR, 128)
    msg = shape(nb, DEPTH, 128)
    field = shape(nb, n, 128)
    work = [(nb, 40 + 2 * GUARD, 128)] * 5 + [(5, cb, 24, 128), (5, cb, 8, 128)]
    *fields, to_out, g_a, cr_a, cd_a, ca_a = call(
        functools.partial(edge_rows, len(halos) > 1),
        "edge_rows",
        (*own, *halos),
        [field, field, shape(nb, GUARD + n, 128), field, shape(nb, 8, 128), msg] + [far] * 4,
        work,
    )
    from_out = swap(to_out, "row", nrow, False)
    di, wl, t, sums, to_in, *far_b = call(
        near_rows,
        "near_rows",
        fields,
        [field, field, field, shape(cb, n // 4, 128), msg] + [far] * 4,
        work + [(nb, n + 2 * GUARD, 128)],
    )
    from_in = swap(to_in, "row", nrow, True)
    fine = n + 2 * HR
    coarse = n // 4 + 2 * FAR
    mom, *vectors = call(
        basis,
        "basis",
        (*fields, g_a, cr_a, cd_a, ca_a, di, wl, t, sums, *far_b, from_in, from_out),
        [shape(nrow * ncol, 1, 128)] + [shape(nb, fine + 2 * GUARD, 128)] * 5 + [tile, shape(nb, 8, 128)],
        [(5, 2, nb, HR, 128)] + [(nb, fine + 2 * GUARD, 128)] * 5 + [(cb, coarse + 2 * GUARD, 128)] * 9
        + [(3, cb, coarse + 2 * GUARD, 128), (3, 4, cb, coarse + 2 * GUARD, 128), (5, cb, 16, 128), (2, cb, 8, 128)],
    )
    mom = lax.all_to_all(mom, ("row", "col"), 0, 0, tiled=True)
    out = shape(n, width)
    return tuple(call(combine, "combine", (mom, *vectors, fields[0]), [out, out], [(4, nb - 1, n, 128)]))


def solution(mesh):
    spec = P("row", "col")
    return jax.shard_map(
        functools.partial(local, mesh.shape["row"], mesh.shape["col"]),
        mesh=mesh,
        in_specs=(spec,) * 6,
        out_specs=(spec, spec),
        check_vma=False,
    )
```

```python
import functools

import jax
import jax.numpy as jnp
from jax import lax
from jax.experimental import pallas as pl
from jax.experimental.pallas import tpu as pltpu
from jax.sharding import PartitionSpec as P

DAMP = 2.0 / 3.0
SHIFT = 1.0
HC = 64
SENT = 48
HR = 8
FAR = 12
DEPTH = 4 * HR + FAR - 1 + 5
GUARD = 8
VMEM = pl.BlockSpec(memory_space=pltpu.VMEM)
HBM = pl.BlockSpec(memory_space=pltpu.HBM)
F32 = jnp.float32


def lanes(shape):
    return lax.broadcasted_iota(jnp.int32, shape, 1)


def rows(shape):
    return lax.broadcasted_iota(jnp.int32, shape, 0)


def roll_right(x, k=1):
    return pltpu.roll(x, k, 1)


def roll_left(x, k=1):
    return pltpu.roll(x, x.shape[1] - k, 1)


def group_sum(x):
    four = lanes(x.shape) % 4
    one = jnp.where(four < 3, roll_left(x), roll_right(x, 3))
    two = jnp.where(four < 2, roll_left(x, 2), roll_right(x, 2))
    three = jnp.where(four < 1, roll_left(x, 3), roll_right(x))
    return (x + two) + (one + three)


def split(x):
    return [x[:, j : j + 128] for j in range(0, x.shape[1], 128)]


def join(parts):
    return jnp.concatenate(parts, axis=1)


class Wide:
    def __init__(self, width):
        self.coarse_blocks = width // 128 + 1

    left, right = staticmethod(roll_right), staticmethod(roll_left)
    total = staticmethod(group_sum)
    spread = take = staticmethod(lambda x: x)
    steps_in = steps_out = (lambda parts: parts,)

    def coarse_left(self, e):
        return roll_right(e, 4)

    def coarse_right(self, e):
        return roll_left(e, 4)

    def last_column(self, x):
        return group_sum(jnp.where(lanes(x.shape) % 4 == 3, x, F32(0.0)))

    def pack(self, a, b, c, d):
        four = lanes(a.shape) % 4
        return jnp.where(four < 2, jnp.where(four == 0, a, b), jnp.where(four == 2, c, d))

    def unpack(self, m, k):
        return group_sum(jnp.where(lanes(m.shape) % 4 == k, m, F32(0.0)))

    def unpack_rows(self, m):
        return group_sum(jnp.where(lanes(m.shape) % 4 == rows(m.shape) % 4, m, F32(0.0)))

    def at_sides(self, w_l, d_l, w_r, d_r):
        return self.first_only(w_l * d_l) + self.last_only(w_r * d_r)

    def first_only(self, x):
        return jnp.where(lanes(x.shape) % 4 == 0, x, F32(0.0))

    def last_only(self, x):
        return jnp.where(lanes(x.shape) % 4 == 3, x, F32(0.0))


class Planes:
    coarse_blocks = 2

    def left(self, x):
        a, b, c, d, h = split(x)
        first = lanes(h.shape) == 0
        d, h = roll_right(d), roll_right(h)
        return join([jnp.where(first, h, d), a, b, c, jnp.where(first, d, h)])

    def right(self, x):
        a, b, c, d, h = split(x)
        last = lanes(h.shape) == 127
        a, h = roll_left(a), roll_left(h)
        return join([b, c, d, jnp.where(last, h, a), jnp.where(last, a, h)])

    def coarse_left(self, e):
        o, h = split(e)
        lane = lanes(h.shape)
        end = jnp.broadcast_to(o[:, 127:128], h.shape)
        return join([jnp.where(lane == 0, roll_right(h), roll_right(o)), jnp.where(lane < 4, end, roll_right(h, 4))])

    def coarse_right(self, e):
        o, h = split(e)
        lane = lanes(h.shape)
        end = jnp.broadcast_to(o[:, 0:1], h.shape)
        return join([jnp.where(lane == 127, roll_left(h), roll_left(o)), jnp.where(lane >= 124, end, roll_left(h, 4))])

    def total(self, x):
        a, b, c, d, h = split(x)
        return join([(a + b) + (c + d), group_sum(h)])

    def last_column(self, x):
        h = x[:, 512:640]
        return join([x[:, 384:512], group_sum(jnp.where(lanes(h.shape) % 4 == 3, h, F32(0.0)))])

    def spread(self, e):
        o, h = split(e)
        return join([o, o, o, o, h])

    def take(self, x):
        return join([x[:, 0:128], x[:, 512:640]])

    def pack(self, *fields):
        own, halo = zip(*[split(f) for f in fields])
        a, b, c, d = halo
        four = lanes(a.shape) % 4
        mixed = jnp.where(four < 2, jnp.where(four == 0, a, b), jnp.where(four == 2, c, d))
        return join([*own, mixed])

    def unpack(self, m, k):
        h = m[:, 512:640]
        return join([m[:, k * 128 : k * 128 + 128], group_sum(jnp.where(lanes(h.shape) % 4 == k, h, F32(0.0)))])

    def unpack_rows(self, m):
        a, b, c, d, h = split(m)
        key = rows(h.shape) % 4
        own = jnp.where(key < 2, jnp.where(key == 0, a, b), jnp.where(key == 2, c, d))
        return join([own, group_sum(jnp.where(lanes(h.shape) % 4 == key, h, F32(0.0)))])

    def at_sides(self, w_l, d_l, w_r, d_r):
        w_l, d_l, w_r, d_r = split(w_l), split(d_l), split(w_r), split(d_r)
        four = lanes(d_l[1].shape) % 4
        none = jnp.zeros_like(d_l[1])
        halo = jnp.where(four == 0, w_l[4] * d_l[1], jnp.where(four == 3, w_r[4] * d_r[1], none))
        return join([w_l[0] * d_l[0], none, none, w_r[3] * d_r[0], halo])

    def first_only(self, x):
        a, _, _, _, h = split(x)
        none = jnp.zeros_like(h)
        return join([a, none, none, none, jnp.where(lanes(h.shape) % 4 == 0, h, none)])

    def last_only(self, x):
        _, _, _, d, h = split(x)
        none = jnp.zeros_like(h)
        return join([none, none, none, d, jnp.where(lanes(h.shape) % 4 == 3, h, none)])

    def gather_in(self, parts):
        lane = lanes(parts[0].shape)
        index = (lane % 32) * 4 + lane // 32
        return [jnp.take_along_axis(p, index, axis=1) for p in parts]

    def gather_out(self, parts):
        lane = lanes(parts[0].shape)
        index = (lane % 4) * 32 + lane // 4
        return [jnp.take_along_axis(p, index, axis=1) for p in parts]

    def swap_halves(self, parts):
        a, b, c, d = parts
        low = lanes(a.shape) < 64
        return [
            jnp.where(low, a, roll_right(c, 64)),
            jnp.where(low, b, roll_right(d, 64)),
            jnp.where(low, roll_right(a, 64), c),
            jnp.where(low, roll_right(b, 64), d),
        ]

    def swap_quarters(self, parts):
        a, b, c, d = parts
        low = lanes(a.shape) % 64 < 32
        return [
            jnp.where(low, a, roll_right(b, 32)),
            jnp.where(low, roll_left(a, 32), b),
            jnp.where(low, c, roll_right(d, 32)),
            jnp.where(low, roll_left(c, 32), d),
        ]

    @property
    def steps_in(self):
        return self.gather_in, self.swap_halves, self.swap_quarters

    @property
    def steps_out(self):
        return self.swap_halves, self.swap_quarters, self.gather_out


class Rows:
    def __init__(self, own, ends):
        self.own, self.ends = own, ends

    def chunk(self, start):
        start -= GUARD + HR
        if 0 <= start < self.own.shape[1]:
            return ld(self.own, start)
        return ld(self.ends.at[int(start >= 0)], 0)


def layout(blocks):
    return Planes() if blocks == 5 else Wide(128 * (blocks - 1))


def ld(ref, start, count=8, step=1):
    rows_of = pl.ds(start, count, stride=step) if step > 1 else pl.ds(start, count)
    return jnp.concatenate([ref[j, rows_of, :] for j in range(ref.shape[0])], axis=1)


def st(ref, start, value, step=1):
    count = value.shape[0]
    rows_of = pl.ds(start, count, stride=step) if step > 1 else pl.ds(start, count)
    for j in range(ref.shape[0]):
        ref[j, rows_of, :] = value[:, j * 128 : (j + 1) * 128]


def tree(parts):
    while len(parts) > 1:
        parts = [sum(parts[j + 1 : j + 2], parts[j]) for j in range(0, len(parts), 2)]
    return parts[0]


def four_rows(ref, start, count):
    parts = [ld(ref, start + k, count, 4) for k in range(4)]
    return (parts[0] + parts[1]) + (parts[2] + parts[3])


def position():
    row, col = lax.axis_index("row"), lax.axis_index("col")
    end_row = row == lax.axis_size("row") - 1
    end_col = col == lax.axis_size("col") - 1
    return lax.rem(row, 2) == 1, lax.rem(col, 2) == 1, end_row, end_col


def reorder(steps, sources, targets, spare):
    pairs = list(zip(sources, spare))
    for k, step in enumerate(steps):
        for (x, y), target in zip(pairs, targets):
            x, y = (y, x) if k % 2 else (x, y)
            y = target if k == len(steps) - 1 else y
            for r in range(0, x.shape[1], 8):
                for j, block in enumerate(step([x[j, r : r + 8, :] for j in range(x.shape[0])])):
                    if len(y.shape) == 2:
                        y[r : r + 8, j * 128 : j * 128 + 128] = block
                    else:
                        y[j, r : r + 8, :] = block


def fetch(sources, targets, sems):
    copies = [pltpu.make_async_copy(x, y, sems.at[k]) for k, (x, y) in enumerate(zip(sources, targets))]
    for copy in copies:
        copy.start()
    for copy in copies:
        copy.wait()


def edge_columns(inner, *refs):
    fields, (out, *held, sems) = refs[:6], refs[6:]
    n, width = fields[0].shape
    half = n // 2
    _, col_odd, end_row, _ = position()
    last = jnp.logical_not(col_odd) if inner else col_odd
    offset = pl.multiple_of(jnp.where(last, width - 128, 0), 128)
    row, lane = rows((8, 128)), lanes((8, 128))
    zero = F32(0.0)
    fetch([f.at[:, pl.ds(offset, 128)] for f in fields], held, sems)

    def to(x, target):
        return pltpu.roll(x, jnp.where(last, (target + SENT) % 128, target % 128), 1)

    def chunk(r, second):
        g_x, g_y, w_x, w_y, a, p = [f[r : r + 8, :] for f in held]
        if r == n - 8:
            w_y = jnp.where((row == 7) & end_row, zero, w_y)
        fx = w_x * g_x
        fy = w_y * g_y
        before = jnp.zeros((1, 128), F32) if r == 0 else held[3][r - 1 : r, :] * held[1][r - 1 : r, :]
        before_y = jnp.where(row == 0, jnp.broadcast_to(before, fy.shape), pltpu.roll(fy, 1, 0))
        src = to(a * p - fx + before_y - fy, 0)
        src = src + jnp.where((lane == 0) & jnp.logical_not(last), zero, to(fx, 1))
        flux = jnp.broadcast_to(fx[:, 127:128], fx.shape)
        right = jnp.where((lane == SENT) & last, flux, to(w_x, SENT))
        down = to(w_y, 2 * SENT)
        out[r : r + 8, :] = jnp.where(lane < SENT, src, jnp.where(lane < 2 * SENT, right, down))
        start = 80 if second else 16
        beyond = jnp.where((lane == start) & last, to(w_x, start + 1), zero)
        rest = jnp.where(lane < start, to(w_y, 32) if second else down, to(a, start) + beyond)
        return rest, fy[7:8, :]

    for r in range(0, half, 8):
        first, _ = chunk(r, False)
        second, tail = chunk(r + half, True)
        out[n + r : n + r + 8, :] = jnp.where(lane < HC, first, second)
    out[n + half :, :] = to(jnp.broadcast_to(tail, (8, 128)), 0)


def tile_fields(*refs):
    fields, (r_o, wx_o, wy_o, an_o, fx_o, fy_o, *held, raw, spare, tail, sems) = refs[:6], refs[6:]
    gx, gy, wx, wy, an, pr = held
    n, width = gx.shape
    form = layout(width // 128 + 1)
    fetch(fields, held, sems)
    _, _, end_row, end_col = position()
    row, lane = rows((8, width)), lanes((8, width))
    zero = F32(0.0)
    carry = jnp.zeros((1, width), F32)
    for r in range(0, n, 8):
        w_x = jnp.where((lane == width - 1) & end_col, zero, wx[r : r + 8, :])
        w_y = wy[r : r + 8, :]
        if r == n - 8:
            w_y = jnp.where((row == 7) & end_row, zero, w_y)
        fx = w_x * gx[r : r + 8, :]
        fy = w_y * gy[r : r + 8, :]
        a = an[r : r + 8, :]
        before_x = jnp.where(lane == 0, zero, roll_right(fx))
        before_y = jnp.where(row == 0, jnp.broadcast_to(carry, fy.shape), pltpu.roll(fy, 1, 0))
        carry = fy[7:8, :]
        src = a * pr[r : r + 8, :] + before_x - fx + before_y - fy
        for k, x in enumerate((src, w_x, w_y, a)):
            st(raw.at[k], r, x)
        fx_o[r : r + 8, :] = jnp.broadcast_to(fx[:, width - 1 : width], (8, 128))
    st(tail.at[0], 0, jnp.broadcast_to(carry, (8, width)))
    pick = lambda ref: [ref.at[k] for k in range(4)]
    reorder(form.steps_in, [*pick(raw), tail.at[0]], [r_o, wx_o, wy_o, an_o, fy_o], [*pick(spare), tail.at[1]])


def edge_rows(has_outer, r_t, wx_t, wy_t, an_t, fx_t, fy_t, *refs):
    inner, refs = refs[0], refs[1:]
    outer = None
    if has_outer:
        outer, refs = refs[0], refs[1:]
    r_o, wx_o, wy_o, an_o, fy_o, *rest = refs
    own, n, _ = r_t.shape
    form = layout(own + 1)
    row_odd, odd, _, _ = position()
    lane = lanes((8, 128))
    zero = F32(0.0)

    messages = [(inner, odd)] + ([(outer, jnp.logical_not(odd))] if has_outer else [])

    def placed(x, source, before):
        return pltpu.roll(x, jnp.where(before, (128 - SENT - source) % 128, -source % 128), 1)

    def within(x, before):
        start = jnp.where(before, 128 - SENT, 0)
        return jnp.where((lane >= start) & (lane < start + SENT), x, zero)

    def halo(m, before, r):
        half = n // 2
        main = m[r : r + 8, :]
        second = r >= half
        rest = m[n + r % half : n + r % half + 8, :]
        src = placed(main, 0, before)
        right = jnp.where(lane == 128 - SENT, zero, placed(main, SENT, before))
        if second:
            near = lane < jnp.where(before, 128 - SENT + 32, 32)
            down = jnp.where(near, placed(main, 2 * SENT, before), placed(rest, 32, before))
        else:
            down = placed(jnp.where(lane < 2 * SENT, rest, main), 2 * SENT, before)
        a = placed(rest, 80 if second else 16, before)
        flux = jnp.where(before, jnp.broadcast_to(main[:, SENT : SENT + 1], main.shape), zero)
        return [within(x, before) for x in (src, right, down, a)] + [flux]

    for r in range(0, n, 8):
        parts = [halo(m, before, r) for m, before in messages]
        src_h, wx_h, wy_h, an_h, incoming = [tree(list(x)) for x in zip(*parts)]
        src_h = jnp.where(lane == 0, src_h + fx_t[r : r + 8, :], src_h)
        for out, tile, h in ((r_o, r_t, src_h), (wx_o, wx_t, wx_h), (wy_o, wy_t, wy_h), (an_o, an_t, an_h)):
            top = GUARD if out is wy_o else 0
            for j in range(own):
                x = tile[j, r : r + 8, :]
                if out is r_o and j == 0:
                    x = jnp.where(lane == 0, x + incoming, x)
                out[j, top + r : top + r + 8, :] = x
            out[own, top + r : top + r + 8, :] = h
    st(wy_o, 0, jnp.zeros((GUARD, (own + 1) * 128), F32))
    for j in range(own):
        fy_o[j] = fy_t[j]
    tails = [within(placed(m[n + n // 2 :, :], 0, before), before) for m, before in messages]
    fy_o[own] = tree(tails)

    message(form, row_odd, r_o, wx_o, wy_o, an_o, fy_o, *rest)


def near_rows(r_i, wx_i, wy_i, an_i, fy_i, di, wl, t_o, s_o, *rest):
    form = layout(wx_i.shape[0])
    row_odd, _, _, _ = position()
    *rest, U = rest
    message(form, jnp.logical_not(row_odd), r_i, wx_i, wy_i, an_i, fy_i, *rest)
    n, G = wx_i.shape[1], GUARD
    for r in range(0, wx_i.shape[1], 8):
        w_x, w_y = ld(wx_i, r), ld(wy_i, GUARD + r)
        w_l = form.left(w_x)
        st(wl, r, w_l)
        diag = ld(an_i, r) + w_x + w_l + w_y + ld(wy_i, GUARD + r - 1)
        inverse = jnp.where(diag > F32(0.0), F32(1.0) / diag, F32(0.0))
        st(di, r, inverse)
        st(U, G + r, inverse * ld(r_i, r))
    for r in range(0, n, 8):
        x = ld(U, G + r)
        down = ld(wy_i, G + r) * (x - ld(U, G + r + 1))
        up = ld(wy_i, G + r - 1) * (x - ld(U, G + r - 1))
        beside = ld(wl, r) * (x - form.left(x)) + ld(wx_i, r) * (x - form.right(x))
        st(t_o, r, (ld(an_i, r) * x + beside) + (down + up))
    for c in range(0, n // 4, 8):
        st(s_o, c, form.total(four_rows(t_o, 4 * c, 8)))


def message(form, bottom, r_o, wx_o, wy_o, an_o, fy_o, msg, g_o, cr_o, cd_o, ca_o, U, DI, V, WL, T, H, K):
    n = r_o.shape[1]
    zero = F32(0.0)
    G = GUARD

    def pick(low, high):
        return jnp.where(bottom, high, low)

    def align(x):
        return pl.multiple_of(x, 8)

    base = align(pick(0, n - 40))
    for r in range(0, 40, 8):
        at = align(base + r)
        w_x = ld(wx_o, at)
        w_l = form.left(w_x)
        st(WL, G + r, w_l)
        diag = ld(an_o, at) + w_x + w_l + ld(wy_o, align(at + G)) + ld(wy_o, base + (r + G - 1))
        inverse = jnp.where(diag > zero, F32(1.0) / diag, zero)
        st(DI, G + r, inverse)
        st(U, G + r, ld(r_o, at) * inverse)
    for source, image in ((U, T), (V, U)):
        for r in range(0, 40, 8):
            at = align(base + r)
            x = ld(source, G + r)
            beside = ld(WL, G + r) * (x - form.left(x)) + ld(wx_o, at) * (x - form.right(x))
            down = ld(wy_o, align(at + G)) * (x - ld(source, G + r + 1))
            up = ld(wy_o, base + (r + G - 1)) * (x - ld(source, G + r - 1))
            y = (ld(an_o, at) * x + beside) + (down + up)
            st(image, G + r, y)
            if image is T:
                st(V, G + r, ld(DI, G + r) * y)
    near = align(pick(0, 8))
    sums = form.total(four_rows(T, align(near + G), 8))
    sums_2 = form.total(four_rows(U, pick(0, 20) + G, 4))
    parts = {}

    def add(name, x):
        parts[name] = parts[name] + x if name in parts else x

    for k in range(4):
        at = base + (near + k)
        w_x = ld(wx_o, at, 8, 4)
        first, last = form.first_only(ld(WL, near + (G + k), 8, 4)), form.last_only(w_x)
        a = ld(an_o, at, 8, 4) + first + last
        inverse = ld(DI, near + (G + k), 8, 4)
        sides = []
        if k == 0:
            w = ld(wy_o, at + (G - 1), 8, 4)
            sides.append(("u", w))
            a = a + w
        if k == 3:
            w = ld(wy_o, at + G, 8, 4)
            sides.append(("d", w))
            a = a + w
        weighted = inverse * a
        add("aa", weighted * a)
        for name, w in (("l", first), ("r", last)):
            add("a" + name, weighted * w)
            scaled = inverse * w
            add(name + name, scaled * w)
            for other, v in sides:
                add(name + other, scaled * v)
        for name, w in sides:
            add("a" + name, weighted * w)
            add(name + name, inverse * w * w)
    parts = {name: form.total(x) for name, x in parts.items()}
    for k, name in enumerate(("uu", "dd", "au", "ru", "lu")):
        st(H.at[k], G, parts[name])
    uu, au, ru, lu = [ld(H.at[k], G + 1) for k in (0, 2, 3, 4)]
    dd = ld(H.at[1], G - 1)
    centre = parts["aa"] + form.coarse_right(parts["ll"]) + form.coarse_left(parts["rr"]) + uu + dd
    east = -(parts["ar"] + form.coarse_right(parts["al"]))
    south = -(parts["ad"] + au)
    south_east = form.coarse_right(parts["ld"]) + ru
    south_west = form.coarse_left(parts["rd"]) + lu
    for k, x in enumerate((centre, east, south, south_east, south_west)):
        st(K.at[k], 0, x)

    c = align(pick(0, n - 4 * FAR))
    coarse = (
        form.total(four_rows(r_o, c, FAR)),
        form.last_column(four_rows(wx_o, c, FAR)),
        form.total(ld(wy_o, c + (G + 3), FAR, 4)),
        form.total(four_rows(an_o, c, FAR)),
    )
    for out, x in zip((g_o, cr_o, cd_o, ca_o), coarse):
        st(out, 0, x)
    start = align(pick(0, n - HR))
    for k, (ref, top) in enumerate(((r_o, 0), (wx_o, 0), (wy_o, G), (an_o, 0))):
        st(msg, k * HR, ld(ref, align(start + top), HR))
    outer, inner = pick(HR - 1, 0), pick(HR - 2, 1)
    st(msg, outer, form.pack(*[sums[k : k + 1] for k in range(4)]))
    st(msg, inner, form.pack(*[sums[k : k + 1] for k in range(4, 8)]))
    st(msg, HR + outer, form.spread(form.total(ld(wy_o, n - 4 * FAR - 1 + G, 1))))
    st(msg, HR + inner, form.pack(*[sums_2[k : k + 1] for k in range(4)]))
    st(msg, 3 * HR + outer, ld(fy_o, 0, 1))
    packed = form.pack(*coarse)
    st(msg, 4 * HR, jnp.where(bottom, packed[: FAR - 1], packed[1:]))
    for k in range(5):
        four = [ld(K.at[k], pick(0, 3) + i, 1) for i in range(4)]
        st(msg, 4 * HR + FAR - 1 + k, form.pack(*four))


def apply_a(form, v, w_l, w_r, w_y, an, r):
    x = ld(v, r)
    down = ld(w_y, r) * (x - ld(v, r + 1))
    up = ld(w_y, r - 1) * (x - ld(v, r - 1))
    beside = w_l.chunk(r) * (x - form.left(x)) + w_r.chunk(r) * (x - form.right(x))
    return (an.chunk(r) * x + beside) + (down + up)


def basis(r_i, wx_i, wy_i, an_i, fy_i, g_a, cr_a, cd_a, ca_a, di_i, wl_i, t_i, s_i, g_b, cr_b, cd_b, ca_b, msg_in, msg_out, mom, PA, PB, PC, QA, QB, q2, r0,
         ENDS, WY, WM, T0, T1, T2, C_L, C_R, C_D, C_A, C_I, M_L, M_R, M_U, M_D, EA, EC, GC, SUM, E, D, KF, KV):
    blocks, n, _ = r_i.shape
    form = layout(blocks)
    fine = n + 2 * HR
    coarse = n // 4 + 2 * FAR
    zero = F32(0.0)
    odd, _, _, _ = position()
    own_blocks = blocks - 1
    B = GUARD

    def sides(a, b):
        x, y = ld(msg_in, a, b - a), ld(msg_out, a, b - a)
        return jnp.where(odd, x, y), jnp.where(odd, y, x)

    zeros = jnp.zeros((B, blocks * 128), F32)
    coarse_zeros = jnp.zeros((B, form.coarse_blocks * 128), F32)
    R, WX, AN, DI, WL = [Rows(own, ENDS.at[k]) for k, own in enumerate((r_i, wx_i, an_i, di_i, wl_i))]
    for ref in (WY, PA, PB, PC):
        st(ref, 0, zeros)
        st(ref, B + fine, zeros)
    for k, ends in ((0, ENDS.at[0]), (1, ENDS.at[1]), (3, ENDS.at[2])):
        for end, x in enumerate(sides(k * HR, (k + 1) * HR)):
            st(ends.at[end], 0, x)
    up, down = sides(2 * HR, 3 * HR)
    st(WY, B, up)
    st(WY, B + HR + n, down)
    for r in range(0, n, 8):
        st(WY, B + HR + r, ld(wy_i, GUARD + r))
    flux_up, _ = sides(3 * HR, 3 * HR + 1)
    first_rows = ld(r_i, 0) + jnp.where(rows(zeros.shape) == 0, jnp.broadcast_to(flux_up, zeros.shape), zero)
    below = ENDS.at[0, 1]
    st(below, 0, ld(below, 0, 1) + ld(fy_i, 0, 1))

    for end in (0, 1):
        st(ENDS.at[4, end], 0, form.left(ld(ENDS.at[1, end], 0)))

    def inverse(r):
        diag = AN.chunk(r) + WX.chunk(r) + WL.chunk(r) + ld(WY, r) + ld(WY, r - 1)
        return jnp.where(diag > zero, F32(1.0) / diag, zero)

    st(ENDS.at[3, 0], 0, inverse(B))
    st(ENDS.at[3, 1], 0, inverse(B + HR + n))
    first_inverse = inverse(B + HR)

    def read(field, r, first):
        return first if r == B + HR else field.chunk(r)

    for ref in (EA, EC, C_D, E.at[0], E.at[1], E.at[2]):
        st(ref, 0, coarse_zeros)
        st(ref, B + coarse, coarse_zeros)
    up, down = sides(4 * HR, 4 * HR + FAR - 1)
    for k, (ref, a, b) in enumerate(((GC, g_a, g_b), (C_R, cr_a, cr_b), (C_D, cd_a, cd_b), (C_A, ca_a, ca_b))):
        st(ref, B, form.unpack(up, k))
        st(ref, B + coarse - FAR + 1, form.unpack(down, k))
        x, y = ld(a, 0, FAR), ld(b, 0, FAR)
        st(ref, B + FAR, jnp.where(odd, y, x))
        st(ref, B + 2 * FAR, jnp.where(odd, x, y))
    st(GC, B + FAR, ld(GC, B + FAR, 1) + form.total(flux_up))
    beyond, _ = sides(HR, HR + 1)
    st(C_D, B - 1, form.take(beyond))
    for c in (FAR - 1, coarse - FAR):
        f = B + 4 * c - 40
        end, at = (0, 4) if c < FAR else (1, 0)
        st(GC, B + c, form.total(four_rows(ENDS.at[0, end], at, 1)))
        st(C_R, B + c, form.last_column(four_rows(ENDS.at[1, end], at, 1)))
        st(C_D, B + c, form.total(ld(WY, f + 3, 1)))
        st(C_A, B + c, form.total(four_rows(ENDS.at[2, end], at, 1)))
    for c in range(B, B + coarse, 8):
        c_r = ld(C_R, c)
        c_l = form.coarse_left(c_r)
        total = ld(C_A, c) + c_l + c_r + ld(C_D, c - 1) + ld(C_D, c)
        st(C_L, c, c_l)
        inverse_c = jnp.where(total > zero, F32(DAMP) / total, zero)
        st(C_I, c, inverse_c)
        for ref, w in ((M_L, c_l), (M_R, c_r), (M_U, ld(C_D, c - 1)), (M_D, ld(C_D, c))):
            st(ref, c, inverse_c * w)
        g = inverse_c * ld(GC, c)
        st(EA, c, g)
        st(GC, c, g)

    def smooth(turn, lo, hi):
        if lo > 0:
            st(EA, B + lo - 8, coarse_zeros)
            st(EC, B + lo - 8, coarse_zeros)
        if hi < coarse:
            st(EA, B + hi, coarse_zeros)
            st(EC, B + hi, coarse_zeros)
        for old, new in ((EA, EC), (EC, EA), (EA, E.at[turn])):
            for c in range(B + lo, B + hi, 8):
                e = ld(old, c)
                fixed = F32(1.0 - DAMP) * e + ld(GC, c)
                vertical = ld(M_U, c) * ld(old, c - 1) + ld(M_D, c) * ld(old, c + 1)
                beside = ld(M_L, c) * form.coarse_left(e) + ld(M_R, c) * form.coarse_right(e)
                st(new, c, (fixed + vertical) + beside)

    def differences(turn, lo, hi, with_sums):
        e_ref = E.at[turn]
        for c in range(B + lo, B + hi, 8):
            e = ld(e_ref, c)
            parts = (e - form.coarse_left(e), e - form.coarse_right(e), e - ld(e_ref, c - 1), e - ld(e_ref, c + 1))
            for k, x in enumerate(parts):
                st(D.at[turn, k], c, x)
            if with_sums:
                d_l, d_r, d_u, d_d = parts
                image = ld(C_A, c) * e + ld(C_L, c) * d_l + ld(C_R, c) * d_r
                g = ld(SUM, c) + (image + (ld(C_D, c - 1) * d_u + ld(C_D, c) * d_d))
                st(SUM, c, g)
                g = ld(C_I, c) * g
                st(GC, c, g)
                st(EA, c, g)

    def lifted(turn, r):
        at = B + 10 + (r - B) // 4
        shape = (8, form.coarse_blocks * 128)
        row = rows(shape)

        def two(ref):
            a, b = [jnp.broadcast_to(ld(ref, at + k, 1), shape) for k in (0, 1)]
            return jnp.where(row < 4, a, b)

        e, d_l, d_r, d_u, d_d = two(E.at[turn]), *[two(D.at[turn, k]) for k in range(4)]
        e = form.spread(e)
        vertical = ld(WM, r) * form.spread(jnp.where(row % 4 == 0, d_u, d_d))
        return e, AN.chunk(r) * e + (form.at_sides(WL.chunk(r), d_l, WX.chunk(r), d_r) + vertical)

    def operate(v, t, chunks):
        for r in chunks:
            st(t, r, apply_a(form, v, WL, WX, WY, AN, r))

    def stretch(a, b):
        shape = (8, a.shape[1])
        return form.unpack_rows(jnp.where(rows(shape) < 4, jnp.broadcast_to(a, shape), jnp.broadcast_to(b, shape)))

    def second_sums(side, c, sums):
        for k in range(5):
            at = 4 * HR + FAR - 1 + k
            row = sides(at, at + 1)[side]
            st(KF.at[k], 8, form.unpack_rows(jnp.broadcast_to(row, (4, row.shape[1]))))
        centre, east, south, south_east, south_west = [ld(KF.at[k], 8, 4) for k in range(5)]
        north, north_west, north_east = [ld(KF.at[k], 7, 4) for k in (2, 3, 4)]
        e, below, above = [ld(E.at[0], B + c + d, 4) for d in (0, 1, -1)]
        image = centre * e + east * form.coarse_right(e) + form.coarse_left(east * e)
        image = image + south * below + north * above
        image = image + south_east * form.coarse_right(below) + form.coarse_left(north_west * above)
        image = image + south_west * form.coarse_left(below) + form.coarse_right(north_east * above)
        st(KV.at[side], 0, image + form.unpack_rows(jnp.broadcast_to(sums, (4, sums.shape[1]))))

    chunks = range(B, B + fine, 8)
    end = B + fine
    for r in (*chunks[:3], *chunks[-3:]):
        st(PA, r, read(DI, r, first_inverse) * read(R, r, first_rows))
    operate(PA, T0, (*chunks[:2], *chunks[-2:]))
    far_up, _ = sides(0, 1)
    near_up, _ = sides(1, 2)
    _, near_down = sides(HR - 1, HR)
    _, far_down = sides(HR - 2, HR - 1)
    st(SUM, B, coarse_zeros)
    st(SUM, B + coarse - 8, coarse_zeros)
    st(SUM, B + 4, stretch(far_up, near_up)[0:7])
    st(SUM, B + coarse - FAR + 1, stretch(near_down, far_down)[1:])
    st(SUM, B + FAR + 1, ld(s_i, 1, n // 4 - 2))
    st(SUM, B + FAR - 1, form.total(four_rows(T0, B + 4, 2)))
    st(SUM, B + coarse - FAR - 1, form.total(four_rows(T0, end - 12, 2)))
    for r in chunks:
        w_u, w_d = ld(WY, r - 1), ld(WY, r)
        row = rows(w_d.shape) % 4
        st(WM, r, jnp.where(row == 0, w_u, jnp.where(row == 3, w_d, zero)))

    smooth(0, 0, coarse)
    differences(0, 0, coarse, True)
    second_sums(0, 7, sides(HR + 1, HR + 2)[0])
    second_sums(1, coarse - FAR, sides(2 * HR - 2, 2 * HR - 1)[1])
    for r in chunks:
        e, image = lifted(0, r)
        inner = chunks[2] <= r < chunks[-2]
        p = read(DI, r, first_inverse) * read(R, r, first_rows) + e
        q = (ld(t_i, r - B - HR) if inner else ld(T0, r)) + image
        st(PA, r, p)
        st(QA, r, q)
        st(PB, r, read(DI, r, first_inverse) * q - F32(SHIFT) * p)
    st(r0, 0, first_rows)
    operate(PB, T1, chunks)
    for c, side in ((8, 0), (coarse - FAR + 1, 1)):
        st(SUM, B + c, ld(KV.at[side], 1, 3) - F32(SHIFT) * ld(SUM, B + c, 3))
    for c in range(FAR - 1, coarse - FAR + 1, 8):
        st(SUM, B + c, form.total(four_rows(T1, B + 4 * c - 40, min(8, coarse - FAR + 1 - c))))
    smooth(1, 0, coarse)
    differences(1, 8, coarse - 8, True)
    for r in chunks:
        e, image = lifted(1, r)
        p = ld(PB, r) + e
        q = ld(T1, r) + image
        st(PB, r, p)
        st(QB, r, q)
        st(PC, r, read(DI, r, first_inverse) * q - F32(SHIFT) * p)
    operate(PC, T2, chunks[1:-1])
    smooth(2, 8, coarse - 8)
    differences(2, 8, coarse - 8, False)
    acc = [jnp.zeros((8, 128), F32) for _ in range(9)]
    for r in range(0, n, 8):
        f = B + HR + r
        e, image = lifted(2, f)
        image = ld(T2, f) + image
        st(PC, f, ld(PC, f) + e)
        sums = [[] for _ in acc]
        for j in range(own_blocks):
            i2 = image[:, j * 128 : (j + 1) * 128]
            q2[j, r : r + 8, :] = i2
            z0, z1, z2, i0, i1 = [x[j, f : f + 8, :] for x in (PA, PB, PC, QA, QB)]
            res = read(R, f, first_rows)[:, j * 128 : (j + 1) * 128]
            pairs = ((z0, i0), (z1, i0), (z1, i1), (z2, i0), (z2, i1), (z2, i2), (z0, res), (z1, res), (z2, res))
            for k, (x, y) in enumerate(pairs):
                sums[k].append(x * y)
        for k, parts in enumerate(sums):
            acc[k] = acc[k] + tree(parts)
    lane = lanes((8, 128))
    line = jnp.zeros((8, 128), F32)
    for k in range(9):
        total = jnp.sum(jnp.sum(acc[k], axis=0, keepdims=True), axis=1, keepdims=True)
        line = jnp.where(lane == k, jnp.broadcast_to(total, (8, 128)), line)
    for j in range(mom.shape[0]):
        mom[j] = line[0:1]


def combine(mom, p0, p1, p2, q0, q1, q2, r_first, r_i, heights, residual, work):
    blocks, n, _ = q2.shape
    skip = GUARD + HR
    form = layout(blocks + 1)
    tot = jnp.broadcast_to(tree([mom[j] for j in range(mom.shape[0])]), (8, 128))
    m = [jnp.broadcast_to(tot[:, k : k + 1], (8, 128)) for k in range(9)]
    g00, g10, g11, g20, g21, g22, b0, b1, b2 = m
    l10, l20 = g10 / g00, g20 / g00
    d1 = g11 - l10 * g10
    t21 = g21 - l20 * g10
    l21 = t21 / d1
    d2 = g22 - l20 * g20 - l21 * t21
    y1 = b1 - l10 * b0
    y2 = b2 - l20 * b0 - l21 * y1
    x2 = y2 / d2
    x1 = y1 / d1 - l21 * x2
    x0 = b0 / g00 - l10 * x1 - l20 * x2
    sums, spare = [[work.at[k], work.at[k + 1]] for k in (0, 2)]
    for r in range(0, n, 8):
        for j in range(blocks):
            z0, z1, z2, i0, i1 = [x[j, skip + r : skip + r + 8, :] for x in (p0, p1, p2, q0, q1)]
            i2, res = q2[j, r : r + 8, :], r_first[j] if r == 0 else r_i[j, r : r + 8, :]
            sums[0][j, r : r + 8, :] = x0 * z0 + x1 * z1 + x2 * z2
            sums[1][j, r : r + 8, :] = res - (x0 * i0 + x1 * i1 + x2 * i2)
    reorder(form.steps_out, sums, [heights, residual], spare)


def swap(x, axis, size, inner):
    if inner:
        pairs = [(i, i ^ 1) for i in range(size) if i ^ 1 < size]
    else:
        pairs = [(i, j) for i in range(size) for j in [((i + 1) ^ 1) - 1] if 0 <= j < size]
    return lax.ppermute(x, axis, pairs)


def local(nrow, ncol, gx, gy, wx, wy, an, pr):
    n, width = gx.shape
    ext = width + 2 * HC
    fields = tuple(pltpu.with_memory_space_constraint(f, pltpu.HBM) for f in (gx, gy, wx, wy, an, pr))
    nb = ext // 128
    shape = lambda *dims: jax.ShapeDtypeStruct(dims, F32)
    params = pltpu.CompilerParams(vmem_limit_bytes=48 * 1024 * 1024)

    def call(kernel, name, args, outs, scratch=(), us=1, fetches=0):
        sems = [pltpu.SemaphoreType.DMA((fetches,))] if fetches else []
        return pl.pallas_call(
            kernel,
            in_specs=[HBM if fetches else VMEM] * len(args),
            out_specs=[VMEM] * len(outs),
            out_shape=outs,
            scratch_shapes=[pltpu.VMEM(dims, F32) for dims in scratch] + sems,
            compiler_params=params,
            cost_estimate=pl.CostEstimate(flops=us * 2_000_000, bytes_accessed=us * 2_000_000, transcendentals=0),
            name=name,
        )(*args)

    halos = []
    for inner in (True, False) if ncol > 2 else (True,):
        (edge,) = call(functools.partial(edge_columns, inner), "edge_columns", fields, [shape(n + n // 2 + 8, 128)], [(n, 128)] * 6, 1, 6)
        halos.append(swap(edge, "col", ncol, inner))
    tile = shape(nb - 1, n, 128)
    own = call(tile_fields, "tile_fields", fields, [tile] * 4 + [shape(n, 128), shape(nb - 1, 8, 128)], [(n, width)] * 6 + [(4, nb - 1, n, 128)] * 2 + [(2, nb - 1, 8, 128)], 1, 6)
    cb = layout(nb).coarse_blocks
    far = shape(cb, FAR, 128)
    msg = shape(nb, DEPTH, 128)
    field = shape(nb, n, 128)
    work = [(nb, 40 + 2 * GUARD, 128)] * 5 + [(5, cb, 24, 128), (5, cb, 8, 128)]
    *fields, to_out, g_a, cr_a, cd_a, ca_a = call(
        functools.partial(edge_rows, len(halos) > 1),
        "edge_rows",
        (*own, *halos),
        [field, field, shape(nb, GUARD + n, 128), field, shape(nb, 8, 128), msg] + [far] * 4,
        work,
    )
    from_out = swap(to_out, "row", nrow, False)
    di, wl, t, sums, to_in, *far_b = call(
        near_rows,
        "near_rows",
        fields,
        [field, field, field, shape(cb, n // 4, 128), msg] + [far] * 4,
        work + [(nb, n + 2 * GUARD, 128)],
    )
    from_in = swap(to_in, "row", nrow, True)
    fine = n + 2 * HR
    coarse = n // 4 + 2 * FAR
    mom, *vectors = call(
        basis,
        "basis",
        (*fields, g_a, cr_a, cd_a, ca_a, di, wl, t, sums, *far_b, from_in, from_out),
        [shape(nrow * ncol, 1, 128)] + [shape(nb, fine + 2 * GUARD, 128)] * 5 + [tile, shape(nb, 8, 128)],
        [(5, 2, nb, HR, 128)] + [(nb, fine + 2 * GUARD, 128)] * 5 + [(cb, coarse + 2 * GUARD, 128)] * 13
        + [(3, cb, coarse + 2 * GUARD, 128), (3, 4, cb, coarse + 2 * GUARD, 128), (5, cb, 16, 128), (2, cb, 8, 128)],
    )
    mom = lax.all_to_all(mom, ("row", "col"), 0, 0, tiled=True)
    out = shape(n, width)
    return tuple(call(combine, "combine", (mom, *vectors, fields[0]), [out, out], [(4, nb - 1, n, 128)]))


def solution(mesh):
    spec = P("row", "col")
    return jax.shard_map(
        functools.partial(local, mesh.shape["row"], mesh.shape["col"]),
        mesh=mesh,
        in_specs=(spec,) * 6,
        out_specs=(spec, spec),
        check_vma=False,
    )
```
